32 devices in a mesh: dp: 8 (over z, y), tier: 2 (over x), head: 2 (over core).
Axes of the slice: x: 2, y: 2, z: 4, core: 2. Of those that a mesh axis runs over, the one named last changes fastest.
Arguments:
- inputs: bfloat16 [24, 512, 1024], P('dp', 'tier'), may hold values from -6 to 6
- memories: bfloat16 [24, 2, 512, 1024], P('dp', 'tier'), may hold values from -6 to 6
- seg_len: int32 [24], P('dp'), may hold values from 128 to 512, as said below
- mem_count: int32 [24, 2], P('dp', 'tier'), may hold values from 1 to 512, as said below
- w_query: bfloat16 [1024, 1024], P(None, 'head'), may hold values from -0.1875 to 0.1875
- w_key: bfloat16 [1024, 1024], P(None, 'head'), may hold values from -0.1875 to 0.1875
- w_value: bfloat16 [1024, 1024], P(None, 'head'), may hold values from -0.1875 to 0.1875
- w_attn_out: bfloat16 [1024, 1024], P('head'), may hold values from -3 to 3
- w_ffn_in: bfloat16 [1024, 4096], P(None, 'head'), may hold values from -0.1875 to 0.1875
- w_ffn_out: bfloat16 [4096, 1024], P('head'), may hold values from -0.09375 to 0.09375
- w_compress: bfloat16 [3, 1024, 1024], P(None, None, ('tier', 'head')), may hold values from -0.109375 to 0.109375
- gain_attn: float32 [1024], replicated, may hold values from 0.25 to 1.75
- bias_attn: float32 [1024], replicated, may hold values from -2.5 to 2.5
- gain_ffn: float32 [1024], replicated, may hold values from 0.25 to 1.75
- bias_ffn: float32 [1024], replicated, may hold values from -2.5 to 2.5
- cotan_output: bfloat16 [24, 512, 1024], P('dp', 'tier'), may hold values from -6 to 6
- cotan_compressed: bfloat16 [24, 170, 1024], P('dp', None, ('tier', 'head')), may hold values from -6 to 6
Outputs:
- layer_output: bfloat16 [24, 512, 1024], P('dp', 'tier')
- compressed: bfloat16 [24, 170, 1024], P('dp', None, ('tier', 'head'))
- grad_inputs: bfloat16 [24, 512, 1024], P('dp', 'tier')
- grad_query: float32 [1024, 1024], P(None, 'head')
- grad_key: float32 [1024, 1024], P(None, 'head')
- grad_value: float32 [1024, 1024], P(None, 'head')
- grad_attn_out: float32 [1024, 1024], P('head')
- grad_ffn_in: float32 [1024, 4096], P(None, 'head')
- grad_ffn_out: float32 [4096, 1024], P('head')
- grad_compress: float32 [3, 1024, 1024], P(None, None, ('tier', 'head'))
- grad_gain_attn: float32 [1024], replicated
- grad_bias_attn: float32 [1024], replicated
- grad_gain_ffn: float32 [1024], replicated
- grad_bias_ffn: float32 [1024], replicated
The draws below stay inside these ranges and needn't reach their ends.
Inputs may be any that keep to these rules, and one draw needn't show every extreme that they name: `seg_len`: each segment holds 512, 256 or 128 tokens; in each group of streams k * 3 to k * 3 + 2, one holds 512 (others may too). `mem_count`: in each group of streams k * 3 to k * 3 + 2, one has a full recent memory and one a full compressed memory (others may too).
All inputs are finite; a program needn't handle non-finite values.
Results may differ from the reference program's by a relative error of at most 0.017.
Values may be sent and summed in bfloat16 or wider, within the bound.
No kernel may reach another device: no remote copies, remote signals or barrier semaphores. Data moves between devices by JAX's collectives and lax.ppermute only.
A program may use at most 192 MiB of HBM per device.

```python
import jax
import jax.numpy as jnp
from jax import lax

D = 1024
HEADS = 8
HD = 128
FF = 4096
SEG = 512
MEM = 512
RATE = 3
STREAMS_DEV = 3
COMP = 170
STREAMS = 24


def group_pick(key, columns):
    chosen = jax.random.randint(key, (STREAMS // STREAMS_DEV, columns), 0, STREAMS_DEV)
    owner_rows = jnp.repeat(chosen, STREAMS_DEV, axis=0)
    return (jnp.arange(STREAMS) % STREAMS_DEV)[:, None] == owner_rows


def draw_seg_len(key, part):
    key = jax.random.fold_in(key, 5)
    first_key, second_key = jax.random.split(key)
    halvings = jax.random.randint(first_key, (STREAMS, 1), 0, 3)
    lengths = SEG // jnp.power(2, halvings)
    return jnp.where(group_pick(second_key, 1), SEG, lengths)[:, 0].astype(jnp.int32)


def draw_mem_count(key, part):
    key = jax.random.fold_in(key, 11)
    first_key, second_key = jax.random.split(key)
    filled = jax.random.randint(first_key, (STREAMS, 2), 1, MEM + 1)
    return jnp.where(group_pick(second_key, 2), MEM, filled).astype(jnp.int32)


def block_levels(stream_key, extent, cuts, smallest, largest):
    level = 1.0
    for position, parts in cuts:
        steps = jax.random.uniform(jax.random.fold_in(jax.random.fold_in(stream_key, 6), position), (parts,), jnp.float32, smallest / len(cuts), largest / len(cuts))
        level = level * jnp.repeat(jnp.exp(steps), extent[position] // parts).reshape((-1,) + (1,) * (len(extent) - 1 - position))
    return level


def scatter_about(own_key, extent, scale, limit, cuts=(), held_as=jnp.bfloat16):
    array = scale * jax.random.normal(own_key, extent, jnp.float32)
    if cuts:
        array = array * block_levels(own_key, extent, cuts, -0.22, 0.18)
    return jnp.clip(array, -limit, limit).astype(held_as)


def setup_inputs(seed: int = 0) -> dict:
    seeds = jax.random.split(jax.random.key(seed), 18)
    inputs = scatter_about(seeds[0], (STREAMS, SEG, D), 1.0, 6.0, ((0, 8), (1, 2)))
    memories = scatter_about(seeds[1], (STREAMS, 2, MEM, D), 1.0, 6.0, ((0, 8), (1, 2)))
    seg_len = draw_seg_len(jax.random.fold_in(seeds[17], 71), 0)
    mem_count = draw_mem_count(jax.random.fold_in(seeds[17], 71), 0)
    w_query = scatter_about(seeds[4], (D, D), D ** -0.5, 0.1875, ((1, 2),))
    w_key = scatter_about(seeds[5], (D, D), D ** -0.5, 0.1875, ((1, 2),))
    w_value = scatter_about(seeds[6], (D, D), D ** -0.5, 0.1875, ((1, 2),))
    w_attn_out = scatter_about(seeds[7], (D, D), (max(D // 256, 2)) ** -0.5, 3.0, ((0, 2),))
    w_ffn_in = scatter_about(seeds[8], (D, FF), D ** -0.5, 0.1875, ((1, 2),))
    w_ffn_out = scatter_about(seeds[9], (FF, D), FF ** -0.5, 0.09375, ((0, 2),))
    w_compress = scatter_about(seeds[10], (RATE, D, D), (RATE * D) ** -0.5, 0.109375, ((2, 4),))
    gain_attn = jnp.clip(1.0 + 0.15 * jax.random.normal(seeds[11], (D,), jnp.float32), 0.25, 1.75)
    bias_attn = scatter_about(seeds[12], (D,), 0.3, 2.5, (), jnp.float32)
    gain_ffn = jnp.clip(1.0 + 0.15 * jax.random.normal(seeds[13], (D,), jnp.float32), 0.25, 1.75)
    bias_ffn = scatter_about(seeds[14], (D,), 0.3, 2.5, (), jnp.float32)
    cotan_output = scatter_about(seeds[15], (STREAMS, SEG, D), 1.0, 6.0, ((0, 8), (1, 2)))
    cotan_compressed = scatter_about(seeds[16], (STREAMS, COMP, D), 1.0, 6.0, ((0, 8), (2, 4)))
    return {"inputs": inputs, "memories": memories, "seg_len": seg_len, "mem_count": mem_count, "w_query": w_query, "w_key": w_key, "w_value": w_value, "w_attn_out": w_attn_out, "w_ffn_in": w_ffn_in, "w_ffn_out": w_ffn_out, "w_compress": w_compress, "gain_attn": gain_attn, "bias_attn": bias_attn, "gain_ffn": gain_ffn, "bias_ffn": bias_ffn, "cotan_output": cotan_output, "cotan_compressed": cotan_compressed}


EPS = 1e-05
NEG = -1000000000.0
HIGHEST = lax.Precision.HIGHEST

@jax.custom_vjp
def low(v):
    return lax.optimization_barrier(v.astype(jnp.bfloat16)).astype(jnp.float32)

@jax.custom_vjp
def low_back(v):
    return v

def low_keep(v):
    return (low(v), None)

def low_pass(kept, grad):
    return (grad,)

def back_keep(v):
    return (v, None)

def back_low(kept, grad):
    return (low(grad),)
low.defvjp(low_keep, low_pass)
low_back.defvjp(back_keep, back_low)

def norm_rows(values, gain_vector, bias_vector):
    centre = values - lax.optimization_barrier(jnp.mean(values, axis=-1, keepdims=True))
    spread = lax.optimization_barrier(jnp.mean(centre * centre, axis=-1, keepdims=True))
    return centre * lax.rsqrt(spread + EPS) * gain_vector + bias_vector

def matmul(first_operand, second_operand):
    return jnp.dot(first_operand, second_operand, precision=HIGHEST, preferred_element_type=jnp.float32)

def split_heads(values):
    return values.reshape(values.shape[0], HEADS, HD).transpose(1, 0, 2)

def tier_part(queries, key_heads, value_heads, allowed):
    scores = jnp.einsum('hqd,hkd->hqk', queries, key_heads, precision=HIGHEST) * HD ** (-0.5)
    scores = jnp.where(allowed[None], low_back(scores), NEG)
    totals = jax.nn.logsumexp(scores, axis=-1, keepdims=True)
    weights = low(jnp.exp(scores - totals))
    partial_value = low_back(jnp.einsum('hqk,hkd->hqd', weights, value_heads, precision=HIGHEST))
    return (partial_value, totals)

def layer_stream(params, stream):
    w_query, w_key, w_value, w_attn_out, w_ffn_in, w_ffn_out, w_compress, gain_attn, bias_attn, gain_ffn, bias_ffn = params
    tokens, recent, packed, length, counts = stream
    row_index = jnp.arange(SEG)
    slot_index = jnp.arange(MEM)
    normed = low(norm_rows(tokens, gain_attn, bias_attn))
    recent_normed = low(norm_rows(recent, gain_attn, bias_attn))
    packed_normed = low(norm_rows(packed, gain_attn, bias_attn))

    def project(values, weight):
        return split_heads(low(low_back(matmul(values, weight))))
    queries = project(normed, w_query)
    near_rows = jnp.concatenate([recent_normed, normed], 0)
    near_keys = project(near_rows, w_key)
    near_values = project(near_rows, w_value)
    far_keys = project(packed_normed, w_key)
    far_values = project(packed_normed, w_value)
    recent_ok = jnp.broadcast_to(slot_index[None, :] < counts[0], (SEG, MEM))
    packed_ok = jnp.broadcast_to(slot_index[None, :] < counts[1], (SEG, MEM))
    causal_ok = (row_index[None, :] <= row_index[:, None]) & (row_index[None, :] < length)
    near_part, near_total = tier_part(queries, near_keys, near_values, jnp.concatenate([recent_ok, causal_ok], 1))
    far_part, far_total = tier_part(queries, far_keys, far_values, packed_ok)
    merged_total = jnp.logaddexp(near_total, far_total)
    merged = jnp.exp(near_total - merged_total) * near_part + jnp.exp(far_total - merged_total) * far_part
    merged = low(low_back(merged.transpose(1, 0, 2).reshape(SEG, HEADS * HD)))
    attended = low_back(matmul(merged, w_attn_out))
    hidden = tokens + attended
    hidden_normed = low(norm_rows(hidden, gain_ffn, bias_ffn))
    lifted = low_back(matmul(hidden_normed, w_ffn_in))
    activated = low(jax.nn.gelu(lifted))
    ffn_result = low_back(matmul(activated, w_ffn_out))
    output = jnp.where((row_index < length)[:, None], hidden + ffn_result, 0.0)
    evicted = jnp.where((slot_index < counts[0])[:, None], recent, 0.0)[:COMP * RATE].reshape(COMP, RATE * D)
    squeezed = matmul(evicted, w_compress.reshape(RATE * D, D))
    squeezed = jnp.where((jnp.arange(COMP) < length // RATE)[:, None], squeezed, 0.0)
    return (output, squeezed)

def reference(inputs, memories, seg_len, mem_count, w_query, w_key, w_value, w_attn_out, w_ffn_in, w_ffn_out, w_compress, gain_attn, bias_attn, gain_ffn, bias_ffn, cotan_output, cotan_compressed):
    params = tuple((weight.astype(jnp.float32) for weight in (w_query, w_key, w_value, w_attn_out, w_ffn_in, w_ffn_out, w_compress, gain_attn, bias_attn, gain_ffn, bias_ffn)))
    stored = memories.astype(jnp.float32)
    one_stream = jax.checkpoint(layer_stream)

    def forward(weights, tokens):
        return lax.map(lambda stream: one_stream(weights, stream), (tokens, stored[:, 0], stored[:, 1], seg_len, mem_count))
    (layer_output, compressed), pull_back = jax.vjp(forward, params, inputs.astype(jnp.float32))
    weight_grads, grad_inputs = pull_back((cotan_output.astype(jnp.float32), cotan_compressed.astype(jnp.float32)))
    return (layer_output.astype(jnp.bfloat16), compressed.astype(jnp.bfloat16), grad_inputs.astype(jnp.bfloat16), weight_grads[0], weight_grads[1], weight_grads[2], weight_grads[3], weight_grads[4], weight_grads[5], weight_grads[6], weight_grads[7], weight_grads[8], weight_grads[9], weight_grads[10])
```

```python
import jax
import jax.numpy as jnp
from jax import lax
from jax.sharding import PartitionSpec as P

HD = 128
SEG = 512
MEM = 512
RATE = 3
COMP = 170


EPS = 1e-05
NEG = -1000000000.0


def from_behind(value, axis, by):
    peers = lax.axis_size(axis)
    pairs = [(i, i + by) for i in range(peers) if 0 <= i + by < peers]
    return lax.ppermute(value, axis, pairs)


def bits_of():
    size = lax.axis_size("dp")
    bits = [("tier", 1)]
    step = 1
    while step < size:
        bits.append(("dp", step))
        step *= 2
    return bits


def bit_value(bit):
    axis, step = bit
    return (lax.axis_index(axis) // step) % 2


def swap(value, bit):
    axis, step = bit
    return lax.ppermute(value, axis, [(i, i ^ step) for i in range(lax.axis_size(axis))])


def add_low(first, second):
    total = first.astype(jnp.float32) + second.astype(jnp.float32)
    return lax.optimization_barrier(total.astype(jnp.bfloat16))


def sum_head(value):
    own = lax.optimization_barrier(value.astype(jnp.bfloat16))
    other = lax.ppermute(own, "head", [(0, 1), (1, 0)])
    return own.astype(jnp.float32) + other.astype(jnp.float32)


def all_reduce(value, order):
    held = value
    scattered = []
    for place, bit in enumerate(order):
        half = held.shape[0] // 2
        if place == len(order) - 1 or half % 16:
            held = add_low(held, swap(held, bit))
        else:
            side = bit_value(bit)
            sent = lax.dynamic_slice_in_dim(held, (1 - side) * half, half, 0)
            kept = lax.dynamic_slice_in_dim(held, side * half, half, 0)
            held = add_low(kept, swap(sent, bit))
            scattered.append((bit, side))
    for bit, side in reversed(scattered):
        other = swap(held, bit)
        held = jnp.where(
            side == 0, jnp.concatenate([held, other], 0), jnp.concatenate([other, held], 0)
        )
    return held


def reduce_parts(value, sizes):
    tier, *rest = bits_of()
    orders = (
        [tier, *rest],
        [rest[0], rest[1], tier, *rest[2:]],
        [rest[1], tier, rest[0], *rest[2:]],
    )
    low = lax.optimization_barrier(value.astype(jnp.bfloat16))
    start = 0
    pieces = []
    for size, order in zip(sizes, orders):
        pieces.append(all_reduce(low[start : start + size], order))
        start += size
    return jnp.concatenate(pieces, 0).astype(jnp.float32)


def norm_stats(values):
    centre = values - jnp.mean(values, axis=-1, keepdims=True)
    inverse = lax.rsqrt(jnp.mean(centre * centre, axis=-1, keepdims=True) + EPS)
    return (centre * inverse, inverse)


def norm_back(grad_normed, normed, inverse, gain_vector):
    scaled = grad_normed * gain_vector
    return inverse * (
        scaled
        - jnp.mean(scaled, axis=-1, keepdims=True)
        - normed * jnp.mean(scaled * normed, axis=-1, keepdims=True)
    )


def split_heads(values):
    return values.reshape(values.shape[0], -1, HD).transpose(1, 0, 2)


def join_heads(values):
    return values.transpose(1, 0, 2).reshape(values.shape[1], -1)


def product(first_operand, second_operand):
    return jnp.dot(first_operand, second_operand, preferred_element_type=jnp.float32)


def scores_of(queries, key_heads, allowed):
    raw_scores = jnp.einsum(
        "hqd,hkd->hqk", queries, key_heads, preferred_element_type=jnp.float32
    ) * HD ** (-0.5)
    return jnp.where(allowed[None], raw_scores, NEG)


def masks_of(length, filled):
    row_index = jnp.arange(SEG)
    slot_index = jnp.arange(MEM)
    memory_ok = jnp.broadcast_to(slot_index[None, :] < filled, (SEG, MEM))
    causal_ok = (row_index[None, :] <= row_index[:, None]) & (row_index[None, :] < length)
    return (memory_ok, causal_ok)


def forward_part(queries, key_heads, value_heads, allowed):
    scores = scores_of(queries, key_heads, allowed)
    totals = jax.nn.logsumexp(scores, axis=-1, keepdims=True)
    weights = jnp.exp(scores - totals).astype(jnp.bfloat16)
    partial_value = jnp.einsum(
        "hqk,hkd->hqd", weights, value_heads, preferred_element_type=jnp.float32
    )
    return (join_heads(partial_value), totals[..., 0].T)


def backward_part(queries, key_heads, value_heads, allowed, own_column, offset, grad_part):
    scores = scores_of(queries, key_heads, allowed)
    raw_weights = jnp.exp(scores - own_column)
    grad_weights = jnp.einsum(
        "hqd,hkd->hqk", grad_part, value_heads, preferred_element_type=jnp.float32
    )
    spent_sum = jnp.sum(raw_weights * grad_weights, axis=-1, keepdims=True)
    grad_scores = (raw_weights * (grad_weights + offset - spent_sum)).astype(jnp.bfloat16)
    factor = HD ** (-0.5)
    grad_queries = (
        jnp.einsum("hqk,hkd->hqd", grad_scores, key_heads, preferred_element_type=jnp.float32)
        * factor
    )
    grad_keys = (
        jnp.einsum("hqk,hqd->hkd", grad_scores, queries, preferred_element_type=jnp.float32)
        * factor
    )
    grad_values = jnp.einsum(
        "hqk,hqd->hkd",
        raw_weights.astype(jnp.bfloat16),
        grad_part,
        preferred_element_type=jnp.float32,
    )
    return (join_heads(grad_queries), join_heads(grad_keys), join_heads(grad_values))


def on_device(
    inputs,
    memories,
    seg_len,
    mem_count,
    w_query,
    w_key,
    w_value,
    w_attn_out,
    w_ffn_in,
    w_ffn_out,
    w_compress,
    gain_attn,
    bias_attn,
    gain_ffn,
    bias_ffn,
    cotan_output,
    cotan_compressed,
):
    tier_index = lax.axis_index("tier")
    streams, half_rows, model_width = inputs.shape
    features = w_query.shape[1]
    heads_here = features // HD
    tokens = inputs.astype(jnp.float32)
    row_index = tier_index * half_rows + jnp.arange(half_rows)
    row_valid = (row_index[None, :] < seg_len[:, None])[..., None]
    normed_first, inverse_first = norm_stats(tokens)
    normed_own = (normed_first * gain_attn + bias_attn).astype(jnp.bfloat16)
    normed_full = lax.all_gather(normed_own, "tier", axis=1, tiled=True)
    stored = memories[:, 0].astype(jnp.float32)
    stored_normed, stored_inverse = norm_stats(stored)
    stored_low = (stored_normed * gain_attn + bias_attn).astype(jnp.bfloat16)
    counts = mem_count[:, 0]

    def attend(stream_item):
        segment_normed, memory_rows, length, filled = stream_item
        queries = product(segment_normed, w_query).astype(jnp.bfloat16)
        memory_keys = product(memory_rows, w_key).astype(jnp.bfloat16)
        memory_values = product(memory_rows, w_value).astype(jnp.bfloat16)
        memory_ok, causal_ok = masks_of(length, filled)

        def near_side(unused):
            segment_keys = product(segment_normed, w_key).astype(jnp.bfloat16)
            segment_values = product(segment_normed, w_value).astype(jnp.bfloat16)
            partial_value, totals = forward_part(
                split_heads(queries),
                split_heads(jnp.concatenate([memory_keys, segment_keys], 0)),
                split_heads(jnp.concatenate([memory_values, segment_values], 0)),
                jnp.concatenate([memory_ok, causal_ok], 1),
            )
            return (partial_value, totals, segment_keys, segment_values)

        def far_side(unused):
            partial_value, totals = forward_part(
                split_heads(queries),
                split_heads(memory_keys),
                split_heads(memory_values),
                memory_ok,
            )
            empty_rows = jnp.zeros_like(queries)
            return (partial_value, totals, empty_rows, empty_rows)

        partial_value, totals, segment_keys, segment_values = lax.cond(
            tier_index == 0, near_side, far_side, 0
        )
        return (
            partial_value,
            totals,
            queries,
            memory_keys,
            memory_values,
            segment_keys,
            segment_values,
        )

    partials, own_totals, queries, memory_keys, memory_values, segment_keys, segment_values = (
        lax.map(attend, (normed_full, stored_low, seg_len, counts))
    )
    both_parts, both_totals = (
        lax.all_to_all(partials[None], "tier", split_axis=2, concat_axis=0, tiled=True),
        lax.all_to_all(own_totals[None], "tier", split_axis=2, concat_axis=0, tiled=True),
    )
    merged_totals = jnp.logaddexp(both_totals[0], both_totals[1])
    mixing = jnp.exp(both_totals - merged_totals[None])
    merged = jnp.sum(
        both_parts.reshape(2, streams, half_rows, heads_here, HD) * mixing[..., None], axis=0
    ).reshape(streams, half_rows, features)
    merged_low = merged.astype(jnp.bfloat16)
    attended = sum_head(product(merged_low, w_attn_out))
    hidden = tokens + attended
    normed_second, inverse_second = norm_stats(hidden)
    hidden_low = (normed_second * gain_ffn + bias_ffn).astype(jnp.bfloat16)
    lifted = product(hidden_low, w_ffn_in)
    activated = jax.nn.gelu(lifted).astype(jnp.bfloat16)
    ffn_result = sum_head(product(activated, w_ffn_out))
    layer_output = jnp.where(row_valid, hidden + ffn_result, 0.0).astype(jnp.bfloat16)
    slot_valid = (jnp.arange(MEM)[None, :] < counts[:, None])[..., None]
    evicted_own = jnp.where(slot_valid, memories[:, 0], jnp.zeros_like(memories[:, 0]))[
        :, : COMP * RATE
    ]
    evicted_sent = from_behind(evicted_own, "tier", 1)
    evicted = jnp.where(tier_index == 0, evicted_own, evicted_sent).reshape(
        streams * COMP, RATE * model_width
    )
    squeeze_valid = (jnp.arange(COMP)[None, :] < (seg_len // RATE)[:, None])[..., None]
    squeezed = product(evicted, w_compress.reshape(RATE * model_width, -1)).reshape(
        streams, COMP, -1
    )
    compressed = jnp.where(squeeze_valid, squeezed, 0.0).astype(jnp.bfloat16)
    grad_squeezed = jnp.where(
        squeeze_valid, cotan_compressed, jnp.zeros_like(cotan_compressed)
    ).reshape(streams * COMP, -1)
    grad_compress_low = jnp.einsum(
        "rk,rc->kc", evicted, grad_squeezed, preferred_element_type=jnp.float32
    ).astype(jnp.bfloat16)
    grad_compress = (
        all_reduce(lax.optimization_barrier(grad_compress_low), bits_of()[1:])
        .astype(jnp.float32)
        .reshape(RATE, model_width, -1)
    )
    grad_out = jnp.where(row_valid, cotan_output.astype(jnp.float32), 0.0)
    grad_ffn_low = grad_out.astype(jnp.bfloat16)
    grad_ffn_out = jnp.einsum(
        "srk,srd->kd", activated, grad_ffn_low, preferred_element_type=jnp.float32
    )
    grad_activated = jnp.einsum(
        "srd,kd->srk", grad_ffn_low, w_ffn_out, preferred_element_type=jnp.float32
    )
    gelu_value, gelu_pull = jax.vjp(jax.nn.gelu, lifted)
    grad_lifted = gelu_pull(grad_activated)[0].astype(jnp.bfloat16)
    grad_ffn_in = jnp.einsum(
        "srd,srk->dk", hidden_low, grad_lifted, preferred_element_type=jnp.float32
    )
    grad_hidden_normed = sum_head(
        jnp.einsum("srk,dk->srd", grad_lifted, w_ffn_in, preferred_element_type=jnp.float32)
    )
    grad_gain_ffn = jnp.sum(grad_hidden_normed * normed_second, axis=(0, 1))
    grad_bias_ffn = jnp.sum(grad_hidden_normed, axis=(0, 1))
    grad_hidden = grad_out + norm_back(grad_hidden_normed, normed_second, inverse_second, gain_ffn)
    grad_attended = grad_hidden.astype(jnp.bfloat16)
    grad_attn_out = jnp.einsum(
        "srf,srd->fd", merged_low, grad_attended, preferred_element_type=jnp.float32
    )
    grad_merged = jnp.einsum(
        "srd,fd->srf", grad_attended, w_attn_out, preferred_element_type=jnp.float32
    ).astype(jnp.bfloat16)
    grad_merged_wide = grad_merged.astype(jnp.float32)
    delta_rows = jnp.sum(
        (grad_merged_wide * merged).reshape(streams, half_rows, heads_here, HD), axis=-1
    )
    grad_full, delta_full, totals_full = (
        lax.all_gather(grad_merged_wide, "tier", axis=1, tiled=True),
        lax.all_gather(delta_rows, "tier", axis=1, tiled=True),
        lax.all_gather(merged_totals, "tier", axis=1, tiled=True),
    )

    def attend_back(stream_item):
        (
            queries_one,
            memory_keys_one,
            memory_values_one,
            segment_keys_one,
            segment_values_one,
            partial_one,
            own_one,
            grad_one,
            delta_one,
            total_one,
            length,
            filled,
        ) = stream_item
        weight_own = jnp.exp(own_one - total_one)
        grad_heads = grad_one.reshape(SEG, heads_here, HD)
        own_dot = jnp.sum(grad_heads * partial_one.reshape(SEG, heads_here, HD), axis=-1)
        offset = (weight_own * (own_dot - delta_one)).T[:, :, None]
        grad_part = split_heads(
            (grad_heads * weight_own[..., None]).reshape(SEG, features).astype(jnp.bfloat16)
        )
        own_column = own_one.T[:, :, None]
        memory_ok, causal_ok = masks_of(length, filled)
        query_heads = split_heads(queries_one)

        def near_back(unused):
            grad_queries, grad_keys, grad_values = backward_part(
                query_heads,
                split_heads(jnp.concatenate([memory_keys_one, segment_keys_one], 0)),
                split_heads(jnp.concatenate([memory_values_one, segment_values_one], 0)),
                jnp.concatenate([memory_ok, causal_ok], 1),
                own_column,
                offset,
                grad_part,
            )
            return (
                grad_queries,
                grad_keys[:MEM],
                grad_values[:MEM],
                grad_keys[MEM:],
                grad_values[MEM:],
            )

        def far_back(unused):
            grad_queries, grad_keys, grad_values = backward_part(
                query_heads,
                split_heads(memory_keys_one),
                split_heads(memory_values_one),
                memory_ok,
                own_column,
                offset,
                grad_part,
            )
            empty_rows = jnp.zeros((SEG, features), jnp.float32)
            return (grad_queries, grad_keys, grad_values, empty_rows, empty_rows)

        return lax.cond(tier_index == 0, near_back, far_back, 0)

    grad_queries, grad_memory_keys, grad_memory_values, grad_segment_keys, grad_segment_values = (
        lax.map(
            attend_back,
            (
                queries,
                memory_keys,
                memory_values,
                segment_keys,
                segment_values,
                partials,
                own_totals,
                grad_full,
                delta_full,
                totals_full,
                seg_len,
                counts,
            ),
        )
    )
    summed_queries, summed_keys, summed_values = (
        lax.psum_scatter(
            grad_queries.astype(jnp.bfloat16), "tier", scatter_dimension=1, tiled=True
        ).astype(jnp.float32),
        lax.psum_scatter(
            grad_segment_keys.astype(jnp.bfloat16), "tier", scatter_dimension=1, tiled=True
        ).astype(jnp.float32),
        lax.psum_scatter(
            grad_segment_values.astype(jnp.bfloat16), "tier", scatter_dimension=1, tiled=True
        ).astype(jnp.float32),
    )
    grad_queries_low = summed_queries.astype(jnp.bfloat16)
    grad_keys_low = summed_keys.astype(jnp.bfloat16)
    grad_values_low = summed_values.astype(jnp.bfloat16)
    grad_mem_keys = grad_memory_keys.astype(jnp.bfloat16)
    grad_mem_values = grad_memory_values.astype(jnp.bfloat16)
    grad_query = jnp.einsum(
        "srd,srf->df", normed_own, grad_queries_low, preferred_element_type=jnp.float32
    )
    grad_key = jnp.einsum(
        "srd,srf->df", normed_own, grad_keys_low, preferred_element_type=jnp.float32
    ) + jnp.einsum("smd,smf->df", stored_low, grad_mem_keys, preferred_element_type=jnp.float32)
    grad_value = jnp.einsum(
        "srd,srf->df", normed_own, grad_values_low, preferred_element_type=jnp.float32
    ) + jnp.einsum("smd,smf->df", stored_low, grad_mem_values, preferred_element_type=jnp.float32)
    grad_normed_part = (
        jnp.einsum("srf,df->srd", grad_queries_low, w_query, preferred_element_type=jnp.float32)
        + jnp.einsum("srf,df->srd", grad_keys_low, w_key, preferred_element_type=jnp.float32)
        + jnp.einsum("srf,df->srd", grad_values_low, w_value, preferred_element_type=jnp.float32)
    )
    grad_stored_part = jnp.einsum(
        "smf,df->smd", grad_mem_keys, w_key, preferred_element_type=jnp.float32
    ) + jnp.einsum("smf,df->smd", grad_mem_values, w_value, preferred_element_type=jnp.float32)
    stored_gain_part = jnp.sum(grad_stored_part * stored_normed, axis=(0, 1))
    stored_bias_part = jnp.sum(grad_stored_part, axis=(0, 1))
    grad_normed = sum_head(grad_normed_part)
    grad_gain_attn = 0.5 * jnp.sum(grad_normed * normed_first, axis=(0, 1)) + stored_gain_part
    grad_bias_attn = 0.5 * jnp.sum(grad_normed, axis=(0, 1)) + stored_bias_part
    grad_inputs = (
        grad_hidden + norm_back(grad_normed, normed_first, inverse_first, gain_attn)
    ).astype(jnp.bfloat16)
    vectors = lax.psum(
        jnp.stack(
            [grad_gain_attn, grad_bias_attn, 0.5 * grad_gain_ffn, 0.5 * grad_bias_ffn], axis=0
        ),
        ("dp", "tier", "head"),
    )
    return (
        layer_output,
        compressed,
        grad_inputs,
        reduce_parts(grad_query, (256, 384, 384)),
        reduce_parts(grad_key, (256, 384, 384)),
        reduce_parts(grad_value, (256, 384, 384)),
        reduce_parts(grad_attn_out, (128, 192, 192)),
        reduce_parts(grad_ffn_in, (256, 384, 384)),
        reduce_parts(grad_ffn_out, (512, 768, 768)),
        grad_compress,
        vectors[0],
        vectors[1],
        vectors[2],
        vectors[3],
    )


def solution(mesh):
    return jax.shard_map(
        on_device,
        mesh=mesh,
        in_specs=(
            P("dp", "tier", None),
            P("dp", "tier", None, None),
            P("dp"),
            P("dp", "tier"),
            P(None, "head"),
            P(None, "head"),
            P(None, "head"),
            P("head", None),
            P(None, "head"),
            P("head", None),
            P(None, None, ("tier", "head")),
            P(),
            P(),
            P(),
            P(),
            P("dp", "tier", None),
            P("dp", None, ("tier", "head")),
        ),
        out_specs=(
            P("dp", "tier", None),
            P("dp", None, ("tier", "head")),
            P("dp", "tier", None),
            P(None, "head"),
            P(None, "head"),
            P(None, "head"),
            P("head", None),
            P(None, "head"),
            P("head", None),
            P(None, None, ("tier", "head")),
            P(),
            P(),
            P(),
            P(),
        ),
        check_vma=False,
    )
```

```python
import functools

import jax
import jax.numpy as jnp
from jax import lax
from jax.experimental import pallas as pl
from jax.experimental.pallas import tpu as pltpu
from jax.sharding import PartitionSpec as P

HD = 128
RATE = 3
EPS = 1e-05
NEG = -1000000000.0
LOG2E = 1.4426950408889634
SCALE = HD ** (-0.5)
GELU_ROOT = 0.7978845608028654
GELU_CUBE = 0.044715

LOW = jnp.bfloat16
WIDE = jnp.float32
NN = (((1,), (0,)), ((), ()))
NT = (((1,), (1,)), ((), ()))
TN = (((0,), (0,)), ((), ()))


def dot(first, second, dims=NN):
    return lax.dot_general(first, second, dims, preferred_element_type=WIDE)


def norm_stats(values):
    centre = values - jnp.mean(values, axis=-1, keepdims=True)
    inverse = lax.rsqrt(jnp.mean(centre * centre, axis=-1, keepdims=True) + EPS)
    return (centre * inverse, inverse)


def norm_back(grad_normed, normed, inverse, gain_vector):
    scaled = grad_normed * gain_vector
    return inverse * (
        scaled
        - jnp.mean(scaled, axis=-1, keepdims=True)
        - normed * jnp.mean(scaled * normed, axis=-1, keepdims=True)
    )


def per_stream(array_shape):
    block = (1,) + tuple(array_shape[1:])
    zeros = (0,) * (len(block) - 1)
    return pl.BlockSpec(block, lambda s: (s,) + zeros)


def whole(array_shape):
    zeros = (0,) * len(array_shape)
    return pl.BlockSpec(tuple(array_shape), lambda *_: zeros)


def scalars():
    return pl.BlockSpec(memory_space=pltpu.SMEM)


def shaped(shape, dtype=LOW):
    return jax.ShapeDtypeStruct(tuple(shape), dtype)


def call(kernel, grid, in_specs, out_specs, out_shape, scratch=(), flops=0, moved=0, vmem=48):
    return pl.pallas_call(
        kernel,
        grid=grid,
        in_specs=in_specs,
        out_specs=out_specs,
        out_shape=out_shape,
        scratch_shapes=list(scratch),
        compiler_params=pltpu.CompilerParams(vmem_limit_bytes=vmem * 1024 * 1024),
        cost_estimate=pl.CostEstimate(flops=flops, bytes_accessed=moved, transcendentals=0),
    )


def project_kernel(x_ref, gain_ref, bias_ref, *refs):
    count = (len(refs) - 1) // 2
    weights, unit_ref, outs = refs[:count], refs[count], refs[count + 1 :]
    rows = x_ref.shape[-2]
    normed, _ = norm_stats(x_ref[...].reshape(rows, -1).astype(WIDE))
    unit_ref[0] = normed.astype(LOW)
    low = (normed * gain_ref[...] + bias_ref[...]).astype(LOW)
    for weight_ref, out_ref in zip(weights, outs):
        out_ref[0] = dot(low, weight_ref[...]).astype(LOW)


def project(rows, gain, bias, weights):
    streams, count, width = rows.shape[0], rows.shape[-2], rows.shape[-1]
    features = weights[0].shape[1]
    outs = [shaped((streams, count, width))] + [
        shaped((streams, count, features)) for _ in weights
    ]
    return call(
        project_kernel,
        (streams,),
        [per_stream(rows.shape), whole(gain.shape), whole(bias.shape)]
        + [whole(w.shape) for w in weights],
        [per_stream(o.shape) for o in outs],
        outs,
        flops=2 * streams * count * width * features * len(weights),
        moved=4 * streams * count * width,
    )(rows, gain, bias, *weights)


def slot_masks(own, meta_ref, stream, streams, slots, rows):
    tier = meta_ref[0]
    length = meta_ref[1 + stream]
    filled = meta_ref[1 + streams + stream]
    memory_ok = lax.broadcasted_iota(jnp.int32, (slots, rows), 0) < filled
    key_row = lax.broadcasted_iota(jnp.int32, (rows, rows), 0)
    segment_ok = (tier * rows + key_row) < length
    if own:
        query_row = lax.broadcasted_iota(jnp.int32, (rows, rows), 1)
        segment_ok = segment_ok & (key_row <= query_row)
    return memory_ok, segment_ok


def by_tier(own, meta_ref, body):
    if own:
        body(True)
        return

    @pl.when(meta_ref[0] == 0)
    def _():
        body(True)

    @pl.when(meta_ref[0] != 0)
    def _():
        body(False)


def attend_kernel(own, meta_ref, q_ref, km_ref, vm_ref, ks_ref, vs_ref, out_ref, total_ref):
    streams = pl.num_programs(0)
    stream = pl.program_id(0)
    slots, rows = km_ref.shape[1], q_ref.shape[1]
    heads = q_ref.shape[2] // HD

    def body(with_segment):
        memory_ok, segment_ok = slot_masks(own, meta_ref, stream, streams, slots, rows)
        for head in range(heads):
            cols = slice(head * HD, (head + 1) * HD)
            query = q_ref[0, :, cols]
            scores = jnp.where(
                memory_ok, dot(km_ref[0, :, cols], query, NT) * (SCALE * LOG2E), NEG
            )
            top = jnp.max(scores, axis=0, keepdims=True)
            if with_segment:
                near = jnp.where(
                    segment_ok, dot(ks_ref[0, :, cols], query, NT) * (SCALE * LOG2E), NEG
                )
                top = jnp.maximum(top, jnp.max(near, axis=0, keepdims=True))
            raw = jnp.exp2(scores - top)
            spent = jnp.sum(raw, axis=0, keepdims=True)
            mixed = dot(vm_ref[0, :, cols], raw.astype(LOW), TN)
            if with_segment:
                raw_near = jnp.exp2(near - top)
                spent = spent + jnp.sum(raw_near, axis=0, keepdims=True)
                mixed = mixed + dot(vs_ref[0, :, cols], raw_near.astype(LOW), TN)
            out_ref[0, :, cols] = (mixed / spent).T.astype(LOW)
            total_ref[0, head : head + 1, :] = top + jnp.log2(spent)

    by_tier(own, meta_ref, body)


def attend(own, meta, q, km, vm, ks, vs):
    streams, rows, features = q.shape
    heads = features // HD
    outs = [shaped(q.shape), shaped((streams, heads, rows), WIDE)]
    return call(
        functools.partial(attend_kernel, own),
        (streams,),
        [scalars()] + [per_stream(a.shape) for a in (q, km, vm, ks, vs)],
        [per_stream(o.shape) for o in outs],
        outs,
        flops=8 * streams * rows * features * (km.shape[1] + rows),
        moved=4 * km.size + 8 * q.size,
    )(meta, q, km, vm, ks, vs)


def merge_kernel(own_ref, own_total_ref, other_ref, other_total_ref, w_ref, low_ref, total_ref, part_ref):
    first, second = own_total_ref[0], other_total_ref[0]
    top = jnp.maximum(first, second)
    total = top + jnp.log2(jnp.exp2(first - top) + jnp.exp2(second - top))
    total_ref[0] = total
    share_own, share_other = jnp.exp2(first - total), jnp.exp2(second - total)
    rows = own_ref.shape[1]
    for head in range(own_ref.shape[2] // HD):
        cols = slice(head * HD, (head + 1) * HD)
        column_own = jnp.broadcast_to(share_own[head : head + 1], (HD, rows)).T
        column_other = jnp.broadcast_to(share_other[head : head + 1], (HD, rows)).T
        merged = (
            own_ref[0, :, cols].astype(WIDE) * column_own
            + other_ref[0, :, cols].astype(WIDE) * column_other
        )
        low_ref[0, :, cols] = merged.astype(LOW)
    part_ref[0] = dot(low_ref[0], w_ref[...]).astype(LOW)


def merge(own, own_total, other, other_total, w_attn_out):
    streams, rows, features = own.shape
    outs = [
        shaped(own.shape),
        shaped(own_total.shape, WIDE),
        shaped((streams, rows, w_attn_out.shape[1])),
    ]
    return call(
        merge_kernel,
        (streams,),
        [per_stream(a.shape) for a in (own, own_total, other, other_total)]
        + [whole(w_attn_out.shape)],
        [per_stream(o.shape) for o in outs],
        outs,
        flops=2 * own.size * w_attn_out.shape[1],
        moved=6 * own.size + w_attn_out.size * 2,
    )(own, own_total, other, other_total, w_attn_out)


def valid_rows(meta_ref, streams, rows):
    place = lax.broadcasted_iota(jnp.int32, (streams * rows, 1), 0)
    ok = None
    for stream in range(streams):
        inside = (place >= stream * rows) & (
            place < stream * rows + meta_ref[1 + stream] - meta_ref[0] * rows
        ) & (place < (stream + 1) * rows)
        ok = inside if ok is None else ok | inside
    return ok


def ffn_kernel(first, streams, meta_ref, x_ref, a_ref, b_ref, cot_ref, gain_ref, bias_ref, wi_ref, wo_ref, *refs):
    if first:
        grads_ref, ffn_ref, back_ref, low_ref, grad_ref, ffn_acc, back_acc = refs
    else:
        ffn_in, back_in, grads_ref, ffn_ref, back_ref, low_ref, grad_ref, ffn_acc, back_acc = refs
    step = pl.program_id(0)
    units = wi_ref.shape[1]

    @pl.when(step == 0)
    def _():
        hidden = x_ref[...].astype(WIDE) + (a_ref[...].astype(WIDE) + b_ref[...].astype(WIDE))
        normed, _ = norm_stats(hidden)
        low_ref[...] = (normed * gain_ref[...] + bias_ref[...]).astype(LOW)
        ok = valid_rows(meta_ref, streams, x_ref.shape[0] // streams)
        grad_ref[...] = jnp.where(ok, cot_ref[...].astype(WIDE), 0.0).astype(LOW)
        if first:
            ffn_acc[...] = jnp.zeros_like(ffn_acc)
            back_acc[...] = jnp.zeros_like(back_acc)
        else:
            ffn_acc[...] = ffn_in[...]
            back_acc[...] = back_in[...]

    lifted = dot(low_ref[...], wi_ref[...])
    square = lifted * lifted
    bent = jnp.tanh(GELU_ROOT * lifted * (1.0 + GELU_CUBE * square))
    half = 0.5 * (1.0 + bent)
    activated = (lifted * half).astype(LOW)
    slope = half + 0.5 * lifted * (1.0 - bent * bent) * (
        GELU_ROOT * (1.0 + 3.0 * GELU_CUBE * square)
    )
    place = pl.multiple_of(step * units, units)
    grads_ref[0, pl.ds(place, units), :] = dot(activated, grad_ref[...], TN).astype(LOW)
    grad_activated = dot(grad_ref[...], wo_ref[...], NT)
    grad_lifted = (slope * grad_activated).astype(LOW)
    grads_ref[1, :, pl.ds(place, units)] = dot(low_ref[...], grad_lifted, TN).astype(LOW)
    ffn_acc[...] += dot(activated, wo_ref[...])
    back_acc[...] += dot(grad_lifted, wi_ref[...], NT)

    @pl.when(step == pl.num_programs(0) - 1)
    def _():
        ffn_ref[...] = ffn_acc[...].astype(ffn_ref.dtype)
        back_ref[...] = back_acc[...].astype(back_ref.dtype)


def ffn_half(part, streams, meta, x, a, b, cot, gain, bias, w_in, w_out, carried=()):
    rows, width = x.shape
    units = w_in.shape[1] // 2
    block = units // 2
    base = part * 2
    first = not carried
    kind = WIDE if first else LOW
    outs = [shaped((2, width, units)), shaped(x.shape, kind), shaped(x.shape, kind)]
    return call(
        functools.partial(ffn_kernel, first, streams),
        (2,),
        [scalars()]
        + [whole(v.shape) for v in (x, a, b, cot, gain, bias)]
        + [
            pl.BlockSpec((width, block), lambda j: (0, base + j)),
            pl.BlockSpec((block, width), lambda j: (base + j, 0)),
        ]
        + [whole(v.shape) for v in carried],
        [whole(o.shape) for o in outs],
        outs,
        scratch=[
            pltpu.VMEM(x.shape, LOW),
            pltpu.VMEM(x.shape, LOW),
            pltpu.VMEM(x.shape, WIDE),
            pltpu.VMEM(x.shape, WIDE),
        ],
        flops=12 * rows * width * units,
        moved=8 * rows * width + 8 * units * width,
        vmem=60,
    )(meta, x, a, b, cot, gain, bias, w_in, w_out, *carried)


def hidden_back_kernel(
    meta_ref,
    x_ref,
    a_ref,
    b_ref,
    back_ref,
    back_other_ref,
    ffn_ref,
    ffn_other_ref,
    cot_ref,
    merged_ref,
    total_ref,
    w_ref,
    gain_ref,
    out_ref,
    grad_hidden_ref,
    grad_merged_ref,
    stats_ref,
    grad_w_ref,
    vector_ref,
    w_acc,
):
    stream = pl.program_id(0)
    rows = x_ref.shape[1]
    hidden = x_ref[0].astype(WIDE) + (a_ref[0].astype(WIDE) + b_ref[0].astype(WIDE))
    normed, inverse = norm_stats(hidden)
    place = meta_ref[0] * rows + lax.broadcasted_iota(jnp.int32, (rows, 1), 0)
    ok = place < meta_ref[1 + stream]
    result = hidden + (ffn_ref[0].astype(WIDE) + ffn_other_ref[0].astype(WIDE))
    out_ref[0] = jnp.where(ok, result, 0.0).astype(LOW)
    back = back_ref[0].astype(WIDE) + back_other_ref[0].astype(WIDE)
    grad_out = jnp.where(ok, cot_ref[0].astype(WIDE), 0.0)
    grad_hidden = grad_out + norm_back(back, normed, inverse, gain_ref[...])
    grad_hidden_ref[0] = grad_hidden
    low = grad_hidden.astype(LOW)
    merged = merged_ref[0]
    grad_merged = dot(low, w_ref[...], NT).astype(LOW)
    grad_merged_ref[0] = grad_merged
    heads = merged.shape[1] // HD
    stats_ref[0, :heads, :] = total_ref[0]
    product = grad_merged.astype(WIDE) * merged.astype(WIDE)
    for head in range(heads):
        turned = product[:, head * HD : (head + 1) * HD].T
        stats_ref[0, heads + head : heads + head + 1, :] = jnp.sum(turned, axis=0, keepdims=True)
    grad_w = dot(merged, low, TN)
    gain_part = jnp.sum(back * normed, axis=0, keepdims=True)
    bias_part = jnp.sum(back, axis=0, keepdims=True)

    @pl.when(stream == 0)
    def _():
        w_acc[...] = grad_w
        vector_ref[0:1, :] = gain_part
        vector_ref[1:2, :] = bias_part

    @pl.when(stream != 0)
    def _():
        w_acc[...] += grad_w
        vector_ref[0:1, :] += gain_part
        vector_ref[1:2, :] += bias_part

    @pl.when(stream == pl.num_programs(0) - 1)
    def _():
        grad_w_ref[...] = w_acc[...].astype(LOW)


def hidden_back(meta, x, a, b, back, back_other, ffn, ffn_other, cot, merged, total, w, gain):
    streams, rows, width = x.shape
    heads = merged.shape[2] // HD
    outs = [
        shaped(x.shape),
        shaped(x.shape, WIDE),
        shaped(merged.shape),
        shaped((streams, 2 * heads, rows), WIDE),
        shaped(w.shape),
        shaped((2, width), WIDE),
    ]
    streamed = (x, a, b, back, back_other, ffn, ffn_other, cot, merged, total)
    return call(
        hidden_back_kernel,
        (streams,),
        [scalars()] + [per_stream(v.shape) for v in streamed] + [whole(w.shape), whole(gain.shape)],
        [per_stream(o.shape) for o in outs[:4]] + [whole(o.shape) for o in outs[4:]],
        outs,
        scratch=[pltpu.VMEM(w.shape, WIDE)],
        flops=4 * streams * rows * w.size,
        moved=24 * x.size,
    )(meta, *streamed, w, gain)


def attend_back_kernel(own, meta_ref, q_ref, gm_ref, stats_ref, km_ref, vm_ref, ks_ref, vs_ref, *refs):
    if own:
        gq_ref, gkm_ref, gvm_ref, gks_ref, gvs_ref = refs
        before = None
    else:
        before, (gq_ref, gkm_ref, gvm_ref, gks_ref, gvs_ref) = refs[:4], refs[4:]
    streams = pl.num_programs(0)
    stream = pl.program_id(0)
    slots, rows = km_ref.shape[1], q_ref.shape[1]
    heads = q_ref.shape[2] // HD

    def put(ref, index, cols, value):
        if before is not None:
            value = value + before[index][0, :, cols]
        ref[0, :, cols] = value.astype(ref.dtype)

    def body(with_segment):
        memory_ok, segment_ok = slot_masks(own, meta_ref, stream, streams, slots, rows)
        for head in range(heads):
            cols = slice(head * HD, (head + 1) * HD)
            query = q_ref[0, :, cols]
            grad = gm_ref[0, :, cols]
            total = stats_ref[0, head : head + 1, :]
            delta = stats_ref[0, heads + head : heads + head + 1, :]

            def tier(key, value, ok):
                scores = jnp.where(ok, dot(key, query, NT) * (SCALE * LOG2E), NEG)
                weights = jnp.exp2(scores - total)
                grad_scores = (weights * (dot(value, grad, NT) - delta)).astype(LOW)
                return (
                    dot(key, grad_scores, TN),
                    dot(grad_scores, query) * SCALE,
                    dot(weights.astype(LOW), grad),
                )

            turned, grad_key, grad_value = tier(km_ref[0, :, cols], vm_ref[0, :, cols], memory_ok)
            put(gkm_ref, 0, cols, grad_key)
            put(gvm_ref, 1, cols, grad_value)
            if with_segment:
                more, grad_key, grad_value = tier(
                    ks_ref[0, :, cols], vs_ref[0, :, cols], segment_ok
                )
                turned = turned + more
                put(gks_ref, 2, cols, grad_key)
                put(gvs_ref, 3, cols, grad_value)
            else:
                gks_ref[0, :, cols] = before[2][0, :, cols].astype(gks_ref.dtype)
                gvs_ref[0, :, cols] = before[3][0, :, cols].astype(gvs_ref.dtype)
            gq_ref[0, :, cols] = (turned * SCALE).T.astype(LOW)

    by_tier(own, meta_ref, body)


def attend_back(own, meta, q, gm, stats, km, vm, ks, vs, before=()):
    streams, rows, features = q.shape
    kind = WIDE if own else LOW
    outs = [shaped(q.shape)] + [shaped(a.shape, kind) for a in (km, vm, ks, vs)]
    return call(
        functools.partial(attend_back_kernel, own),
        (streams,),
        [scalars()] + [per_stream(a.shape) for a in (q, gm, stats, km, vm, ks, vs, *before)],
        [per_stream(o.shape) for o in outs],
        outs,
        flops=20 * streams * rows * features * (km.shape[1] + rows),
        moved=12 * km.size + 12 * q.size,
    )(meta, q, gm, stats, km, vm, ks, vs, *before)


def key_value_grads_kernel(
    unit_ref, stored_ref, gks_ref, gvs_ref, gkm_ref, gvm_ref, wk_ref, wv_ref, gain_ref, bias_ref,
    grads_ref, part_ref, column_ref, k_acc, v_acc, sums
):
    stream = pl.program_id(0)

    @pl.when(stream == 0)
    def _():
        k_acc[...] = jnp.zeros_like(k_acc)
        v_acc[...] = jnp.zeros_like(v_acc)
        sums[...] = jnp.zeros_like(sums)

    unit, stored = unit_ref[0], stored_ref[0]
    gks, gvs, gkm, gvm = gks_ref[0], gvs_ref[0], gkm_ref[0], gvm_ref[0]
    k_acc[...] += dot(unit, gks, TN) + dot(stored, gkm, TN)
    v_acc[...] += dot(unit, gvs, TN) + dot(stored, gvm, TN)
    for place, pair in enumerate(((gks, gkm), (gvs, gvm))):
        for piece in pair:
            sums[place : place + 1, :] += jnp.sum(piece.astype(WIDE), axis=0, keepdims=True)
    part_ref[0] = dot(gks, wk_ref[...], NT) + dot(gvs, wv_ref[...], NT)

    @pl.when(stream == pl.num_programs(0) - 1)
    def _():
        features = wk_ref.shape[1]
        gain, bias = gain_ref[...], bias_ref[...]
        grads_ref[:, :features] = (gain * k_acc[...] + bias * sums[0:1, :]).astype(LOW)
        grads_ref[:, features:] = (gain * v_acc[...] + bias * sums[1:2, :]).astype(LOW)
        wk, wv = wk_ref[...].astype(WIDE), wv_ref[...].astype(WIDE)
        column_ref[:, 0:1] = jnp.sum(wk * k_acc[...] + wv * v_acc[...], axis=1, keepdims=True)
        column_ref[:, 1:2] = jnp.sum(wk * sums[0:1, :] + wv * sums[1:2, :], axis=1, keepdims=True)


def key_value_grads(unit, stored, gks, gvs, gkm, gvm, wk, wv, gain, bias):
    width, features = wk.shape
    outs = [shaped((width, 2 * features)), shaped(unit.shape, WIDE), shaped((width, 2), WIDE)]
    streamed = (unit, stored, gks, gvs, gkm, gvm)
    fixed = (wk, wv, gain, bias)
    return call(
        key_value_grads_kernel,
        (unit.shape[0],),
        [per_stream(v.shape) for v in streamed] + [whole(v.shape) for v in fixed],
        [whole(outs[0].shape), per_stream(outs[1].shape), whole(outs[2].shape)],
        outs,
        scratch=[
            pltpu.VMEM(wk.shape, WIDE),
            pltpu.VMEM(wk.shape, WIDE),
            pltpu.VMEM((2, features), WIDE),
        ],
        flops=4 * (unit.size * 2 + stored.size) * features,
        moved=2 * (unit.size * 3 + stored.size) + 8 * wk.size,
    )(*streamed, *fixed)


def query_grads_kernel(
    unit_ref, own_ref, other_ref, part_ref, wq_ref, gain_ref, bias_ref, column_in_ref,
    grads_ref, normed_ref, column_ref, q_acc, sums
):
    stream = pl.program_id(0)

    @pl.when(stream == 0)
    def _():
        q_acc[...] = jnp.zeros_like(q_acc)
        sums[...] = jnp.zeros_like(sums)

    wide = own_ref[0].astype(WIDE) + other_ref[0].astype(WIDE)
    grad = wide.astype(LOW)
    q_acc[...] += dot(unit_ref[0], grad, TN)
    sums[...] += jnp.sum(grad.astype(WIDE), axis=0, keepdims=True)
    normed_ref[0] = (part_ref[0] + dot(grad, wq_ref[...], NT)).astype(LOW)

    @pl.when(stream == pl.num_programs(0) - 1)
    def _():
        grads_ref[...] = (gain_ref[...] * q_acc[...] + bias_ref[...] * sums[...]).astype(LOW)
        wq = wq_ref[...].astype(WIDE)
        column_ref[:, 0:1] = column_in_ref[:, 0:1] + jnp.sum(
            wq * q_acc[...], axis=1, keepdims=True
        )
        column_ref[:, 1:2] = column_in_ref[:, 1:2] + jnp.sum(
            wq * sums[...], axis=1, keepdims=True
        )


def query_grads(unit, own, other, part, wq, gain, bias, column):
    outs = [shaped(wq.shape), shaped(unit.shape), shaped(column.shape, WIDE)]
    streamed = (unit, own, other, part)
    fixed = (wq, gain, bias, column)
    return call(
        query_grads_kernel,
        (unit.shape[0],),
        [per_stream(v.shape) for v in streamed] + [whole(v.shape) for v in fixed],
        [whole(outs[0].shape), per_stream(outs[1].shape), whole(outs[2].shape)],
        outs,
        scratch=[pltpu.VMEM(wq.shape, WIDE), pltpu.VMEM((1, wq.shape[1]), WIDE)],
        flops=4 * unit.size * wq.shape[1],
        moved=10 * unit.size + 8 * wq.size,
    )(*streamed, *fixed)


def input_back_kernel(x_ref, own_ref, other_ref, hidden_ref, gain_ref, out_ref):
    normed, inverse = norm_stats(x_ref[0].astype(WIDE))
    grad = own_ref[0].astype(WIDE) + other_ref[0].astype(WIDE)
    out_ref[0] = (hidden_ref[0] + norm_back(grad, normed, inverse, gain_ref[...])).astype(LOW)


def input_back(x, own, other, grad_hidden, gain):
    streamed = (x, own, other, grad_hidden)
    return call(
        input_back_kernel,
        (x.shape[0],),
        [per_stream(v.shape) for v in streamed] + [whole(gain.shape)],
        per_stream(x.shape),
        shaped(x.shape),
        flops=30 * x.size,
        moved=12 * x.size,
    )(*streamed, gain)


def compress_kernel(meta_ref, own_ref, other_ref, w_ref, cot_ref, out_ref, grad_ref, acc):
    stream = pl.program_id(0)
    streams = pl.num_programs(0)
    head = meta_ref[1 + 2 * streams]
    slots, part = own_ref.shape[1], own_ref.shape[2]
    count = out_ref.shape[1]
    place = lax.broadcasted_iota(jnp.int32, (count, slots), 0)
    slot = lax.broadcasted_iota(jnp.int32, (count, slots), 1)
    ok = lax.broadcasted_iota(jnp.int32, (count, 1), 0) < meta_ref[1 + stream] // RATE
    cot = jnp.where(ok, cot_ref[0].astype(WIDE), 0.0).astype(LOW)

    @pl.when(stream == 0)
    def _():
        acc[...] = jnp.zeros_like(acc)

    result = jnp.zeros(out_ref.shape[1:], WIDE)
    for shift in range(RATE):
        pick = jnp.where(slot == place * RATE + shift, 1.0, 0.0).astype(LOW)
        for ref, side in ((own_ref, head), (other_ref, 1 - head)):
            rows = dot(pick, ref[0]).astype(LOW)
            start = pl.multiple_of(side * part, part)
            result = result + dot(rows, w_ref[shift, pl.ds(start, part), :])
            acc[shift, pl.ds(start, part), :] += dot(rows, cot, TN)
    out_ref[0] = jnp.where(ok, result, 0.0).astype(LOW)

    @pl.when(stream == streams - 1)
    def _():
        grad_ref[...] = acc[...].astype(LOW)


def compress(meta, own, other, w, cot):
    streams = own.shape[0]
    outs = [shaped(cot.shape), shaped(w.shape)]
    return call(
        compress_kernel,
        (streams,),
        [scalars(), per_stream(own.shape), per_stream(other.shape), whole(w.shape), per_stream(cot.shape)],
        [per_stream(cot.shape), whole(w.shape)],
        outs,
        scratch=[pltpu.VMEM(w.shape, WIDE)],
        flops=4 * cot.shape[0] * cot.shape[1] * w.size,
        moved=4 * own.size + 4 * w.size,
    )(meta, own, other, w, cot)


def bits_of():
    size = lax.axis_size("dp")
    bits = [("tier", 1)]
    step = 1
    while step < size:
        bits.append(("dp", step))
        step *= 2
    return bits


def bit_value(bit):
    axis, step = bit
    return (lax.axis_index(axis) // step) % 2


def swap(value, bit):
    axis, step = bit
    return lax.ppermute(value, axis, [(i, i ^ step) for i in range(lax.axis_size(axis))])


def swap_head(value):
    return swap(value, ("head", 1))


def swap_tier(value):
    return swap(value, ("tier", 1))


def add_low(first, second):
    total = first.astype(WIDE) + second.astype(WIDE)
    return lax.optimization_barrier(total.astype(LOW))


def all_reduce(value, order):
    held = value
    scattered = []
    for place, bit in enumerate(order):
        half = held.shape[0] // 2
        if place == len(order) - 1 or half % 16:
            held = add_low(held, swap(held, bit))
        else:
            side = bit_value(bit)
            sent = lax.dynamic_slice_in_dim(held, (1 - side) * half, half, 0)
            kept = lax.dynamic_slice_in_dim(held, side * half, half, 0)
            held = add_low(kept, swap(sent, bit))
            scattered.append((bit, side))
    for bit, side in reversed(scattered):
        other = swap(held, bit)
        held = jnp.where(
            side == 0, jnp.concatenate([held, other], 0), jnp.concatenate([other, held], 0)
        )
    return held


def reduce_parts(low, sizes):
    tier, *rest = bits_of()
    orders = (
        [tier, *rest],
        [rest[0], rest[1], tier, *rest[2:]],
        [rest[1], tier, rest[0], *rest[2:]],
    )
    start = 0
    pieces = []
    for size, order in zip(sizes, orders):
        pieces.append(all_reduce(low[start : start + size], order))
        start += size
    return jnp.concatenate(pieces, 0)


def on_device(
    inputs,
    memories,
    seg_len,
    mem_count,
    w_query,
    w_key,
    w_value,
    w_attn_out,
    w_ffn_in,
    w_ffn_out,
    w_compress,
    gain_attn,
    bias_attn,
    gain_ffn,
    bias_ffn,
    cotan_output,
    cotan_compressed,
):
    tier_index = lax.axis_index("tier")
    head_index = lax.axis_index("head")
    streams, rows, width = inputs.shape
    features = w_query.shape[1]
    counts = mem_count[:, 0]
    meta = jnp.concatenate(
        [tier_index[None], seg_len, counts, head_index[None]], 0
    ).astype(jnp.int32)
    gain_row, bias_row = gain_attn[None], bias_attn[None]
    gain_second, bias_second = gain_ffn[None], bias_ffn[None]

    unit, queries, keys, values = project(inputs, gain_row, bias_row, (w_query, w_key, w_value))
    queries_other = swap_tier(queries)
    stored, memory_keys, memory_values = project(memories, gain_row, bias_row, (w_key, w_value))
    tiers = (memory_keys, memory_values, keys, values)
    part_other, part_other_total = attend(False, meta, queries_other, *tiers)
    came, came_total = swap_tier(part_other), swap_tier(part_other_total)
    part_own, part_own_total = attend(True, meta, queries, *tiers)
    merged, totals, attended = merge(part_own, part_own_total, came, came_total, w_attn_out)
    attended_other = swap_head(attended)

    flat = (streams * rows, width)
    ffn_args = (
        inputs.reshape(flat),
        attended.reshape(flat),
        attended_other.reshape(flat),
        cotan_output.reshape(flat),
        gain_second,
        bias_second,
        w_ffn_in,
        w_ffn_out,
    )
    grads_first, ffn_wide, back_wide = ffn_half(0, streams, meta, *ffn_args)
    grads_second, ffn_part, back_part = ffn_half(
        1, streams, meta, *ffn_args, carried=(ffn_wide, back_wide)
    )
    ffn_part, back_part = ffn_part.reshape(inputs.shape), back_part.reshape(inputs.shape)
    back_other = swap_head(back_part)
    ffn_other = swap_head(ffn_part)

    layer_output, grad_hidden, grad_merged, stats, grad_attn_out, vectors_ffn = hidden_back(
        meta,
        inputs,
        attended,
        attended_other,
        back_part,
        back_other,
        ffn_part,
        ffn_other,
        cotan_output,
        merged,
        totals,
        w_attn_out,
        gain_second,
    )
    grad_merged_other, stats_other = swap_tier(grad_merged), swap_tier(stats)
    own_query, *sums = attend_back(True, meta, queries, grad_merged, stats, *tiers)
    other_query, grad_km, grad_vm, grad_ks, grad_vs = attend_back(
        False, meta, queries_other, grad_merged_other, stats_other, *tiers, before=tuple(sums)
    )
    came_query = swap_tier(other_query)
    grad_key_value, normed_part, column = key_value_grads(
        unit, stored, grad_ks, grad_vs, grad_km, grad_vm, w_key, w_value,
        gain_attn[:, None], bias_attn[:, None],
    )
    grad_query, normed_low, column = query_grads(
        unit, own_query, came_query, normed_part, w_query,
        gain_attn[:, None], bias_attn[:, None], column,
    )
    grad_inputs = input_back(inputs, normed_low, swap_head(normed_low), grad_hidden, gain_row)

    slots = memories.shape[2]
    slot_valid = (jnp.arange(slots)[None, :] < counts[:, None])[..., None]
    half = width // 2
    evicted = lax.dynamic_slice_in_dim(memories[:, 0], head_index * half, half, 2)
    evicted = jnp.where(slot_valid, evicted, jnp.zeros_like(evicted))
    evicted_came = lax.ppermute(evicted, "tier", [(0, 1)])
    evicted = jnp.where(tier_index == 0, evicted, evicted_came)
    compressed, grad_compress_low = compress(
        meta, evicted, swap_head(evicted), w_compress, cotan_compressed
    )
    grad_compress = all_reduce(
        grad_compress_low.reshape(RATE * width, -1), bits_of()[1:]
    )

    first = reduce_parts(grads_first.reshape(2 * width, -1), (512, 768, 768))
    second = reduce_parts(grads_second.reshape(2 * width, -1), (512, 768, 768))
    third = reduce_parts(
        jnp.concatenate([grad_key_value, grad_attn_out], 0), (512, 512, 512)
    )
    fourth = reduce_parts(grad_query, (256, 384, 384))
    grad_ffn_out = jnp.concatenate([first[:width], second[:width]], 0).astype(WIDE)
    grad_ffn_in = jnp.concatenate([first[width:], second[width:]], 1).astype(WIDE)
    vectors = lax.psum(
        jnp.concatenate([column.T, 0.5 * vectors_ffn], axis=0), ("dp", "tier", "head")
    )
    return (
        layer_output,
        compressed,
        grad_inputs,
        fourth.astype(WIDE),
        third[:width, :features].astype(WIDE),
        third[:width, features:].astype(WIDE),
        third[width:].astype(WIDE),
        grad_ffn_in,
        grad_ffn_out,
        grad_compress.astype(WIDE).reshape(RATE, width, -1),
        vectors[0],
        vectors[1],
        vectors[2],
        vectors[3],
    )


def solution(mesh):
    return jax.shard_map(
        on_device,
        mesh=mesh,
        in_specs=(
            P("dp", "tier", None),
            P("dp", "tier", None, None),
            P("dp"),
            P("dp", "tier"),
            P(None, "head"),
            P(None, "head"),
            P(None, "head"),
            P("head", None),
            P(None, "head"),
            P("head", None),
            P(None, None, ("tier", "head")),
            P(),
            P(),
            P(),
            P(),
            P("dp", "tier", None),
            P("dp", None, ("tier", "head")),
        ),
        out_specs=(
            P("dp", "tier", None),
            P("dp", None, ("tier", "head")),
            P("dp", "tier", None),
            P(None, "head"),
            P(None, "head"),
            P(None, "head"),
            P("head", None),
            P(None, "head"),
            P("head", None),
            P(None, None, ("tier", "head")),
            P(),
            P(),
            P(),
            P(),
        ),
        check_vma=False,
    )
```

```python
import functools

import jax
import jax.numpy as jnp
from jax import lax
from jax.experimental import pallas as pl
from jax.experimental.pallas import tpu as pltpu
from jax.sharding import PartitionSpec as P

HD = 128
RATE = 3
EPS = 1e-05
NEG = -1000000000.0
LOG2E = 1.4426950408889634
SCALE = HD ** (-0.5)
GELU_ROOT = 0.7978845608028654
GELU_CUBE = 0.044715

ORDER = (
    "ffn", "hidden", "own", "ffn3", "output", "other", "f1", "f2", "grads", "evict", "f1",
    "query", "kv", "input", "f1", "kv", "f2", "kv", "f1", "f2", "oq", "evict2", "kv", "compr",
    "f1", "kv", "oq", "f2", "oq", "compress", "kv", "f2", "oq", "f1", "compress", "oq", "f2",
    "kv", "compress", "oq", "compress", "f1", "oq", "compress", "f2",
)

PATHS = {
    "f1": "xyz/yzx",
    "f2": "zyx/yxz",
    "kv": "xzy/zxy",
    "oq": "zxy/xyz",
    "compress": "yz/zy",
}

COST = 1e8
VMEM_WIDE = 40

LOW = jnp.bfloat16
WIDE = jnp.float32
NN = (((1,), (0,)), ((), ()))
NT = (((1,), (1,)), ((), ()))
TN = (((0,), (0,)), ((), ()))


def dot(first, second, dims=NN):
    return lax.dot_general(first, second, dims, preferred_element_type=WIDE)


def norm_stats(values):
    centre = values - jnp.mean(values, axis=-1, keepdims=True)
    inverse = lax.rsqrt(jnp.mean(centre * centre, axis=-1, keepdims=True) + EPS)
    return (centre * inverse, inverse)


def norm_back(grad_normed, normed, inverse, gain_vector):
    scaled = grad_normed * gain_vector
    return inverse * (
        scaled
        - jnp.mean(scaled, axis=-1, keepdims=True)
        - normed * jnp.mean(scaled * normed, axis=-1, keepdims=True)
    )


def per_stream(array_shape):
    block = (1,) + tuple(array_shape[1:])
    zeros = (0,) * (len(block) - 1)
    return pl.BlockSpec(block, lambda s: (s,) + zeros)


def whole(array_shape):
    return pl.BlockSpec(memory_space=pltpu.VMEM)


def whole_block(array_shape):
    zeros = (0,) * len(array_shape)
    return pl.BlockSpec(tuple(array_shape), lambda *_: zeros)


def scalars():
    return pl.BlockSpec(memory_space=pltpu.SMEM)


def shaped(shape, dtype=LOW):
    return jax.ShapeDtypeStruct(tuple(shape), dtype)


class Chain:
    def __init__(self):
        self.last = None

    def call(self, kernel, grid, in_specs, out_specs, out_shape, scratch=(), vmem=16, alias=None, us=1.0):
        last = self.last
        count = len(in_specs)

        def ordered(*refs):
            kernel(*refs[:count], *refs[count + 1 :])

        def run(*args):
            specs = list(in_specs)
            args = list(args)
            body = kernel
            if last is not None:
                specs.append(pl.BlockSpec(memory_space=pl.ANY))
                args.append(last)
                body = ordered
            outs = pl.pallas_call(
                body,
                grid=grid,
                in_specs=specs,
                out_specs=out_specs,
                out_shape=out_shape,
                scratch_shapes=list(scratch),
                input_output_aliases=alias or {},
                compiler_params=pltpu.CompilerParams(vmem_limit_bytes=vmem * 1024 * 1024),
                cost_estimate=pl.CostEstimate(
                    flops=int(us * COST), bytes_accessed=0, transcendentals=0
                ),
            )(*args)
            if not alias:
                self.last = outs[0] if isinstance(outs, (list, tuple)) else outs
            return outs

        return run


META_TIER, META_HEAD, META_DP, META_STREAMS = 0, 1, 2, 3


def any_spec():
    return pl.BlockSpec(memory_space=pl.ANY)


def query_kernel(meta_ref, x_ref, gain_ref, bias_ref, w_ref, unit_ref, low_ref, *outs):
    for stream in range(x_ref.shape[0]):
        normed, _ = norm_stats(x_ref[stream].astype(WIDE))
        unit_ref[stream] = normed.astype(LOW)
        low = (normed * gain_ref[...] + bias_ref[...]).astype(LOW)
        low_ref[stream] = low
        outs[stream][...] = dot(low, w_ref[...]).astype(LOW)


def query_rows(chain, meta, x, gain, bias, w):
    streams, rows, width = x.shape
    outs = [shaped(x.shape), shaped(x.shape)]
    outs += [shaped((rows, w.shape[1]))] * streams
    unit, low, *queries = chain.call(
        query_kernel,
        (1,),
        [scalars()] + [whole(v.shape) for v in (x, gain, bias, w)],
        [whole(o.shape) for o in outs],
        outs,
        us=3,
    )(meta, x, gain, bias, w)
    return unit, low, queries


def key_value_kernel(low_ref, wk_ref, wv_ref, k_ref, v_ref):
    k_ref[0] = dot(low_ref[0], wk_ref[...]).astype(LOW)
    v_ref[0] = dot(low_ref[0], wv_ref[...]).astype(LOW)


def key_values(chain, low, wk, wv):
    outs = [shaped(low.shape[:2] + wk.shape[1:])] * 2
    return chain.call(
        key_value_kernel,
        (low.shape[0],),
        [per_stream(low.shape), whole(wk.shape), whole(wv.shape)],
        [per_stream(o.shape) for o in outs],
        outs,
        us=2.5,
    )(low, wk, wv)


def stored_kernel(x_ref, gain_ref, bias_ref, wk_ref, wv_ref, unit_ref, k_ref, v_ref):
    normed, _ = norm_stats(x_ref[0, 0].astype(WIDE))
    unit_ref[0] = normed.astype(LOW)
    low = (normed * gain_ref[...] + bias_ref[...]).astype(LOW)
    k_ref[0] = dot(low, wk_ref[...]).astype(LOW)
    v_ref[0] = dot(low, wv_ref[...]).astype(LOW)


def stored_rows(chain, x, gain, bias, wk, wv):
    streams, _, slots, width = x.shape
    outs = [shaped((streams, slots, width))] + [shaped((streams, slots, wk.shape[1]))] * 2
    return chain.call(
        stored_kernel,
        (streams,),
        [per_stream(x.shape)] + [whole(v.shape) for v in (gain, bias, wk, wv)],
        [per_stream(o.shape) for o in outs],
        outs,
        us=6,
    )(x, gain, bias, wk, wv)


def slot_masks(own, meta_ref, stream, streams, slots, rows):
    tier = meta_ref[META_TIER]
    length = meta_ref[META_STREAMS + stream]
    filled = meta_ref[META_STREAMS + streams + stream]
    memory_ok = lax.broadcasted_iota(jnp.int32, (slots, rows), 0) < filled
    key_row = lax.broadcasted_iota(jnp.int32, (rows, rows), 0)
    segment_ok = (tier * rows + key_row) < length
    if own:
        query_row = lax.broadcasted_iota(jnp.int32, (rows, rows), 1)
        segment_ok = segment_ok & (key_row <= query_row)
    return memory_ok, segment_ok


def by_tier(own, meta_ref, body):
    if own:
        body(True)
        return

    @pl.when(meta_ref[META_TIER] == 0)
    def _():
        body(True)

    @pl.when(meta_ref[META_TIER] != 0)
    def _():
        body(False)


def put_packed(ref, row, value):
    count, width = value.shape
    for part in range(3):
        low = value.astype(LOW)
        ref[row + part * count : row + (part + 1) * count, :width] = low
        value = value - low.astype(WIDE)


def get_packed(ref, row, count, width):
    parts = [
        ref[row + part * count : row + (part + 1) * count, :width].astype(WIDE) for part in range(3)
    ]
    return parts[0] + (parts[1] + parts[2])


def packed_rows(count):
    return -(-3 * count // 16) * 16


def attend_kernel(own, stream, streams, meta_ref, q_ref, km_ref, vm_ref, ks_ref, vs_ref, out_ref, totals):
    slots, rows = km_ref.shape[1], q_ref.shape[0]
    heads = q_ref.shape[1] // HD

    def body(with_segment):
        memory_ok, segment_ok = slot_masks(own, meta_ref, stream, streams, slots, rows)
        for head in range(heads):
            cols = slice(head * HD, (head + 1) * HD)
            query = q_ref[:, cols]
            scores = jnp.where(
                memory_ok, dot(km_ref[0, :, cols], query, NT) * (SCALE * LOG2E), NEG
            )
            top = jnp.max(scores, axis=0, keepdims=True)
            if with_segment:
                near = jnp.where(
                    segment_ok, dot(ks_ref[0, :, cols], query, NT) * (SCALE * LOG2E), NEG
                )
                top = jnp.maximum(top, jnp.max(near, axis=0, keepdims=True))
            raw = jnp.exp2(scores - top)
            spent = jnp.sum(raw, axis=0, keepdims=True)
            mixed = dot(vm_ref[0, :, cols], raw.astype(LOW), TN)
            if with_segment:
                raw_near = jnp.exp2(near - top)
                spent = spent + jnp.sum(raw_near, axis=0, keepdims=True)
                mixed = mixed + dot(vs_ref[0, :, cols], raw_near.astype(LOW), TN)
            out_ref[:rows, cols] = (mixed / spent).T.astype(LOW)
            totals[head : head + 1, :] = top + jnp.log2(spent)
        put_packed(out_ref, rows, totals[...])

    by_tier(own, meta_ref, body)


def one_stream(array, stream):
    return pl.BlockSpec((1,) + array.shape[1:], lambda i: (stream, 0, 0))


def attend(chain, own, stream, meta, q, km, vm, ks, vs):
    rows, features = q.shape
    heads = features // HD
    out = shaped((rows + packed_rows(heads), features))
    return chain.call(
        functools.partial(attend_kernel, own, stream, km.shape[0]),
        (1,),
        [scalars(), whole(q.shape)] + [one_stream(a, stream) for a in (km, vm, ks, vs)],
        whole(out.shape),
        out,
        scratch=[pltpu.VMEM((heads, rows), WIDE)],
        us=2.6,
    )(meta, q, km, vm, ks, vs)


def merge_kernel(w_ref, own_ref, other_ref, low_ref, total_ref, part_ref):
    rows, features = low_ref.shape
    heads = features // HD
    first = get_packed(own_ref, rows, heads, rows)
    second = get_packed(other_ref, rows, heads, rows)
    top = jnp.maximum(first, second)
    total = top + jnp.log2(jnp.exp2(first - top) + jnp.exp2(second - top))
    total_ref[...] = total
    share_own, share_other = jnp.exp2(first - total), jnp.exp2(second - total)
    for head in range(heads):
        cols = slice(head * HD, (head + 1) * HD)
        column_own = jnp.broadcast_to(share_own[head : head + 1], (HD, rows)).T
        column_other = jnp.broadcast_to(share_other[head : head + 1], (HD, rows)).T
        merged = (
            own_ref[:rows, cols].astype(WIDE) * column_own
            + other_ref[:rows, cols].astype(WIDE) * column_other
        )
        low_ref[:, cols] = merged.astype(LOW)
    part_ref[...] = dot(low_ref[...], w_ref[...]).astype(LOW)


def merge(chain, rows, own, other, w):
    features = own.shape[1]
    outs = [
        shaped((rows, features)),
        shaped((features // HD, rows), WIDE),
        shaped((rows, w.shape[1])),
    ]
    args = (w, own, other)
    return chain.call(
        merge_kernel,
        (1,),
        [whole(v.shape) for v in args],
        [whole(o.shape) for o in outs],
        outs,
        us=1.0,
    )(*args)


def evicted_kernel(streams, meta_ref, memory_ref, evicted_ref):
    part = evicted_ref.shape[2]
    start = pl.multiple_of(meta_ref[META_HEAD] * part, part)
    filled = meta_ref[META_STREAMS + streams + pl.program_id(0)]
    ok = lax.broadcasted_iota(jnp.int32, (evicted_ref.shape[1], 1), 0) < filled
    rows = memory_ref[0, 0, :, pl.ds(start, part)].astype(WIDE)
    evicted_ref[0] = jnp.where(ok, rows, 0.0).astype(LOW)


def evicted_rows(chain, meta, memories):
    streams, _, slots, width = memories.shape
    out = (streams, slots, width // 2)
    return chain.call(
        functools.partial(evicted_kernel, streams),
        (streams,),
        [scalars(), per_stream(memories.shape)],
        per_stream(out),
        shaped(out),
        us=2,
    )(meta, memories)


def copied_kernel(in_ref, out_ref):
    out_ref[...] = in_ref[...]


def copied(chain, array):
    return chain.call(
        copied_kernel, (1,), [whole(array.shape)], whole(array.shape), shaped(array.shape)
    )(array)


def valid_rows(meta_ref, streams, rows):
    place = lax.broadcasted_iota(jnp.int32, (streams * rows, 1), 0)
    ok = None
    for stream in range(streams):
        inside = (
            (place >= stream * rows)
            & (place < stream * rows + meta_ref[META_STREAMS + stream] - meta_ref[META_TIER] * rows)
            & (place < (stream + 1) * rows)
        )
        ok = inside if ok is None else ok | inside
    return ok


def side_of(meta_ref, bit):
    axis, step = bit
    if axis == "tier":
        return meta_ref[META_TIER]
    return lax.rem(lax.div(meta_ref[META_DP], jnp.int32(step)), jnp.int32(2))


def pair_side(meta_ref, bits):
    first, second = (side_of(meta_ref, bit) for bit in bits)
    return jnp.where(meta_ref[META_HEAD] == 0, first, second)


def ffn_kernel(streams, bits, meta_ref, *refs):
    x_ref, a_ref, b_ref, cot_ref, gain_ref, bias_ref, wi_ref, wo_ref = refs[:8]
    act_ref, back_ref = refs[8:10]
    parts, (low_ref, turned_ref, grad_ref, back_acc) = refs[10:-4], refs[-4:]
    step = pl.program_id(0)
    units = wi_ref.shape[1]

    @pl.when(step == 0)
    def _():
        hidden = x_ref[...].astype(WIDE) + (a_ref[...].astype(WIDE) + b_ref[...].astype(WIDE))
        normed, _ = norm_stats(hidden)
        low = (normed * gain_ref[...] + bias_ref[...]).astype(LOW)
        low_ref[...] = low
        turned_ref[...] = low.T
        ok = valid_rows(meta_ref, streams, x_ref.shape[0] // streams)
        grad_ref[...] = jnp.where(ok, cot_ref[...].astype(WIDE), 0.0).astype(LOW)

    lifted = dot(low_ref[...], wi_ref[...])
    square = lifted * lifted
    bent = jnp.tanh(GELU_ROOT * lifted * (1.0 + GELU_CUBE * square))
    half = 0.5 * (1.0 + bent)
    activated = (lifted * half).astype(LOW)
    act_ref[...] = activated
    slope = half + 0.5 * lifted * (1.0 - bent * bent) * (
        GELU_ROOT * (1.0 + 3.0 * GELU_CUBE * square)
    )
    grad_out = dot(activated, grad_ref[...], TN).astype(LOW)
    grad_lifted = (slope * dot(grad_ref[...], wo_ref[...], NT)).astype(LOW)
    grad_in = dot(turned_ref[...], grad_lifted).astype(LOW)
    place = pl.multiple_of((step % 2) * units, units)
    for part in range(2):
        sent, kept = parts[2 * part : 2 * part + 2]
        side = pair_side(meta_ref, bits[part])
        for out_ref, in_ref, which in ((kept, sent, 0), (sent, kept, 1)):

            @pl.when((step // 2 == part) & (side == which))
            def _():
                out_ref[pl.ds(place, units), :] = grad_out
                in_ref[:, pl.ds(place, units)] = grad_in

    more = dot(grad_lifted, wi_ref[...], NT)

    @pl.when(step == 0)
    def _():
        back_acc[...] = more

    @pl.when(step != 0)
    def _():
        back_acc[...] += more

    @pl.when(step == pl.num_programs(0) - 1)
    def _():
        back_ref[...] = back_acc[...].astype(LOW)


def ffn(chain, streams, orders, meta, whole_args, w_in, w_out):
    rows, width = whole_args[0].shape
    units = w_in.shape[1]
    steps = 4
    block = units // steps
    outs = [shaped((rows, units)), shaped((rows, width))]
    parts = [shaped((units // 2, width))] * 4
    turned = pltpu.VMEM((width, rows), LOW)
    return chain.call(
        functools.partial(ffn_kernel, streams, tuple((p[0][0], p[1][0]) for p in orders)),
        (steps,),
        [scalars()]
        + [whole(v.shape) for v in whole_args]
        + [
            pl.BlockSpec((width, block), lambda j: (0, j)),
            pl.BlockSpec((block, width), lambda j: (j, 0)),
        ],
        [pl.BlockSpec((rows, block), lambda j: (0, j)), whole((rows, width))]
        + [whole(o.shape) for o in parts],
        outs + parts,
        scratch=[
            pltpu.VMEM((rows, width), LOW),
            turned,
            pltpu.VMEM((rows, width), LOW),
            pltpu.VMEM((rows, width), WIDE),
        ],
        vmem=32,
        us=24,
    )(meta, *whole_args, w_in, w_out)


def ffn_out_kernel(act_ref, w_ref, out_ref, acc):
    step = pl.program_id(0)
    more = dot(act_ref[...], w_ref[...])

    @pl.when(step == 0)
    def _():
        acc[...] = more

    @pl.when(step != 0)
    def _():
        acc[...] += more

    @pl.when(step == pl.num_programs(0) - 1)
    def _():
        out_ref[...] = acc[...].astype(LOW)


def ffn_out(chain, act, w):
    rows, units = act.shape
    width = w.shape[1]
    steps = 4
    block = units // steps
    return chain.call(
        ffn_out_kernel,
        (steps,),
        [pl.BlockSpec((rows, block), lambda j: (0, j)), pl.BlockSpec((block, width), lambda j: (j, 0))],
        whole((rows, width)),
        shaped((rows, width)),
        scratch=[pltpu.VMEM((rows, width), WIDE)],
        us=4,
    )(act, w)


def output_kernel(meta_ref, x_ref, a_ref, b_ref, own_ref, other_ref, out_ref):
    rows = x_ref.shape[1]
    place = meta_ref[META_TIER] * rows + lax.broadcasted_iota(jnp.int32, (rows, 1), 0)
    ok = place < meta_ref[META_STREAMS + pl.program_id(0)]
    hidden = x_ref[0].astype(WIDE) + (a_ref[0].astype(WIDE) + b_ref[0].astype(WIDE))
    result = hidden + (own_ref[0].astype(WIDE) + other_ref[0].astype(WIDE))
    out_ref[0] = jnp.where(ok, result, 0.0).astype(LOW)


def output_rows(chain, meta, *streamed):
    shape = streamed[0].shape
    return chain.call(
        output_kernel,
        (shape[0],),
        [scalars()] + [per_stream(v.shape) for v in streamed],
        per_stream(shape),
        shaped(shape),
        us=3,
    )(meta, *streamed)


def hidden_back_kernel(
    meta_ref,
    x_ref,
    a_ref,
    b_ref,
    back_ref,
    back_other_ref,
    cot_ref,
    merged_ref,
    total_ref,
    w_ref,
    gain_ref,
    grad_hidden_ref,
    grad_merged_ref,
    grad_w_ref,
    vector_ref,
    w_acc,
    stats,
):
    stream = pl.program_id(0)
    rows = x_ref.shape[1]
    hidden = x_ref[0].astype(WIDE) + (a_ref[0].astype(WIDE) + b_ref[0].astype(WIDE))
    normed, inverse = norm_stats(hidden)
    place = meta_ref[META_TIER] * rows + lax.broadcasted_iota(jnp.int32, (rows, 1), 0)
    ok = place < meta_ref[META_STREAMS + stream]
    back = back_ref[0].astype(WIDE) + back_other_ref[0].astype(WIDE)
    grad_out = jnp.where(ok, cot_ref[0].astype(WIDE), 0.0)
    grad_hidden = grad_out + norm_back(back, normed, inverse, gain_ref[...])
    grad_hidden_ref[0] = grad_hidden
    low = grad_hidden.astype(LOW)
    merged = merged_ref[0]
    grad_merged = dot(low, w_ref[...], NT).astype(LOW)
    grad_merged_ref[0, :rows, :] = grad_merged
    heads = merged.shape[1] // HD
    stats[:heads, :] = total_ref[0]
    product = grad_merged.astype(WIDE) * merged.astype(WIDE)
    for head in range(heads):
        turned = product[:, head * HD : (head + 1) * HD].T
        stats[heads + head : heads + head + 1, :] = jnp.sum(turned, axis=0, keepdims=True)
    put_packed(grad_merged_ref.at[0], rows, stats[...])
    grad_w = dot(merged, low, TN)
    gain_part = jnp.sum(back * normed, axis=0, keepdims=True)
    bias_part = jnp.sum(back, axis=0, keepdims=True)

    @pl.when(stream == 0)
    def _():
        w_acc[...] = grad_w
        vector_ref[0:1, :] = gain_part
        vector_ref[1:2, :] = bias_part

    @pl.when(stream != 0)
    def _():
        w_acc[...] += grad_w
        vector_ref[0:1, :] += gain_part
        vector_ref[1:2, :] += bias_part

    @pl.when(stream == pl.num_programs(0) - 1)
    def _():
        grad_w_ref[...] = w_acc[...].astype(LOW)


def hidden_back(chain, meta, x, a, b, back, back_other, cot, merged, total, w, gain):
    streams, rows, width = x.shape
    heads = merged.shape[2] // HD
    outs = [
        shaped(x.shape, WIDE),
        shaped((streams, rows + packed_rows(2 * heads), merged.shape[2])),
        shaped(w.shape),
        shaped((2, width), WIDE),
    ]
    streamed = (x, a, b, back, back_other, cot, merged, total)
    return chain.call(
        hidden_back_kernel,
        (streams,),
        [scalars()] + [per_stream(v.shape) for v in streamed] + [whole(w.shape), whole(gain.shape)],
        [per_stream(o.shape) for o in outs[:2]] + [whole(o.shape) for o in outs[2:]],
        outs,
        scratch=[pltpu.VMEM(w.shape, WIDE), pltpu.VMEM((2 * heads, rows), WIDE)],
        us=6.5,
        vmem=VMEM_WIDE,
    )(meta, *streamed, w, gain)


def attend_back_kernel(own, meta_ref, q_ref, gm_ref, km_ref, vm_ref, ks_ref, vs_ref, *refs):
    if own:
        gq_ref, gkm_ref, gvm_ref, gks_ref, gvs_ref = refs
        before = None
    else:
        before, (gq_ref, gkm_ref, gvm_ref, gks_ref, gvs_ref) = refs[:4], refs[4:]
    streams = pl.num_programs(0)
    stream = pl.program_id(0)
    slots, rows = km_ref.shape[1], q_ref.shape[1]
    heads = q_ref.shape[2] // HD
    stats = get_packed(gm_ref.at[0], rows, 2 * heads, rows)

    def put(ref, index, cols, value):
        if before is not None:
            value = value + before[index][0, :, cols]
        ref[0, :, cols] = value.astype(ref.dtype)

    def body(with_segment):
        memory_ok, segment_ok = slot_masks(own, meta_ref, stream, streams, slots, rows)
        for head in range(heads):
            cols = slice(head * HD, (head + 1) * HD)
            query = q_ref[0, :, cols]
            grad = gm_ref[0, :rows, cols]
            total = stats[head : head + 1, :]
            delta = stats[heads + head : heads + head + 1, :]

            def tier(key, value, ok):
                scores = jnp.where(ok, dot(key, query, NT) * (SCALE * LOG2E), NEG)
                weights = jnp.exp2(scores - total)
                grad_scores = (weights * (dot(value, grad, NT) - delta)).astype(LOW)
                return (
                    dot(key, grad_scores, TN),
                    dot(grad_scores, query) * SCALE,
                    dot(weights.astype(LOW), grad),
                )

            turned, grad_key, grad_value = tier(km_ref[0, :, cols], vm_ref[0, :, cols], memory_ok)
            put(gkm_ref, 0, cols, grad_key)
            put(gvm_ref, 1, cols, grad_value)
            if with_segment:
                more, grad_key, grad_value = tier(
                    ks_ref[0, :, cols], vs_ref[0, :, cols], segment_ok
                )
                turned = turned + more
                put(gks_ref, 2, cols, grad_key)
                put(gvs_ref, 3, cols, grad_value)
            else:
                gks_ref[0, :, cols] = before[2][0, :, cols].astype(gks_ref.dtype)
                gvs_ref[0, :, cols] = before[3][0, :, cols].astype(gvs_ref.dtype)
            gq_ref[0, :, cols] = (turned * SCALE).T.astype(LOW)

    by_tier(own, meta_ref, body)


def attend_back(chain, own, meta, q, gm, km, vm, ks, vs, before=()):
    kind = WIDE if own else LOW
    outs = [shaped(q.shape)] + [shaped(a.shape, kind) for a in (km, vm, ks, vs)]
    return chain.call(
        functools.partial(attend_back_kernel, own),
        (q.shape[0],),
        [scalars()] + [per_stream(a.shape) for a in (q, gm, km, vm, ks, vs, *before)],
        [per_stream(o.shape) for o in outs],
        outs,
        us=10,
        vmem=VMEM_WIDE,
    )(meta, q, gm, km, vm, ks, vs, *before)


def key_value_kernel_back(
    bits, meta_ref, unit_ref, stored_ref, gks_ref, gvs_ref, gkm_ref, gvm_ref,
    wk_ref, wv_ref, gain_ref, bias_ref, column_ref, sent_ref, kept_ref, k_acc, v_acc, sums
):
    stream = pl.program_id(0)
    width, features = wk_ref.shape

    @pl.when(stream == 0)
    def _():
        k_acc[...] = jnp.zeros_like(k_acc)
        v_acc[...] = jnp.zeros_like(v_acc)
        sums[...] = jnp.zeros_like(sums)

    unit, stored = unit_ref[0].T, stored_ref[0].T
    gks, gvs, gkm, gvm = gks_ref[0], gvs_ref[0], gkm_ref[0], gvm_ref[0]
    k_acc[...] += dot(unit, gks) + dot(stored, gkm)
    v_acc[...] += dot(unit, gvs) + dot(stored, gvm)
    for place, pair in enumerate(((gks, gkm), (gvs, gvm))):
        for piece in pair:
            sums[place : place + 1, :] += jnp.sum(piece.astype(WIDE), axis=0, keepdims=True)

    @pl.when(stream == pl.num_programs(0) - 1)
    def _():
        wk, wv = wk_ref[...].astype(WIDE), wv_ref[...].astype(WIDE)
        column_ref[:, 0:1] = jnp.sum(wk * k_acc[...] + wv * v_acc[...], axis=1, keepdims=True)
        column_ref[:, 1:2] = jnp.sum(wk * sums[0:1, :] + wv * sums[1:2, :], axis=1, keepdims=True)
        half = width // 2
        side = pair_side(meta_ref, bits)
        for ref, which in ((sent_ref, 1 - side), (kept_ref, side)):
            rows = pl.ds(pl.multiple_of(which * half, half), half)
            gain, bias = gain_ref[rows, :], bias_ref[rows, :]
            ref[:, :features] = (gain * k_acc[rows, :] + bias * sums[0:1, :]).astype(LOW)
            ref[:, features:] = (gain * v_acc[rows, :] + bias * sums[1:2, :]).astype(LOW)


def key_value_grads(chain, orders, meta, streamed, fixed):
    width, features = fixed[0].shape
    outs = [shaped((width, 2), WIDE)] + [shaped((width // 2, 2 * features))] * 2
    acc = pltpu.VMEM((width, features), WIDE)
    return chain.call(
        functools.partial(key_value_kernel_back, tuple(order[0] for order in orders)),
        (streamed[0].shape[0],),
        [scalars()] + [per_stream(v.shape) for v in streamed] + [whole(v.shape) for v in fixed],
        [whole(o.shape) for o in outs],
        outs,
        scratch=[acc, acc, pltpu.VMEM((2, features), WIDE)],
        vmem=VMEM_WIDE,
        us=10,
    )(meta, *streamed, *fixed)


def query_kernel_back(
    bits, meta_ref, unit_ref, own_ref, came_ref, gks_ref, gvs_ref,
    wq_ref, wk_ref, wv_ref, gwo_ref, gain_ref, bias_ref, column_in, column_ref, normed_ref,
    sent_ref, kept_ref, q_acc, sums
):
    stream = pl.program_id(0)
    width, features = wq_ref.shape

    @pl.when(stream == 0)
    def _():
        q_acc[...] = jnp.zeros_like(q_acc)
        sums[...] = jnp.zeros_like(sums)

    grad = (own_ref[0].astype(WIDE) + came_ref[0].astype(WIDE)).astype(LOW)
    q_acc[...] += dot(unit_ref[0], grad, TN)
    sums[...] += jnp.sum(grad.astype(WIDE), axis=0, keepdims=True)
    normed_ref[0] = (
        dot(grad, wq_ref[...], NT) + dot(gks_ref[0], wk_ref[...], NT) + dot(gvs_ref[0], wv_ref[...], NT)
    ).astype(LOW)

    @pl.when(stream == pl.num_programs(0) - 1)
    def _():
        wq = wq_ref[...].astype(WIDE)
        column_ref[:, 0:1] = column_in[:, 0:1] + jnp.sum(wq * q_acc[...], axis=1, keepdims=True)
        column_ref[:, 1:2] = column_in[:, 1:2] + jnp.sum(wq * sums[...], axis=1, keepdims=True)
        query = (gain_ref[...] * q_acc[...] + bias_ref[...] * sums[...]).astype(LOW)
        half = width // 2

        def put(out_ref, query_ref):
            out_ref[...] = gwo_ref[...]
            query_ref[:, :features] = query[:half]
            query_ref[:, features:] = query[half:]

        side = pair_side(meta_ref, bits)

        @pl.when(side == 0)
        def _():
            put(kept_ref, sent_ref)

        @pl.when(side != 0)
        def _():
            put(sent_ref, kept_ref)


def query_grads(chain, orders, meta, streamed, fixed):
    width, features = fixed[0].shape
    unit = streamed[0]
    outs = [shaped((width, 2), WIDE), shaped(unit.shape)]
    outs += [shaped((width // 2, 2 * features))] * 2
    return chain.call(
        functools.partial(query_kernel_back, tuple(order[0] for order in orders)),
        (unit.shape[0],),
        [scalars()] + [per_stream(v.shape) for v in streamed] + [whole(v.shape) for v in fixed],
        [whole(outs[0].shape), per_stream(unit.shape)] + [whole(o.shape) for o in outs[2:]],
        outs,
        scratch=[pltpu.VMEM((width, features), WIDE), pltpu.VMEM((1, features), WIDE)],
        vmem=VMEM_WIDE,
        us=9,
    )(meta, *streamed, *fixed)


def input_back_kernel(x_ref, own_ref, other_ref, hidden_ref, gain_ref, out_ref):
    normed, inverse = norm_stats(x_ref[0].astype(WIDE))
    grad = own_ref[0].astype(WIDE) + other_ref[0].astype(WIDE)
    out_ref[0] = (hidden_ref[0] + norm_back(grad, normed, inverse, gain_ref[...])).astype(LOW)


def input_back(chain, x, own, other, grad_hidden, gain):
    streamed = (x, own, other, grad_hidden)
    return chain.call(
        input_back_kernel,
        (x.shape[0],),
        [per_stream(v.shape) for v in streamed] + [whole(gain.shape)],
        per_stream(x.shape),
        shaped(x.shape),
        us=4,
    )(*streamed, gain)


def compress_kernel(bits, meta_ref, memory_ref, came_ref, rest_ref, w_ref, cot_ref, out_ref, *refs):
    sent_ref, kept_ref, acc, grads = refs
    stream = pl.program_id(0)
    streams = pl.num_programs(0)
    head = meta_ref[META_HEAD]
    mine = meta_ref[META_TIER] == 0
    slots, part = came_ref.shape[1], came_ref.shape[2]
    count = out_ref.shape[1]
    place = lax.broadcasted_iota(jnp.int32, (count, slots), 0)
    slot = lax.broadcasted_iota(jnp.int32, (count, slots), 1)
    length = meta_ref[META_STREAMS + stream]
    filled = jnp.where(mine, meta_ref[META_STREAMS + streams + stream], slots)
    ok = lax.broadcasted_iota(jnp.int32, (count, 1), 0) < lax.div(length, jnp.int32(RATE))
    cot = jnp.where(ok, cot_ref[0].astype(WIDE), 0.0).astype(LOW)

    @pl.when(stream == 0)
    def _():
        acc[...] = jnp.zeros_like(acc)

    picks = []
    for shift in range(RATE):
        chosen = (slot == place * RATE + shift) & (slot < filled)
        picks.append(jnp.where(chosen, 1.0, 0.0).astype(LOW))
    result = jnp.zeros(out_ref.shape[1:], WIDE)
    for ref, side in ((came_ref, head), (rest_ref, 1 - head)):
        start = pl.multiple_of(side * part, part)
        stored = jnp.where(mine, memory_ref[0, 0, :, pl.ds(start, part)].astype(WIDE), ref[0].astype(WIDE))
        stored = stored.astype(LOW)
        for shift in range(RATE):
            rows = dot(picks[shift], stored).astype(LOW)
            result = result + dot(rows, w_ref[shift, pl.ds(start, part), :])
            acc[shift, pl.ds(start, part), :] += dot(rows, cot, TN)
    out_ref[0] = jnp.where(ok, result, 0.0).astype(LOW)

    @pl.when(stream == streams - 1)
    def _():
        width = w_ref.shape[1]
        for shift in range(RATE):
            grads[shift * width : (shift + 1) * width, :] = acc[shift].astype(LOW)
        half = sent_ref.shape[0]
        side = pair_side(meta_ref, bits)
        for ref, which in ((sent_ref, 1 - side), (kept_ref, side)):
            ref[...] = grads[pl.ds(pl.multiple_of(which * half, half), half), :]


def compress(chain, orders, meta, memories, came, rest, w, cot):
    flat = (w.shape[0] * w.shape[1], w.shape[2])
    outs = [shaped(cot.shape)] + [shaped((flat[0] // 2, flat[1]))] * 2
    bits = tuple(order[0] for order in orders)
    return chain.call(
        functools.partial(compress_kernel, bits),
        (cot.shape[0],),
        [scalars()]
        + [per_stream(v.shape) for v in (memories, came, rest)]
        + [whole(w.shape), per_stream(cot.shape)],
        [per_stream(cot.shape)] + [whole(o.shape) for o in outs[1:]],
        outs,
        scratch=[pltpu.VMEM(w.shape, WIDE), pltpu.VMEM(flat, LOW)],
        us=5,
    )(meta, memories, came, rest, w, cot)


def bits_of():
    size = lax.axis_size("dp")
    bits = [("tier", 1)]
    step = 1
    while step < size:
        bits.append(("dp", step))
        step *= 2
    return bits


def swap(value, bit):
    axis, step = bit
    return lax.ppermute(value, axis, [(i, i ^ step) for i in range(lax.axis_size(axis))])


def swap_head(value):
    return swap(value, ("head", 1))


def swap_tier(value):
    return swap(value, ("tier", 1))


def swap_pair(value, bits):
    axes = ("dp", "tier", "head")
    sizes = [lax.axis_size(axis) for axis in axes]
    pairs = []
    for dp in range(sizes[0]):
        for tier in range(sizes[1]):
            for head in range(sizes[2]):
                axis, step = bits[head]
                to_dp = dp ^ step if axis == "dp" else dp
                to_tier = tier ^ step if axis == "tier" else tier
                pairs.append(
                    (
                        (dp * sizes[1] + tier) * sizes[2] + head,
                        (to_dp * sizes[1] + to_tier) * sizes[2] + head,
                    )
                )
    return lax.ppermute(value, axes, pairs)


def total_of(first, second):
    return (first.astype(WIDE) + second.astype(WIDE)).astype(LOW)


def scatter_kernel(bits, extra, meta_ref, kept, came, *refs):
    if extra:
        own, other, *refs = refs
        refs[-1][...] = own[...] + other[...]
    half = kept.shape[0] // 2
    side = pair_side(meta_ref, bits)
    for ref, which in zip(refs, (1 - side, side)):
        rows = pl.ds(pl.multiple_of(which * half, half), half)
        ref[...] = total_of(kept[rows, :], came[rows, :])


def add_kernel(bits, extra, meta_ref, kept, came, *refs):
    if extra:
        own, other, *refs = refs
        refs[-1][...] = own[...] + other[...]
    refs[0][...] = total_of(kept[...], came[...])


def gather_kernel(bits, extra, meta_ref, held, came, *refs):
    if extra:
        own, other, *refs = refs
        refs[-1][...] = own[...] + other[...]
    half = held.shape[0]
    side = pair_side(meta_ref, bits)
    refs[0][pl.ds(pl.multiple_of(side * half, half), half), :] = held[...]
    refs[0][pl.ds(pl.multiple_of((1 - side) * half, half), half), :] = came[...]


class Reduce:
    def __init__(self, chain, meta, orders, sent, kept, vector=None):
        self.chain, self.meta, self.orders = chain, meta, orders
        self.stages = len(orders[0])
        self.depth = min(3, self.stages - 1)
        self.kept = kept
        self.stage = 0
        self.vector = vector
        self.vector_bits = [("head", 1)] + bits_of()
        self.send(sent, 0)

    def bits(self, level):
        return tuple(order[level] for order in self.orders)

    def send(self, array, level):
        self.came = swap_pair(array, self.bits(level))
        self.vector_came = None
        if self.vector is not None and self.vector_bits:
            self.vector_came = swap(self.vector, self.vector_bits.pop(0))

    def run(self, kernel, level, outs):
        args = [self.meta, self.kept, self.came]
        extra = self.vector_came is not None
        if extra:
            args += [self.vector, self.vector_came]
            outs = outs + [shaped(self.vector.shape, WIDE)]
        result = self.chain.call(
            functools.partial(kernel, self.bits(level), extra),
            (1,),
            [scalars()] + [whole(v.shape) for v in args[1:]],
            [whole(o.shape) for o in outs],
            outs,
            vmem=8,
        )(*args)
        if extra:
            *result, self.vector = result
        return result

    def ready(self):
        return self.stage >= self.stages + self.depth - 1

    def step(self):
        depth, stage, stages = self.depth, self.stage, self.stages
        self.stage += 1
        rows, width = self.kept.shape
        if stage < depth - 1:
            sent, self.kept = self.run(
                scatter_kernel, stage + 1, [shaped((rows // 2, width))] * 2
            )
            self.send(sent, stage + 1)
        elif stage < stages:
            (self.kept,) = self.run(add_kernel, stage, [shaped((rows, width))])
            self.send(self.kept, stage + 1 if stage + 1 < stages else depth - 1)
        else:
            level = depth - 1 - (stage - stages)
            (self.kept,) = self.run(gather_kernel, level, [shaped((2 * rows, width))])
            self.send(self.kept, level - 1)


def finish_kernel(bits, write, carried, meta_ref, held, came, *refs):
    write(pair_side(meta_ref, bits), held, came, refs[carried:])


def finish(group, write, out_shapes, out_specs, carried=()):
    args = [group.meta, group.kept, group.came, *carried]
    count = len(carried)
    return group.chain.call(
        functools.partial(finish_kernel, group.bits(0), write, count),
        (1,),
        [scalars(), whole(group.kept.shape), whole(group.came.shape)] + [any_spec()] * count,
        out_specs,
        out_shapes,
        vmem=24,
        alias={3 + i: i for i in range(count)},
        us=3,
    )(*args)


def write_rows(side, held, came, outs):
    half = held.shape[0]
    for ref, which in ((held, side), (came, 1 - side)):
        outs[0][pl.ds(pl.multiple_of(which * half, half), half), :] = ref[...].astype(WIDE)


def finish_ffn(group, part, out_shape, in_shape, carried=()):
    specs = [
        pl.BlockSpec((out_shape[0] // 2, out_shape[1]), lambda i: (part, 0)),
        pl.BlockSpec((in_shape[0], in_shape[1] // 2), lambda i: (0, part)),
    ]

    def write(side, held, came, outs):
        for out_ref, in_ref, which in ((held, came, 0), (came, held, 1)):

            @pl.when(side == which)
            def _():
                outs[0][...] = out_ref[...].astype(WIDE)
                outs[1][...] = in_ref[...].astype(WIDE)

    return finish(group, write, [shaped(out_shape, WIDE), shaped(in_shape, WIDE)], specs, carried)


def finish_key_value(group, width, features):
    shapes = [shaped((width, features), WIDE)] * 2

    def write(side, held, came, outs):
        half = held.shape[0]
        for ref, which in ((held, side), (came, 1 - side)):
            rows = pl.ds(pl.multiple_of(which * half, half), half)
            outs[0][rows, :] = ref[:, :features].astype(WIDE)
            outs[1][rows, :] = ref[:, features:].astype(WIDE)

    return finish(group, write, shapes, [whole_block(v.shape) for v in shapes])


def finish_out_query(group, width, features):
    shapes = [shaped((features, width), WIDE), shaped((width, features), WIDE)]

    def write(side, held, came, outs):
        def put(out_ref, query_ref):
            half = out_ref.shape[0]
            outs[0][...] = out_ref[...].astype(WIDE)
            outs[1][:half, :] = query_ref[:, :features].astype(WIDE)
            outs[1][half:, :] = query_ref[:, features:].astype(WIDE)

        @pl.when(side == 0)
        def _():
            put(held, came)

        @pl.when(side != 0)
        def _():
            put(came, held)

    return finish(group, write, shapes, [whole_block(v.shape) for v in shapes])


def finish_compress(group, shape):
    flat = (shape[0] * shape[1], shape[2])
    return finish(group, write_rows, [shaped(flat, WIDE)], [whole_block(flat)])[0].reshape(shape)


def on_device(
    inputs,
    memories,
    seg_len,
    mem_count,
    w_query,
    w_key,
    w_value,
    w_attn_out,
    w_ffn_in,
    w_ffn_out,
    w_compress,
    gain_attn,
    bias_attn,
    gain_ffn,
    bias_ffn,
    cotan_output,
    cotan_compressed,
):
    tier_index = lax.axis_index("tier")
    streams, rows, width = inputs.shape
    features = w_query.shape[1]
    hidden_units = w_ffn_in.shape[1]
    counts = mem_count[:, 0]
    place = jnp.stack([tier_index, lax.axis_index("head"), lax.axis_index("dp")])
    meta = jnp.concatenate([place, seg_len, counts], 0).astype(jnp.int32)
    gain_row, bias_row = gain_attn[None], bias_attn[None]
    gain_second, bias_second = gain_ffn[None], bias_ffn[None]
    chain = Chain()

    unit, low, queries = query_rows(chain, meta, inputs, gain_row, bias_row, w_query)
    queries_other = [swap_tier(q) for q in queries]
    keys, values = key_values(chain, low, w_key, w_value)
    stored, memory_keys, memory_values = stored_rows(
        chain, memories, gain_row, bias_row, w_key, w_value
    )
    tiers = (memory_keys, memory_values, keys, values)
    own, came = [], []
    for stream in range(streams):
        came.append(swap_tier(attend(chain, False, stream, meta, queries_other[stream], *tiers)))
        own.append(attend(chain, True, stream, meta, queries[stream], *tiers))
    merged, totals, attended = zip(
        *[merge(chain, rows, mine, other, w_attn_out) for mine, other in zip(own, came)]
    )
    merged, totals, attended = jnp.stack(merged), jnp.stack(totals), jnp.stack(attended)
    attended_other = swap_head(attended)

    tier, low_bit, *more = bits_of()
    high_bit, more = more[0], more[1:]
    axes = {"x": tier, "y": low_bit, "z": high_bit}
    orders = {
        name: tuple(tuple(axes[axis] for axis in path) + tuple(more) for path in paths.split("/"))
        for name, paths in PATHS.items()
    }
    flat = (streams * rows, width)
    hidden_args = (
        inputs.reshape(flat),
        attended.reshape(flat),
        attended_other.reshape(flat),
        cotan_output.reshape(flat),
        gain_second,
        bias_second,
    )
    groups, got = {}, {}

    def begin(name, sent, kept, vector=None):
        groups[name] = Reduce(chain, meta, orders[name], sent, kept, vector)

    def run_ffn():
        names = ("f1", "f2")
        got["act"], back, *parts = ffn(
            chain, streams, [orders[name] for name in names], meta, hidden_args, w_ffn_in, w_ffn_out
        )
        got["back"] = back.reshape(inputs.shape)
        got["back_other"] = swap_head(got["back"])
        for place, name in enumerate(names):
            begin(name, *parts[2 * place : 2 * place + 2])

    def run_ffn3():
        got["ffn"] = ffn_out(chain, got["act"], w_ffn_out).reshape(inputs.shape)
        got["ffn_other"] = swap_head(got["ffn"])

    def run_hidden():
        got["hidden"], got["gm"], got["gwo"], vectors_ffn = hidden_back(
            chain, meta, inputs, attended, attended_other, got["back"], got["back_other"],
            cotan_output, merged, totals, w_attn_out, gain_second,
        )
        got["gm_other"] = swap_tier(got["gm"])
        got["vectors"] = 0.5 * vectors_ffn

    def run_own():
        got["queries"] = jnp.stack(queries)
        got["own"], *got["sums"] = attend_back(chain, True, meta, got["queries"], got["gm"], *tiers)

    def run_other():
        got["other"], *got["grads"] = attend_back(
            chain, False, meta, jnp.stack(queries_other), got["gm_other"], *tiers,
            before=tuple(got["sums"]),
        )
        got["came"] = swap_tier(got["other"])

    def run_output():
        got["output"] = output_rows(
            chain, meta, inputs, attended, attended_other, got["ffn"], got["ffn_other"]
        )

    def run_grads():
        grad_km, grad_vm, grad_ks, grad_vs = got["grads"]
        got["column"], *parts = key_value_grads(
            chain, orders["kv"], meta, (unit, stored, grad_ks, grad_vs, grad_km, grad_vm),
            (w_key, w_value, gain_attn[:, None], bias_attn[:, None]),
        )
        begin("kv", *parts)

    def run_query():
        _, _, grad_ks, grad_vs = got["grads"]
        column, got["normed"], *parts = query_grads(
            chain, orders["oq"], meta, (unit, got["own"], got["came"], grad_ks, grad_vs),
            (
                w_query, w_key, w_value, got["gwo"], gain_attn[:, None], bias_attn[:, None],
                got["column"],
            ),
        )
        got["normed_other"] = swap_head(got["normed"])
        begin("oq", *parts, jnp.concatenate([column.T, got["vectors"]], axis=0))

    def run_evict():
        got["evicted"] = lax.ppermute(evicted_rows(chain, meta, memories), "tier", [(0, 1)])

    def run_evict2():
        got["evicted"] = copied(chain, got["evicted"])
        got["evicted_other"] = swap_head(got["evicted"])

    def run_input():
        got["grad_inputs"] = input_back(
            chain, inputs, got["normed"], got["normed_other"], got["hidden"], gain_row
        )

    def run_compress():
        got["compressed"], *parts = compress(
            chain, orders["compress"], meta, memories, got["evicted"], got["evicted_other"],
            w_compress, cotan_compressed,
        )
        begin("compress", *parts)

    def end(name):
        group = groups.pop(name)
        out_shape, in_shape = w_ffn_out.shape, w_ffn_in.shape
        if name == "f1":
            got["ffn_grads"] = finish_ffn(group, 0, out_shape, in_shape)
        elif name == "f2":
            got["ffn_grads"] = finish_ffn(group, 1, out_shape, in_shape, got["ffn_grads"])
        elif name == "kv":
            got["kv"] = finish_key_value(group, width, features)
        elif name == "oq":
            got["oq"] = finish_out_query(group, width, features)
            got["vector"] = group.vector
        else:
            got["compress"] = finish_compress(group, w_compress.shape)

    runs = {
        "ffn": run_ffn, "ffn3": run_ffn3, "hidden": run_hidden, "own": run_own,
        "other": run_other, "output": run_output, "grads": run_grads, "query": run_query,
        "evict": run_evict, "evict2": run_evict2, "input": run_input, "compr": run_compress,
    }
    for name in ORDER:
        if name in runs:
            runs[name]()
        elif name in groups and groups[name].ready():
            end(name)
        elif name in groups:
            groups[name].step()
    while groups:
        for name in list(groups):
            if groups[name].ready():
                end(name)
            else:
                groups[name].step()
    vectors = got["vector"]
    return (
        got["output"],
        got["compressed"],
        got["grad_inputs"],
        got["oq"][1],
        *got["kv"],
        got["oq"][0],
        got["ffn_grads"][1],
        got["ffn_grads"][0],
        got["compress"],
        vectors[0],
        vectors[1],
        vectors[2],
        vectors[3],
    )


def solution(mesh):
    return jax.shard_map(
        on_device,
        mesh=mesh,
        in_specs=(
            P("dp", "tier", None),
            P("dp", "tier", None, None),
            P("dp"),
            P("dp", "tier"),
            P(None, "head"),
            P(None, "head"),
            P(None, "head"),
            P("head", None),
            P(None, "head"),
            P("head", None),
            P(None, None, ("tier", "head")),
            P(),
            P(),
            P(),
            P(),
            P("dp", "tier", None),
            P("dp", None, ("tier", "head")),
        ),
        out_specs=(
            P("dp", "tier", None),
            P("dp", None, ("tier", "head")),
            P("dp", "tier", None),
            P(None, "head"),
            P(None, "head"),
            P(None, "head"),
            P("head", None),
            P(None, "head"),
            P("head", None),
            P(None, None, ("tier", "head")),
            P(),
            P(),
            P(),
            P(),
        ),
        check_vma=False,
    )
```

```python
import functools

import jax
import jax.numpy as jnp
from jax import lax
from jax.experimental import pallas as pl
from jax.experimental.pallas import tpu as pltpu
from jax.sharding import PartitionSpec as P

HD = 128
RATE = 3
EPS = 1e-05
NEG = -1000000000.0
LOG2E = 1.4426950408889634
SCALE = HD ** (-0.5)
GELU_ROOT = 0.7978845608028654
GELU_CUBE = 0.044715

ORDER = (
    "ffn", "pause", "hidden", "evict2", "own", "ffn3", "f1", "f2", "other", "output", "grads",
    "f1", "f2", "query", "kv", "f1", "f2", "input", "oq", "kv", "f1", "f2", "compr", "oq", "kv",
    "f1", "f2", "compress", "oq", "kv", "f1", "f2", "compress", "oq", "kv", "f1", "f2",
    "compress", "oq", "kv", "compress", "oq", "kv", "compress", "oq",
)

PATHS = {
    "f1": "yxw/zxy",
    "f2": "xwz/yzx",
    "kv": "zxy/xzy",
    "oq": "xyw/yzx",
    "compress": "yz/zy",
}

COST = 1e10
COST_EARLY = 1e8
PAUSE = 10
VMEM_FFN = 32
VMEM_WIDE = 40
EXTRA = 64

LOW = jnp.bfloat16
WIDE = jnp.float32
NN = (((1,), (0,)), ((), ()))
NT = (((1,), (1,)), ((), ()))
TN = (((0,), (0,)), ((), ()))


def dot(first, second, dims=NN):
    return lax.dot_general(first, second, dims, preferred_element_type=WIDE)


def norm_stats(values):
    centre = values - jnp.mean(values, axis=-1, keepdims=True)
    inverse = lax.rsqrt(jnp.mean(centre * centre, axis=-1, keepdims=True) + EPS)
    return (centre * inverse, inverse)


def norm_back(grad_normed, normed, inverse, gain_vector):
    scaled = grad_normed * gain_vector
    return inverse * (
        scaled
        - jnp.mean(scaled, axis=-1, keepdims=True)
        - normed * jnp.mean(scaled * normed, axis=-1, keepdims=True)
    )


def per_stream(array_shape):
    block = (1,) + tuple(array_shape[1:])
    zeros = (0,) * (len(block) - 1)
    return pl.BlockSpec(block, lambda s: (s,) + zeros)


def whole(array_shape):
    return pl.BlockSpec(memory_space=pltpu.VMEM)


def whole_block(array_shape):
    zeros = (0,) * len(array_shape)
    return pl.BlockSpec(tuple(array_shape), lambda *_: zeros)


def scalars():
    return pl.BlockSpec(memory_space=pltpu.SMEM)


def shaped(shape, dtype=LOW):
    return jax.ShapeDtypeStruct(tuple(shape), dtype)


class Chain:
    def __init__(self):
        self.last = None
        self.cost = COST_EARLY

    def call(self, kernel, grid, in_specs, out_specs, out_shape, scratch=(), vmem=16, alias=None, us=1.0):
        last = self.last
        count = len(in_specs)

        def ordered(*refs):
            kernel(*refs[:count], *refs[count + 1 :])

        def run(*args):
            specs = list(in_specs)
            args = list(args)
            body = kernel
            if last is not None:
                specs.append(pl.BlockSpec(memory_space=pl.ANY))
                args.append(last)
                body = ordered
            outs = pl.pallas_call(
                body,
                grid=grid,
                in_specs=specs,
                out_specs=out_specs,
                out_shape=out_shape,
                scratch_shapes=list(scratch),
                input_output_aliases=alias or {},
                compiler_params=pltpu.CompilerParams(vmem_limit_bytes=vmem * 1024 * 1024),
                cost_estimate=pl.CostEstimate(
                    flops=int(us * self.cost), bytes_accessed=0, transcendentals=0
                ),
            )(*args)
            if not alias:
                self.last = outs[0] if isinstance(outs, (list, tuple)) else outs
            return outs

        return run


META_TIER, META_HEAD, META_DP, META_STREAMS = 0, 1, 2, 3


def any_spec():
    return pl.BlockSpec(memory_space=pl.ANY)


def query_kernel(meta_ref, x_ref, gain_ref, bias_ref, w_ref, unit_ref, low_ref, *outs):
    for stream in range(x_ref.shape[0]):
        normed, _ = norm_stats(x_ref[stream].astype(WIDE))
        unit_ref[stream] = normed.astype(LOW)
        low = (normed * gain_ref[...] + bias_ref[...]).astype(LOW)
        low_ref[stream] = low
        outs[stream][...] = dot(low, w_ref[...]).astype(LOW)


def query_rows(chain, meta, x, gain, bias, w):
    streams, rows, width = x.shape
    outs = [shaped(x.shape), shaped(x.shape)]
    outs += [shaped((rows, w.shape[1]))] * streams
    unit, low, *queries = chain.call(
        query_kernel,
        (1,),
        [scalars()] + [whole(v.shape) for v in (x, gain, bias, w)],
        [whole(o.shape) for o in outs],
        outs,
        us=3,
    )(meta, x, gain, bias, w)
    return unit, low, queries


def key_value_kernel(low_ref, wk_ref, wv_ref, k_ref, v_ref):
    k_ref[0] = dot(low_ref[0], wk_ref[...]).astype(LOW)
    v_ref[0] = dot(low_ref[0], wv_ref[...]).astype(LOW)


def key_values(chain, low, wk, wv):
    outs = [shaped(low.shape[:2] + wk.shape[1:])] * 2
    return chain.call(
        key_value_kernel,
        (low.shape[0],),
        [per_stream(low.shape), whole(wk.shape), whole(wv.shape)],
        [per_stream(o.shape) for o in outs],
        outs,
        us=2.5,
    )(low, wk, wv)


def stored_kernel(x_ref, gain_ref, bias_ref, wk_ref, wv_ref, unit_ref, k_ref, v_ref):
    normed, _ = norm_stats(x_ref[0, 0].astype(WIDE))
    unit_ref[0] = normed.astype(LOW)
    low = (normed * gain_ref[...] + bias_ref[...]).astype(LOW)
    k_ref[0] = dot(low, wk_ref[...]).astype(LOW)
    v_ref[0] = dot(low, wv_ref[...]).astype(LOW)


def stored_rows(chain, x, gain, bias, wk, wv):
    streams, _, slots, width = x.shape
    outs = [shaped((streams, slots, width))] + [shaped((streams, slots, wk.shape[1]))] * 2
    return chain.call(
        stored_kernel,
        (streams,),
        [per_stream(x.shape)] + [whole(v.shape) for v in (gain, bias, wk, wv)],
        [per_stream(o.shape) for o in outs],
        outs,
        us=6,
    )(x, gain, bias, wk, wv)


def slot_masks(own, meta_ref, stream, streams, slots, rows):
    tier = meta_ref[META_TIER]
    length = meta_ref[META_STREAMS + stream]
    filled = meta_ref[META_STREAMS + streams + stream]
    memory_ok = lax.broadcasted_iota(jnp.int32, (slots, rows), 0) < filled
    key_row = lax.broadcasted_iota(jnp.int32, (rows, rows), 0)
    segment_ok = (tier * rows + key_row) < length
    if own:
        query_row = lax.broadcasted_iota(jnp.int32, (rows, rows), 1)
        segment_ok = segment_ok & (key_row <= query_row)
    return memory_ok, segment_ok


def by_tier(own, meta_ref, body):
    if own:
        body(True)
        return

    @pl.when(meta_ref[META_TIER] == 0)
    def _():
        body(True)

    @pl.when(meta_ref[META_TIER] != 0)
    def _():
        body(False)


def put_packed(ref, row, value):
    count, width = value.shape
    for part in range(3):
        low = value.astype(LOW)
        ref[row + part * count : row + (part + 1) * count, :width] = low
        value = value - low.astype(WIDE)


def get_packed(ref, row, count, width):
    parts = [
        ref[row + part * count : row + (part + 1) * count, :width].astype(WIDE) for part in range(3)
    ]
    return parts[0] + (parts[1] + parts[2])


def packed_rows(count):
    return -(-3 * count // 16) * 16


def attend_kernel(own, stream, streams, meta_ref, q_ref, km_ref, vm_ref, ks_ref, vs_ref, out_ref, totals):
    slots, rows = km_ref.shape[1], q_ref.shape[0]
    heads = q_ref.shape[1] // HD

    def body(with_segment):
        memory_ok, segment_ok = slot_masks(own, meta_ref, stream, streams, slots, rows)
        for head in range(heads):
            cols = slice(head * HD, (head + 1) * HD)
            query = q_ref[:, cols]
            scores = jnp.where(
                memory_ok, dot(km_ref[0, :, cols], query, NT) * (SCALE * LOG2E), NEG
            )
            top = jnp.max(scores, axis=0, keepdims=True)
            if with_segment:
                near = jnp.where(
                    segment_ok, dot(ks_ref[0, :, cols], query, NT) * (SCALE * LOG2E), NEG
                )
                top = jnp.maximum(top, jnp.max(near, axis=0, keepdims=True))
            raw = jnp.exp2(scores - top)
            spent = jnp.sum(raw, axis=0, keepdims=True)
            mixed = dot(vm_ref[0, :, cols], raw.astype(LOW), TN)
            if with_segment:
                raw_near = jnp.exp2(near - top)
                spent = spent + jnp.sum(raw_near, axis=0, keepdims=True)
                mixed = mixed + dot(vs_ref[0, :, cols], raw_near.astype(LOW), TN)
            out_ref[:rows, cols] = (mixed / spent).T.astype(LOW)
            totals[head : head + 1, :] = top + jnp.log2(spent)
        put_packed(out_ref, rows, totals[...])

    by_tier(own, meta_ref, body)


def one_stream(array, stream):
    return pl.BlockSpec((1,) + array.shape[1:], lambda i: (stream, 0, 0))


def attend(chain, own, stream, meta, q, km, vm, ks, vs):
    rows, features = q.shape
    heads = features // HD
    out = shaped((rows + packed_rows(heads), features))
    return chain.call(
        functools.partial(attend_kernel, own, stream, km.shape[0]),
        (1,),
        [scalars(), whole(q.shape)] + [one_stream(a, stream) for a in (km, vm, ks, vs)],
        whole(out.shape),
        out,
        scratch=[pltpu.VMEM((heads, rows), WIDE)],
        us=2.6,
    )(meta, q, km, vm, ks, vs)


def merge_kernel(w_ref, own_ref, other_ref, low_ref, total_ref, part_ref):
    rows, features = low_ref.shape
    heads = features // HD
    first = get_packed(own_ref, rows, heads, rows)
    second = get_packed(other_ref, rows, heads, rows)
    top = jnp.maximum(first, second)
    total = top + jnp.log2(jnp.exp2(first - top) + jnp.exp2(second - top))
    total_ref[...] = total
    share_own, share_other = jnp.exp2(first - total), jnp.exp2(second - total)
    for head in range(heads):
        cols = slice(head * HD, (head + 1) * HD)
        column_own = jnp.broadcast_to(share_own[head : head + 1], (HD, rows)).T
        column_other = jnp.broadcast_to(share_other[head : head + 1], (HD, rows)).T
        merged = (
            own_ref[:rows, cols].astype(WIDE) * column_own
            + other_ref[:rows, cols].astype(WIDE) * column_other
        )
        low_ref[:, cols] = merged.astype(LOW)
    part_ref[...] = dot(low_ref[...], w_ref[...]).astype(LOW)


def merge(chain, rows, own, other, w):
    features = own.shape[1]
    outs = [
        shaped((rows, features)),
        shaped((features // HD, rows), WIDE),
        shaped((rows, w.shape[1])),
    ]
    args = (w, own, other)
    return chain.call(
        merge_kernel,
        (1,),
        [whole(v.shape) for v in args],
        [whole(o.shape) for o in outs],
        outs,
        us=1.0,
    )(*args)


def evicted_kernel(streams, meta_ref, memory_ref, evicted_ref):
    part = evicted_ref.shape[2]
    start = pl.multiple_of(meta_ref[META_HEAD] * part, part)
    filled = meta_ref[META_STREAMS + streams + pl.program_id(0)]
    ok = lax.broadcasted_iota(jnp.int32, (evicted_ref.shape[1], 1), 0) < filled
    rows = memory_ref[0, 0, :, pl.ds(start, part)].astype(WIDE)
    evicted_ref[0] = jnp.where(ok, rows, 0.0).astype(LOW)


def evicted_rows(chain, meta, memories):
    streams, _, slots, width = memories.shape
    out = (streams, slots, width // 2)
    return chain.call(
        functools.partial(evicted_kernel, streams),
        (streams,),
        [scalars(), per_stream(memories.shape)],
        per_stream(out),
        shaped(out),
        us=2,
    )(meta, memories)


def pause_kernel(out_ref):
    out_ref[...] = jnp.zeros_like(out_ref)


def pause(chain):
    shape = shaped((8, HD), WIDE)
    return chain.call(pause_kernel, (1,), [], whole(shape.shape), shape, us=PAUSE)()


def copied_kernel(in_ref, out_ref):
    out_ref[...] = in_ref[...]


def copied(chain, array):
    return chain.call(
        copied_kernel, (1,), [whole(array.shape)], whole(array.shape), shaped(array.shape)
    )(array)


def pick(stream, refs, scratch):
    for place, ref in enumerate(refs):

        @pl.when(stream == place)
        def _():
            scratch[...] = ref[...]


def valid_rows(meta_ref, streams, rows):
    place = lax.broadcasted_iota(jnp.int32, (streams * rows, 1), 0)
    ok = None
    for stream in range(streams):
        inside = (
            (place >= stream * rows)
            & (place < stream * rows + meta_ref[META_STREAMS + stream] - meta_ref[META_TIER] * rows)
            & (place < (stream + 1) * rows)
        )
        ok = inside if ok is None else ok | inside
    return ok


def side_of(meta_ref, bit):
    axis, step = bit
    if axis == "tier":
        return meta_ref[META_TIER]
    return lax.rem(lax.div(meta_ref[META_DP], jnp.int32(step)), jnp.int32(2))


def pair_side(meta_ref, bits):
    first, second = (side_of(meta_ref, bit) for bit in bits)
    return jnp.where(meta_ref[META_HEAD] == 0, first, second)


def ffn_kernel(streams, bits, meta_ref, *refs):
    x_ref, cot_ref, gain_ref, bias_ref = refs[:4]
    a_refs, b_refs = refs[4 : 4 + streams], refs[4 + streams : 4 + 2 * streams]
    wi_ref, wo_ref, act_ref, back_ref, *refs = refs[4 + 2 * streams :]
    parts, (low_ref, turned_ref, grad_ref, back_acc) = refs[:-4], refs[-4:]
    step = pl.program_id(0)
    units = wi_ref.shape[1]

    @pl.when(step == 0)
    def _():
        rows = x_ref.shape[0] // streams
        for stream in range(streams):
            own = slice(stream * rows, (stream + 1) * rows)
            attended = a_refs[stream][...].astype(WIDE) + b_refs[stream][...].astype(WIDE)
            normed, _ = norm_stats(x_ref[own, :].astype(WIDE) + attended)
            low = (normed * gain_ref[...] + bias_ref[...]).astype(LOW)
            low_ref[own, :] = low
            turned_ref[:, own] = low.T
        ok = valid_rows(meta_ref, streams, x_ref.shape[0] // streams)
        grad_ref[...] = jnp.where(ok, cot_ref[...].astype(WIDE), 0.0).astype(LOW)

    lifted = dot(low_ref[...], wi_ref[...])
    square = lifted * lifted
    bent = jnp.tanh(GELU_ROOT * lifted * (1.0 + GELU_CUBE * square))
    half = 0.5 * (1.0 + bent)
    activated = (lifted * half).astype(LOW)
    act_ref[...] = activated
    slope = half + 0.5 * lifted * (1.0 - bent * bent) * (
        GELU_ROOT * (1.0 + 3.0 * GELU_CUBE * square)
    )
    grad_out = dot(activated, grad_ref[...], TN).astype(LOW)
    grad_lifted = (slope * dot(grad_ref[...], wo_ref[...], NT)).astype(LOW)
    grad_in = dot(turned_ref[...], grad_lifted).astype(LOW)
    place = pl.multiple_of((step % 2) * units, units)
    for part in range(2):
        sent, kept = parts[2 * part : 2 * part + 2]
        side = pair_side(meta_ref, bits[part])
        for out_ref, in_ref, which in ((kept, sent, 0), (sent, kept, 1)):

            @pl.when((step // 2 == part) & (side == which))
            def _():
                out_ref[pl.ds(place, units), :] = grad_out
                in_ref[:, pl.ds(place, units)] = grad_in

    more = dot(grad_lifted, wi_ref[...], NT)

    @pl.when(step == 0)
    def _():
        back_acc[...] = more

    @pl.when(step != 0)
    def _():
        back_acc[...] += more

    @pl.when(step == pl.num_programs(0) - 1)
    def _():
        back_ref[...] = back_acc[...].astype(LOW)


def ffn(chain, streams, orders, meta, whole_args, w_in, w_out):
    rows, width = whole_args[0].shape
    units = w_in.shape[1]
    steps = 4
    block = units // steps
    outs = [shaped((rows, units)), shaped((rows, width))]
    parts = [shaped((units // 2, width))] * 4
    turned = pltpu.VMEM((width, rows), LOW)
    return chain.call(
        functools.partial(ffn_kernel, streams, tuple((p[0][0], p[1][0]) for p in orders)),
        (steps,),
        [scalars()]
        + [whole(v.shape) for v in whole_args]
        + [
            pl.BlockSpec((width, block), lambda j: (0, j)),
            pl.BlockSpec((block, width), lambda j: (j, 0)),
        ],
        [pl.BlockSpec((rows, block), lambda j: (0, j)), whole((rows, width))]
        + [whole(o.shape) for o in parts],
        outs + parts,
        scratch=[
            pltpu.VMEM((rows, width), LOW),
            turned,
            pltpu.VMEM((rows, width), LOW),
            pltpu.VMEM((rows, width), WIDE),
        ],
        vmem=VMEM_FFN,
        us=24,
    )(meta, *whole_args, w_in, w_out)


def ffn_out_kernel(act_ref, w_ref, out_ref, acc):
    step = pl.program_id(0)
    more = dot(act_ref[...], w_ref[...])

    @pl.when(step == 0)
    def _():
        acc[...] = more

    @pl.when(step != 0)
    def _():
        acc[...] += more

    @pl.when(step == pl.num_programs(0) - 1)
    def _():
        out_ref[...] = acc[...].astype(LOW)


def ffn_out(chain, act, w):
    rows, units = act.shape
    width = w.shape[1]
    steps = 4
    block = units // steps
    return chain.call(
        ffn_out_kernel,
        (steps,),
        [pl.BlockSpec((rows, block), lambda j: (0, j)), pl.BlockSpec((block, width), lambda j: (j, 0))],
        whole((rows, width)),
        shaped((rows, width)),
        scratch=[pltpu.VMEM((rows, width), WIDE)],
        us=4,
    )(act, w)


def output_kernel(streams, meta_ref, x_ref, own_ref, other_ref, *refs):
    a_refs, b_refs, out_ref = refs[:streams], refs[streams : 2 * streams], refs[2 * streams]
    rows = x_ref.shape[1]
    place = meta_ref[META_TIER] * rows + lax.broadcasted_iota(jnp.int32, (rows, 1), 0)
    for stream in range(streams):
        ok = place < meta_ref[META_STREAMS + stream]
        attended = a_refs[stream][...].astype(WIDE) + b_refs[stream][...].astype(WIDE)
        hidden = x_ref[stream].astype(WIDE) + attended
        result = hidden + (own_ref[stream].astype(WIDE) + other_ref[stream].astype(WIDE))
        out_ref[stream] = jnp.where(ok, result, 0.0).astype(LOW)


def output_rows(chain, meta, x, own, other, a, b):
    args = (x, own, other, *a, *b)
    return chain.call(
        functools.partial(output_kernel, x.shape[0]),
        (1,),
        [scalars()] + [whole(v.shape) for v in args],
        whole(x.shape),
        shaped(x.shape),
        us=3,
    )(meta, *args)


def hidden_back_kernel(
    streams,
    meta_ref,
    x_ref,
    back_ref,
    back_other_ref,
    cot_ref,
    w_ref,
    gain_ref,
    *refs,
):
    lists, refs = refs[: 4 * streams], refs[4 * streams :]
    grad_hidden_ref, grad_merged_ref, grad_w_ref, vector_ref, w_acc, stats = refs[:6]
    stream = pl.program_id(0)
    rows = x_ref.shape[1]
    for place, scratch in enumerate(refs[6:]):
        pick(stream, lists[place * streams : (place + 1) * streams], scratch)
    a_ref, b_ref, merged_ref, total_ref = refs[6:]
    hidden = x_ref[0].astype(WIDE) + (a_ref[...].astype(WIDE) + b_ref[...].astype(WIDE))
    normed, inverse = norm_stats(hidden)
    place = meta_ref[META_TIER] * rows + lax.broadcasted_iota(jnp.int32, (rows, 1), 0)
    ok = place < meta_ref[META_STREAMS + stream]
    back = back_ref[0].astype(WIDE) + back_other_ref[0].astype(WIDE)
    grad_out = jnp.where(ok, cot_ref[0].astype(WIDE), 0.0)
    grad_hidden = grad_out + norm_back(back, normed, inverse, gain_ref[...])
    grad_hidden_ref[0] = grad_hidden
    low = grad_hidden.astype(LOW)
    merged = merged_ref[...]
    grad_merged = dot(low, w_ref[...], NT).astype(LOW)
    grad_merged_ref[0, :rows, :] = grad_merged
    heads = merged.shape[1] // HD
    stats[:heads, :] = total_ref[...]
    product = grad_merged.astype(WIDE) * merged.astype(WIDE)
    for head in range(heads):
        turned = product[:, head * HD : (head + 1) * HD].T
        stats[heads + head : heads + head + 1, :] = jnp.sum(turned, axis=0, keepdims=True)
    put_packed(grad_merged_ref.at[0], rows, stats[...])
    grad_w = dot(merged, low, TN)
    gain_part = jnp.sum(back * normed, axis=0, keepdims=True)
    bias_part = jnp.sum(back, axis=0, keepdims=True)

    @pl.when(stream == 0)
    def _():
        w_acc[...] = grad_w
        vector_ref[0:1, :] = gain_part
        vector_ref[1:2, :] = bias_part

    @pl.when(stream != 0)
    def _():
        w_acc[...] += grad_w
        vector_ref[0:1, :] += gain_part
        vector_ref[1:2, :] += bias_part

    @pl.when(stream == pl.num_programs(0) - 1)
    def _():
        grad_w_ref[...] = w_acc[...].astype(LOW)


def hidden_back(chain, meta, x, a, b, back, back_other, cot, merged, total, w, gain):
    streams, rows, width = x.shape
    features = w.shape[0]
    heads = features // HD
    outs = [
        shaped(x.shape, WIDE),
        shaped((streams, rows + packed_rows(2 * heads), features)),
        shaped(w.shape),
        shaped((2, width), WIDE),
    ]
    streamed = (x, back, back_other, cot)
    lists = (*a, *b, *merged, *total)
    return chain.call(
        functools.partial(hidden_back_kernel, streams),
        (streams,),
        [scalars()]
        + [per_stream(v.shape) for v in streamed]
        + [whole(v.shape) for v in (w, gain, *lists)],
        [per_stream(o.shape) for o in outs[:2]] + [whole(o.shape) for o in outs[2:]],
        outs,
        scratch=[
            pltpu.VMEM(w.shape, WIDE),
            pltpu.VMEM((2 * heads, rows), WIDE),
            pltpu.VMEM((rows, width), LOW),
            pltpu.VMEM((rows, width), LOW),
            pltpu.VMEM((rows, features), LOW),
            pltpu.VMEM((heads, rows), WIDE),
        ],
        us=6.5,
        vmem=VMEM_WIDE,
    )(meta, *streamed, w, gain, *lists)


def attend_back_kernel(own, streams, meta_ref, gm_ref, km_ref, vm_ref, ks_ref, vs_ref, *refs):
    *refs, q_ref = refs
    pick(pl.program_id(0), refs[: streams], q_ref)
    refs = refs[streams :]
    if own:
        gq_ref, gkm_ref, gvm_ref, gks_ref, gvs_ref = refs
        before = None
    else:
        before, (gq_ref, gkm_ref, gvm_ref, gks_ref, gvs_ref) = refs[:4], refs[4:]
    stream = pl.program_id(0)
    slots, rows = km_ref.shape[1], q_ref.shape[0]
    heads = q_ref.shape[1] // HD
    stats = get_packed(gm_ref.at[0], rows, 2 * heads, rows)

    def put(ref, index, cols, value):
        if before is not None:
            value = value + before[index][0, :, cols]
        ref[0, :, cols] = value.astype(ref.dtype)

    def body(with_segment):
        memory_ok, segment_ok = slot_masks(own, meta_ref, stream, streams, slots, rows)
        for head in range(heads):
            cols = slice(head * HD, (head + 1) * HD)
            query = q_ref[:, cols]
            grad = gm_ref[0, :rows, cols]
            total = stats[head : head + 1, :]
            delta = stats[heads + head : heads + head + 1, :]

            def tier(key, value, ok):
                scores = jnp.where(ok, dot(key, query, NT) * (SCALE * LOG2E), NEG)
                weights = jnp.exp2(scores - total)
                grad_scores = (weights * (dot(value, grad, NT) - delta)).astype(LOW)
                return (
                    dot(key, grad_scores, TN),
                    dot(grad_scores, query) * SCALE,
                    dot(weights.astype(LOW), grad),
                )

            turned, grad_key, grad_value = tier(km_ref[0, :, cols], vm_ref[0, :, cols], memory_ok)
            put(gkm_ref, 0, cols, grad_key)
            put(gvm_ref, 1, cols, grad_value)
            if with_segment:
                more, grad_key, grad_value = tier(
                    ks_ref[0, :, cols], vs_ref[0, :, cols], segment_ok
                )
                turned = turned + more
                put(gks_ref, 2, cols, grad_key)
                put(gvs_ref, 3, cols, grad_value)
            else:
                gks_ref[0, :, cols] = before[2][0, :, cols].astype(gks_ref.dtype)
                gvs_ref[0, :, cols] = before[3][0, :, cols].astype(gvs_ref.dtype)
            gq_ref[0, :, cols] = (turned * SCALE).T.astype(LOW)

    by_tier(own, meta_ref, body)


def attend_back(chain, own, meta, queries, gm, km, vm, ks, vs, before=()):
    streams = len(queries)
    rows, features = queries[0].shape
    kind = WIDE if own else LOW
    outs = [shaped((streams, rows, features))] + [shaped(a.shape, kind) for a in (km, vm, ks, vs)]
    return chain.call(
        functools.partial(attend_back_kernel, own, streams),
        (streams,),
        [scalars()]
        + [per_stream(a.shape) for a in (gm, km, vm, ks, vs)]
        + [whole(q.shape) for q in queries]
        + [per_stream(a.shape) for a in before],
        [per_stream(o.shape) for o in outs],
        outs,
        scratch=[pltpu.VMEM((rows, features), LOW)],
        us=10,
        vmem=VMEM_WIDE,
    )(meta, gm, km, vm, ks, vs, *queries, *before)


def row_of(column):
    return jnp.broadcast_to(column, (column.shape[0], HD)).T[0:1, :]


def key_value_kernel_back(
    bits, meta_ref, unit_ref, stored_ref, gks_ref, gvs_ref, gkm_ref, gvm_ref,
    wk_ref, wv_ref, gain_ref, bias_ref, column_ref, sent_ref, kept_ref, k_acc, v_acc, sums
):
    stream = pl.program_id(0)
    width, features = wk_ref.shape

    @pl.when(stream == 0)
    def _():
        k_acc[...] = jnp.zeros_like(k_acc)
        v_acc[...] = jnp.zeros_like(v_acc)
        sums[...] = jnp.zeros_like(sums)

    unit, stored = unit_ref[0].T, stored_ref[0].T
    gks, gvs, gkm, gvm = gks_ref[0], gvs_ref[0], gkm_ref[0], gvm_ref[0]
    k_acc[...] += dot(unit, gks) + dot(stored, gkm)
    v_acc[...] += dot(unit, gvs) + dot(stored, gvm)
    for place, pair in enumerate(((gks, gkm), (gvs, gvm))):
        for piece in pair:
            sums[place : place + 1, :] += jnp.sum(piece.astype(WIDE), axis=0, keepdims=True)

    @pl.when(stream == pl.num_programs(0) - 1)
    def _():
        wk, wv = wk_ref[...].astype(WIDE), wv_ref[...].astype(WIDE)
        column_ref[0:1, :] = row_of(jnp.sum(wk * k_acc[...] + wv * v_acc[...], axis=1, keepdims=True))
        column_ref[1:2, :] = row_of(
            jnp.sum(wk * sums[0:1, :] + wv * sums[1:2, :], axis=1, keepdims=True)
        )
        half = width // 2
        side = pair_side(meta_ref, bits)
        for ref, which in ((sent_ref, 1 - side), (kept_ref, side)):
            rows = pl.ds(pl.multiple_of(which * half, half), half)
            gain, bias = gain_ref[rows, :], bias_ref[rows, :]
            ref[:, :features] = (gain * k_acc[rows, :] + bias * sums[0:1, :]).astype(LOW)
            ref[:, features:] = (gain * v_acc[rows, :] + bias * sums[1:2, :]).astype(LOW)


def key_value_grads(chain, orders, meta, streamed, fixed):
    width, features = fixed[0].shape
    outs = [shaped((2, width), WIDE)] + [shaped((width // 2, 2 * features))] * 2
    acc = pltpu.VMEM((width, features), WIDE)
    return chain.call(
        functools.partial(key_value_kernel_back, tuple(order[0] for order in orders)),
        (streamed[0].shape[0],),
        [scalars()] + [per_stream(v.shape) for v in streamed] + [whole(v.shape) for v in fixed],
        [whole(o.shape) for o in outs],
        outs,
        scratch=[acc, acc, pltpu.VMEM((2, features), WIDE)],
        vmem=VMEM_WIDE,
        us=10,
    )(meta, *streamed, *fixed)


def query_kernel_back(
    bits, meta_ref, unit_ref, own_ref, came_ref, gks_ref, gvs_ref,
    wq_ref, wk_ref, wv_ref, gwo_ref, gain_ref, bias_ref, column_ref, vector_ref, normed_ref,
    sent_ref, kept_ref, q_acc, sums
):
    stream = pl.program_id(0)
    width, features = wq_ref.shape

    @pl.when(stream == 0)
    def _():
        q_acc[...] = jnp.zeros_like(q_acc)
        sums[...] = jnp.zeros_like(sums)

    grad = (own_ref[0].astype(WIDE) + came_ref[0].astype(WIDE)).astype(LOW)
    q_acc[...] += dot(unit_ref[0], grad, TN)
    sums[...] += jnp.sum(grad.astype(WIDE), axis=0, keepdims=True)
    normed_ref[0] = (
        dot(grad, wq_ref[...], NT) + dot(gks_ref[0], wk_ref[...], NT) + dot(gvs_ref[0], wv_ref[...], NT)
    ).astype(LOW)

    @pl.when(stream == pl.num_programs(0) - 1)
    def _():
        wq = wq_ref[...].astype(WIDE)
        gain_part = row_of(jnp.sum(wq * q_acc[...], axis=1, keepdims=True))
        bias_part = row_of(jnp.sum(wq * sums[...], axis=1, keepdims=True))
        query = (gain_ref[...] * q_acc[...] + bias_ref[...] * sums[...]).astype(LOW)
        half = width // 2
        extra = sent_ref.shape[0] - half

        def put(out_ref, query_ref):
            out_ref[:half, :] = gwo_ref[...]
            out_ref[half:, :] = jnp.zeros((extra, width), LOW)
            out_ref[half : half + 1, :] = (column_ref[0:1, :] + gain_part).astype(LOW)
            out_ref[half + 1 : half + 2, :] = (column_ref[1:2, :] + bias_part).astype(LOW)
            out_ref[half + 2 : half + 4, :] = (0.5 * vector_ref[...]).astype(LOW)
            query_ref[:half, :features] = query[:half]
            query_ref[:half, features:] = query[half:]
            query_ref[half:, :] = jnp.zeros((extra, width), LOW)

        side = pair_side(meta_ref, bits)

        @pl.when(side == 0)
        def _():
            put(kept_ref, sent_ref)

        @pl.when(side != 0)
        def _():
            put(sent_ref, kept_ref)


def query_grads(chain, orders, meta, streamed, fixed):
    width, features = fixed[0].shape
    unit = streamed[0]
    outs = [shaped(unit.shape)]
    outs += [shaped((width // 2 + EXTRA, 2 * features))] * 2
    return chain.call(
        functools.partial(query_kernel_back, tuple(order[0] for order in orders)),
        (unit.shape[0],),
        [scalars()] + [per_stream(v.shape) for v in streamed] + [whole(v.shape) for v in fixed],
        [per_stream(unit.shape)] + [whole(o.shape) for o in outs[1:]],
        outs,
        scratch=[pltpu.VMEM((width, features), WIDE), pltpu.VMEM((1, features), WIDE)],
        vmem=VMEM_WIDE,
        us=9,
    )(meta, *streamed, *fixed)


def input_back_kernel(x_ref, own_ref, other_ref, hidden_ref, gain_ref, out_ref):
    normed, inverse = norm_stats(x_ref[0].astype(WIDE))
    grad = own_ref[0].astype(WIDE) + other_ref[0].astype(WIDE)
    out_ref[0] = (hidden_ref[0] + norm_back(grad, normed, inverse, gain_ref[...])).astype(LOW)


def input_back(chain, x, own, other, grad_hidden, gain):
    streamed = (x, own, other, grad_hidden)
    return chain.call(
        input_back_kernel,
        (x.shape[0],),
        [per_stream(v.shape) for v in streamed] + [whole(gain.shape)],
        per_stream(x.shape),
        shaped(x.shape),
        us=4,
    )(*streamed, gain)


def compress_kernel(bits, meta_ref, memory_ref, came_ref, rest_ref, w_ref, cot_ref, out_ref, *refs):
    sent_ref, kept_ref, acc, grads = refs
    stream = pl.program_id(0)
    streams = pl.num_programs(0)
    head = meta_ref[META_HEAD]
    mine = meta_ref[META_TIER] == 0
    slots, part = came_ref.shape[1], came_ref.shape[2]
    count = out_ref.shape[1]
    place = lax.broadcasted_iota(jnp.int32, (count, slots), 0)
    slot = lax.broadcasted_iota(jnp.int32, (count, slots), 1)
    length = meta_ref[META_STREAMS + stream]
    filled = jnp.where(mine, meta_ref[META_STREAMS + streams + stream], slots)
    ok = lax.broadcasted_iota(jnp.int32, (count, 1), 0) < lax.div(length, jnp.int32(RATE))
    cot = jnp.where(ok, cot_ref[0].astype(WIDE), 0.0).astype(LOW)

    @pl.when(stream == 0)
    def _():
        acc[...] = jnp.zeros_like(acc)

    picks = []
    for shift in range(RATE):
        chosen = (slot == place * RATE + shift) & (slot < filled)
        picks.append(jnp.where(chosen, 1.0, 0.0).astype(LOW))
    result = jnp.zeros(out_ref.shape[1:], WIDE)
    for ref, side in ((came_ref, head), (rest_ref, 1 - head)):
        start = pl.multiple_of(side * part, part)
        stored = jnp.where(mine, memory_ref[0, 0, :, pl.ds(start, part)].astype(WIDE), ref[0].astype(WIDE))
        stored = stored.astype(LOW)
        for shift in range(RATE):
            rows = dot(picks[shift], stored).astype(LOW)
            result = result + dot(rows, w_ref[shift, pl.ds(start, part), :])
            acc[shift, pl.ds(start, part), :] += dot(rows, cot, TN)
    out_ref[0] = jnp.where(ok, result, 0.0).astype(LOW)

    @pl.when(stream == streams - 1)
    def _():
        width = w_ref.shape[1]
        for shift in range(RATE):
            grads[shift * width : (shift + 1) * width, :] = acc[shift].astype(LOW)
        half = sent_ref.shape[0]
        side = pair_side(meta_ref, bits)
        for ref, which in ((sent_ref, 1 - side), (kept_ref, side)):
            ref[...] = grads[pl.ds(pl.multiple_of(which * half, half), half), :]


def compress(chain, orders, meta, memories, came, rest, w, cot):
    flat = (w.shape[0] * w.shape[1], w.shape[2])
    outs = [shaped(cot.shape)] + [shaped((flat[0] // 2, flat[1]))] * 2
    bits = tuple(order[0] for order in orders)
    return chain.call(
        functools.partial(compress_kernel, bits),
        (cot.shape[0],),
        [scalars()]
        + [per_stream(v.shape) for v in (memories, came, rest)]
        + [whole(w.shape), per_stream(cot.shape)],
        [per_stream(cot.shape)] + [whole(o.shape) for o in outs[1:]],
        outs,
        scratch=[pltpu.VMEM(w.shape, WIDE), pltpu.VMEM(flat, LOW)],
        us=5,
    )(meta, memories, came, rest, w, cot)


def bits_of():
    size = lax.axis_size("dp")
    bits = [("tier", 1)]
    step = 1
    while step < size:
        bits.append(("dp", step))
        step *= 2
    return bits


def swap(value, bit):
    axis, step = bit
    return lax.ppermute(value, axis, [(i, i ^ step) for i in range(lax.axis_size(axis))])


def swap_head(value):
    return swap(value, ("head", 1))


def swap_tier(value):
    return swap(value, ("tier", 1))


def swap_pair(value, bits):
    axes = ("dp", "tier", "head")
    sizes = [lax.axis_size(axis) for axis in axes]
    pairs = []
    for dp in range(sizes[0]):
        for tier in range(sizes[1]):
            for head in range(sizes[2]):
                axis, step = bits[head]
                to_dp = dp ^ step if axis == "dp" else dp
                to_tier = tier ^ step if axis == "tier" else tier
                pairs.append(
                    (
                        (dp * sizes[1] + tier) * sizes[2] + head,
                        (to_dp * sizes[1] + to_tier) * sizes[2] + head,
                    )
                )
    return lax.ppermute(value, axes, pairs)


def total_of(first, second):
    return (first.astype(WIDE) + second.astype(WIDE)).astype(LOW)


def scatter_kernel(bits, meta_ref, kept, came, *refs):
    half = kept.shape[0] // 2
    side = pair_side(meta_ref, bits)
    for ref, which in zip(refs, (1 - side, side)):
        rows = pl.ds(pl.multiple_of(which * half, half), half)
        ref[...] = total_of(kept[rows, :], came[rows, :])


def add_kernel(bits, meta_ref, kept, came, *refs):
    refs[0][...] = total_of(kept[...], came[...])


def gather_kernel(bits, meta_ref, held, came, *refs):
    half = held.shape[0]
    side = pair_side(meta_ref, bits)
    refs[0][pl.ds(pl.multiple_of(side * half, half), half), :] = held[...]
    refs[0][pl.ds(pl.multiple_of((1 - side) * half, half), half), :] = came[...]


class Reduce:
    def __init__(self, chain, meta, orders, sent, kept):
        self.chain, self.meta, self.orders = chain, meta, orders
        self.stages = len(orders[0])
        self.depth = min(3, self.stages - 1)
        self.kept = kept
        self.stage = 0
        self.send(sent, 0)

    def bits(self, level):
        return tuple(order[level] for order in self.orders)

    def send(self, array, level):
        self.came = swap_pair(array, self.bits(level))

    def run(self, kernel, level, outs):
        return self.chain.call(
            functools.partial(kernel, self.bits(level)),
            (1,),
            [scalars(), whole(self.kept.shape), whole(self.came.shape)],
            [whole(o.shape) for o in outs],
            outs,
            vmem=8,
        )(self.meta, self.kept, self.came)

    def ready(self):
        return self.stage >= self.stages + self.depth - 1

    def step(self):
        depth, stage, stages = self.depth, self.stage, self.stages
        self.stage += 1
        rows, width = self.kept.shape
        if stage < depth - 1:
            sent, self.kept = self.run(
                scatter_kernel, stage + 1, [shaped((rows // 2, width))] * 2
            )
            self.send(sent, stage + 1)
        elif stage < stages:
            (self.kept,) = self.run(add_kernel, stage, [shaped((rows, width))])
            self.send(self.kept, stage + 1 if stage + 1 < stages else depth - 1)
        else:
            level = depth - 1 - (stage - stages)
            (self.kept,) = self.run(gather_kernel, level, [shaped((2 * rows, width))])
            self.send(self.kept, level - 1)


def finish_kernel(bits, write, carried, meta_ref, held, came, *refs):
    write(pair_side(meta_ref, bits), held, came, refs[carried:])


def finish(group, write, out_shapes, out_specs, carried=()):
    args = [group.meta, group.kept, group.came, *carried]
    count = len(carried)
    return group.chain.call(
        functools.partial(finish_kernel, group.bits(0), write, count),
        (1,),
        [scalars(), whole(group.kept.shape), whole(group.came.shape)] + [any_spec()] * count,
        out_specs,
        out_shapes,
        vmem=24,
        alias={3 + i: i for i in range(count)},
        us=3,
    )(*args)


def write_rows(side, held, came, outs):
    half = held.shape[0]
    for ref, which in ((held, side), (came, 1 - side)):
        outs[0][pl.ds(pl.multiple_of(which * half, half), half), :] = ref[...].astype(WIDE)


def finish_ffn(group, part, out_shape, in_shape, carried=()):
    specs = [
        pl.BlockSpec((out_shape[0] // 2, out_shape[1]), lambda i: (part, 0)),
        pl.BlockSpec((in_shape[0], in_shape[1] // 2), lambda i: (0, part)),
    ]

    def write(side, held, came, outs):
        for out_ref, in_ref, which in ((held, came, 0), (came, held, 1)):

            @pl.when(side == which)
            def _():
                outs[0][...] = out_ref[...].astype(WIDE)
                outs[1][...] = in_ref[...].astype(WIDE)

    return finish(group, write, [shaped(out_shape, WIDE), shaped(in_shape, WIDE)], specs, carried)


def finish_key_value(group, width, features):
    shapes = [shaped((width, features), WIDE)] * 2

    def write(side, held, came, outs):
        half = held.shape[0]
        for ref, which in ((held, side), (came, 1 - side)):
            rows = pl.ds(pl.multiple_of(which * half, half), half)
            outs[0][rows, :] = ref[:, :features].astype(WIDE)
            outs[1][rows, :] = ref[:, features:].astype(WIDE)

    return finish(group, write, shapes, [whole_block(v.shape) for v in shapes])


def finish_out_query(group, width, features):
    shapes = [shaped((features, width), WIDE), shaped((width, features), WIDE), shaped((16, width))]

    def write(side, held, came, outs):
        def put(out_ref, query_ref):
            half = outs[0].shape[0]
            outs[0][...] = out_ref[:half, :].astype(WIDE)
            outs[1][:half, :] = query_ref[:half, :features].astype(WIDE)
            outs[1][half:, :] = query_ref[:half, features:].astype(WIDE)
            outs[2][...] = out_ref[half : half + 16, :]

        @pl.when(side == 0)
        def _():
            put(held, came)

        @pl.when(side != 0)
        def _():
            put(came, held)

    return finish(
        group, write, shapes, [whole_block(v.shape) for v in shapes[:2]] + [whole(shapes[2].shape)]
    )


def finish_compress(group, shape):
    flat = (shape[0] * shape[1], shape[2])
    return finish(group, write_rows, [shaped(flat, WIDE)], [whole_block(flat)])[0].reshape(shape)


def on_device(
    inputs,
    memories,
    seg_len,
    mem_count,
    w_query,
    w_key,
    w_value,
    w_attn_out,
    w_ffn_in,
    w_ffn_out,
    w_compress,
    gain_attn,
    bias_attn,
    gain_ffn,
    bias_ffn,
    cotan_output,
    cotan_compressed,
):
    tier_index = lax.axis_index("tier")
    streams, rows, width = inputs.shape
    features = w_query.shape[1]
    hidden_units = w_ffn_in.shape[1]
    counts = mem_count[:, 0]
    place = jnp.stack([tier_index, lax.axis_index("head"), lax.axis_index("dp")])
    meta = jnp.concatenate([place, seg_len, counts], 0).astype(jnp.int32)
    gain_row, bias_row = gain_attn[None], bias_attn[None]
    gain_second, bias_second = gain_ffn[None], bias_ffn[None]
    chain = Chain()

    unit, low, queries = query_rows(chain, meta, inputs, gain_row, bias_row, w_query)
    queries_other = [swap_tier(q) for q in queries]
    keys, values = key_values(chain, low, w_key, w_value)
    stored, memory_keys, memory_values = stored_rows(
        chain, memories, gain_row, bias_row, w_key, w_value
    )
    tiers = (memory_keys, memory_values, keys, values)
    own, came = [], []
    for stream in range(streams):
        came.append(swap_tier(attend(chain, False, stream, meta, queries_other[stream], *tiers)))
        own.append(attend(chain, True, stream, meta, queries[stream], *tiers))
    got = {}
    merged, totals, attended, attended_other = [], [], [], []
    for stream in range(streams):
        low, total, part = merge(chain, rows, own[stream], came[stream], w_attn_out)
        merged.append(low)
        totals.append(total)
        attended.append(part)
        attended_other.append(swap_head(part))
    got["evicted"] = lax.ppermute(evicted_rows(chain, meta, memories), "tier", [(0, 1)])

    tier, low_bit, *more = bits_of()
    high_bit, far_bit, more = more[0], more[1], more[2:]
    axes = {"x": tier, "y": low_bit, "z": high_bit, "w": far_bit}
    orders = {}
    for name, paths in PATHS.items():
        rest = "yzw" if name == "compress" else "xyzw"
        orders[name] = tuple(
            tuple(axes[axis] for axis in dict.fromkeys(path + rest)) + tuple(more)
            for path in paths.split("/")
        )
    flat = (streams * rows, width)
    hidden_args = (
        inputs.reshape(flat),
        cotan_output.reshape(flat),
        gain_second,
        bias_second,
        *attended,
        *attended_other,
    )
    groups = {}

    def begin(name, sent, kept):
        groups[name] = Reduce(chain, meta, orders[name], sent, kept)

    def run_ffn():
        names = ("f1", "f2")
        got["act"], back, *parts = ffn(
            chain, streams, [orders[name] for name in names], meta, hidden_args, w_ffn_in, w_ffn_out
        )
        got["back"] = back.reshape(inputs.shape)
        got["back_other"] = swap_head(got["back"])
        for place, name in enumerate(names):
            begin(name, *parts[2 * place : 2 * place + 2])

    def run_ffn3():
        got["ffn"] = ffn_out(chain, got["act"], w_ffn_out).reshape(inputs.shape)
        got["ffn_other"] = swap_head(got["ffn"])

    def run_hidden():
        got["hidden"], got["gm"], got["gwo"], vectors_ffn = hidden_back(
            chain, meta, inputs, attended, attended_other, got["back"], got["back_other"],
            cotan_output, merged, totals, w_attn_out, gain_second,
        )
        got["gm_other"] = swap_tier(got["gm"])
        got["vectors"] = vectors_ffn

    def run_own():
        got["own"], *got["sums"] = attend_back(chain, True, meta, queries, got["gm"], *tiers)

    def run_other():
        got["other"], *got["grads"] = attend_back(
            chain, False, meta, queries_other, got["gm_other"], *tiers,
            before=tuple(got["sums"]),
        )
        got["came"] = swap_tier(got["other"])

    def run_output():
        got["output"] = output_rows(
            chain, meta, inputs, got["ffn"], got["ffn_other"], attended, attended_other
        )

    def run_grads():
        grad_km, grad_vm, grad_ks, grad_vs = got["grads"]
        got["column"], *parts = key_value_grads(
            chain, orders["kv"], meta, (unit, stored, grad_ks, grad_vs, grad_km, grad_vm),
            (w_key, w_value, gain_attn[:, None], bias_attn[:, None]),
        )
        begin("kv", *parts)

    def run_query():
        _, _, grad_ks, grad_vs = got["grads"]
        got["normed"], *parts = query_grads(
            chain, orders["oq"], meta, (unit, got["own"], got["came"], grad_ks, grad_vs),
            (
                w_query, w_key, w_value, got["gwo"], gain_attn[:, None], bias_attn[:, None],
                got["column"], got["vectors"],
            ),
        )
        got["normed_other"] = swap_head(got["normed"])
        begin("oq", *parts)

    def run_evict2():
        got["evicted"] = copied(chain, got["evicted"])
        got["evicted_other"] = swap_head(got["evicted"])

    def run_input():
        got["grad_inputs"] = input_back(
            chain, inputs, got["normed"], got["normed_other"], got["hidden"], gain_row
        )

    def run_compress():
        got["compressed"], *parts = compress(
            chain, orders["compress"], meta, memories, got["evicted"], got["evicted_other"],
            w_compress, cotan_compressed,
        )
        begin("compress", *parts)

    def end(name):
        group = groups.pop(name)
        out_shape, in_shape = w_ffn_out.shape, w_ffn_in.shape
        if name == "f1":
            got["ffn_grads"] = finish_ffn(group, 0, out_shape, in_shape)
        elif name == "f2":
            got["ffn_grads"] = finish_ffn(group, 1, out_shape, in_shape, got["ffn_grads"])
        elif name == "kv":
            got["kv"] = finish_key_value(group, width, features)
        elif name == "oq":
            got["oq"] = finish_out_query(group, width, features)
            got["vector"] = got["oq"][2]
        else:
            got["compress"] = finish_compress(group, w_compress.shape)

    runs = {
        "ffn": run_ffn, "ffn3": run_ffn3, "hidden": run_hidden, "own": run_own,
        "other": run_other, "output": run_output, "grads": run_grads, "query": run_query,
        "evict2": run_evict2, "input": run_input, "compr": run_compress, "pause": lambda: pause(chain),
    }
    chain.cost = COST
    for name in ORDER:
        if name in runs:
            runs[name]()
        elif name in groups and groups[name].ready():
            end(name)
        elif name in groups:
            groups[name].step()
    while groups:
        for name in list(groups):
            if groups[name].ready():
                end(name)
            else:
                groups[name].step()
    vectors = got["vector"].astype(WIDE) + swap_head(got["vector"]).astype(WIDE)
    return (
        got["output"],
        got["compressed"],
        got["grad_inputs"],
        got["oq"][1],
        *got["kv"],
        got["oq"][0],
        got["ffn_grads"][1],
        got["ffn_grads"][0],
        got["compress"],
        vectors[0],
        vectors[1],
        vectors[2],
        vectors[3],
    )


def solution(mesh):
    return jax.shard_map(
        on_device,
        mesh=mesh,
        in_specs=(
            P("dp", "tier", None),
            P("dp", "tier", None, None),
            P("dp"),
            P("dp", "tier"),
            P(None, "head"),
            P(None, "head"),
            P(None, "head"),
            P("head", None),
            P(None, "head"),
            P("head", None),
            P(None, None, ("tier", "head")),
            P(),
            P(),
            P(),
            P(),
            P("dp", "tier", None),
            P("dp", None, ("tier", "head")),
        ),
        out_specs=(
            P("dp", "tier", None),
            P("dp", None, ("tier", "head")),
            P("dp", "tier", None),
            P(None, "head"),
            P(None, "head"),
            P(None, "head"),
            P("head", None),
            P(None, "head"),
            P("head", None),
            P(None, None, ("tier", "head")),
            P(),
            P(),
            P(),
            P(),
        ),
        check_vma=False,
    )
```

```python
import functools

import jax
import jax.numpy as jnp
from jax import lax
from jax.experimental import pallas as pl
from jax.experimental.pallas import tpu as pltpu
from jax.sharding import PartitionSpec as P

HD = 128
RATE = 3
EPS = 1e-05
NEG = -1000000000.0
LOG2E = 1.4426950408889634
SCALE = HD ** (-0.5)
GELU_ROOT = 0.7978845608028654
GELU_CUBE = 0.044715

ORDER = (
    "ffn", "pause", "hidden", "evict2", "own", "evict3", "ffn3", "f1", "f2", "other", "output",
    "grads", "f1", "f2", "query", "f1", "f2", "kv", "input", "oq", "f1", "f2", "kv", "compr",
    "oq", "f1", "f2", "kv", "compress", "oq", "f1", "f2", "kv", "compress", "oq", "kv",
    "compress", "oq", "f1", "f2", "kv", "compress", "oq", "kv", "oq",
)

PATHS = {
    "f1": "yxw/zxy",
    "f2": "xwz/yzx",
    "kv": "zxy/xzy",
    "oq": "xyw/yzx",
    "compress": "yz/zy",
}

COST = 1e10
COST_EARLY = 1e8
PAUSE = 10
VMEM_FFN = 32
VMEM_WIDE = 40
EXTRA = 64

LOW = jnp.bfloat16
WIDE = jnp.float32
NN = (((1,), (0,)), ((), ()))
NT = (((1,), (1,)), ((), ()))
TN = (((0,), (0,)), ((), ()))


def dot(first, second, dims=NN):
    return lax.dot_general(first, second, dims, preferred_element_type=WIDE)


def norm_stats(values):
    centre = values - jnp.mean(values, axis=-1, keepdims=True)
    inverse = lax.rsqrt(jnp.mean(centre * centre, axis=-1, keepdims=True) + EPS)
    return (centre * inverse, inverse)


def norm_back(grad_normed, normed, inverse, gain_vector):
    scaled = grad_normed * gain_vector
    return inverse * (
        scaled
        - jnp.mean(scaled, axis=-1, keepdims=True)
        - normed * jnp.mean(scaled * normed, axis=-1, keepdims=True)
    )


def per_stream(array_shape):
    block = (1,) + tuple(array_shape[1:])
    zeros = (0,) * (len(block) - 1)
    return pl.BlockSpec(block, lambda s: (s,) + zeros)


def whole(array_shape):
    return pl.BlockSpec(memory_space=pltpu.VMEM)


def whole_block(array_shape):
    zeros = (0,) * len(array_shape)
    return pl.BlockSpec(tuple(array_shape), lambda *_: zeros)


def scalars():
    return pl.BlockSpec(memory_space=pltpu.SMEM)


def shaped(shape, dtype=LOW):
    return jax.ShapeDtypeStruct(tuple(shape), dtype)


class Chain:
    def __init__(self):
        self.last = None
        self.cost = COST_EARLY

    def call(self, kernel, grid, in_specs, out_specs, out_shape, scratch=(), vmem=16, alias=None, us=1.0):
        last = self.last
        count = len(in_specs)

        def ordered(*refs):
            kernel(*refs[:count], *refs[count + 1 :])

        def run(*args):
            specs = list(in_specs)
            args = list(args)
            body = kernel
            if last is not None:
                specs.append(pl.BlockSpec(memory_space=pl.ANY))
                args.append(last)
                body = ordered
            outs = pl.pallas_call(
                body,
                grid=grid,
                in_specs=specs,
                out_specs=out_specs,
                out_shape=out_shape,
                scratch_shapes=list(scratch),
                input_output_aliases=alias or {},
                compiler_params=pltpu.CompilerParams(vmem_limit_bytes=vmem * 1024 * 1024),
                cost_estimate=pl.CostEstimate(
                    flops=int(us * self.cost), bytes_accessed=0, transcendentals=0
                ),
            )(*args)
            if not alias:
                self.last = outs[0] if isinstance(outs, (list, tuple)) else outs
            return outs

        return run


META_TIER, META_HEAD, META_DP, META_STREAMS = 0, 1, 2, 3


def any_spec():
    return pl.BlockSpec(memory_space=pl.ANY)


def query_kernel(meta_ref, x_ref, gain_ref, bias_ref, w_ref, unit_ref, low_ref, *outs):
    for stream in range(x_ref.shape[0]):
        normed, _ = norm_stats(x_ref[stream].astype(WIDE))
        unit_ref[stream] = normed.astype(LOW)
        low = (normed * gain_ref[...] + bias_ref[...]).astype(LOW)
        low_ref[stream] = low
        outs[stream][...] = dot(low, w_ref[...]).astype(LOW)


def query_rows(chain, meta, x, gain, bias, w):
    streams, rows, width = x.shape
    outs = [shaped(x.shape), shaped(x.shape)]
    outs += [shaped((rows, w.shape[1]))] * streams
    unit, low, *queries = chain.call(
        query_kernel,
        (1,),
        [scalars()] + [whole(v.shape) for v in (x, gain, bias, w)],
        [whole(o.shape) for o in outs],
        outs,
        us=3,
    )(meta, x, gain, bias, w)
    return unit, low, queries


def key_value_kernel(low_ref, wk_ref, wv_ref, k_ref, v_ref):
    k_ref[0] = dot(low_ref[0], wk_ref[...]).astype(LOW)
    v_ref[0] = dot(low_ref[0], wv_ref[...]).astype(LOW)


def key_values(chain, low, wk, wv):
    outs = [shaped(low.shape[:2] + wk.shape[1:])] * 2
    return chain.call(
        key_value_kernel,
        (low.shape[0],),
        [per_stream(low.shape), whole(wk.shape), whole(wv.shape)],
        [per_stream(o.shape) for o in outs],
        outs,
        us=2.5,
    )(low, wk, wv)


def stored_kernel(x_ref, gain_ref, bias_ref, wk_ref, wv_ref, unit_ref, k_ref, v_ref):
    normed, _ = norm_stats(x_ref[0, 0].astype(WIDE))
    unit_ref[0] = normed.astype(LOW)
    low = (normed * gain_ref[...] + bias_ref[...]).astype(LOW)
    k_ref[0] = dot(low, wk_ref[...]).astype(LOW)
    v_ref[0] = dot(low, wv_ref[...]).astype(LOW)


def stored_rows(chain, x, gain, bias, wk, wv):
    streams, _, slots, width = x.shape
    outs = [shaped((streams, slots, width))] + [shaped((streams, slots, wk.shape[1]))] * 2
    return chain.call(
        stored_kernel,
        (streams,),
        [per_stream(x.shape)] + [whole(v.shape) for v in (gain, bias, wk, wv)],
        [per_stream(o.shape) for o in outs],
        outs,
        us=6,
    )(x, gain, bias, wk, wv)


def slot_masks(own, meta_ref, stream, streams, slots, rows):
    tier = meta_ref[META_TIER]
    length = meta_ref[META_STREAMS + stream]
    filled = meta_ref[META_STREAMS + streams + stream]
    memory_ok = lax.broadcasted_iota(jnp.int32, (slots, rows), 0) < filled
    key_row = lax.broadcasted_iota(jnp.int32, (rows, rows), 0)
    segment_ok = (tier * rows + key_row) < length
    if own:
        query_row = lax.broadcasted_iota(jnp.int32, (rows, rows), 1)
        segment_ok = segment_ok & (key_row <= query_row)
    return memory_ok, segment_ok


def by_tier(own, meta_ref, body):
    if own:
        body(True)
        return

    @pl.when(meta_ref[META_TIER] == 0)
    def _():
        body(True)

    @pl.when(meta_ref[META_TIER] != 0)
    def _():
        body(False)


def put_packed(ref, row, value):
    count, width = value.shape
    for part in range(3):
        low = value.astype(LOW)
        ref[row + part * count : row + (part + 1) * count, :width] = low
        value = value - low.astype(WIDE)


def get_packed(ref, row, count, width):
    parts = [
        ref[row + part * count : row + (part + 1) * count, :width].astype(WIDE) for part in range(3)
    ]
    return parts[0] + (parts[1] + parts[2])


def packed_rows(count):
    return -(-3 * count // 16) * 16


def attend_kernel(own, stream, streams, meta_ref, q_ref, km_ref, vm_ref, ks_ref, vs_ref, out_ref, totals):
    slots, rows = km_ref.shape[1], q_ref.shape[0]
    heads = q_ref.shape[1] // HD

    def body(with_segment):
        memory_ok, segment_ok = slot_masks(own, meta_ref, stream, streams, slots, rows)
        for head in range(heads):
            cols = slice(head * HD, (head + 1) * HD)
            query = q_ref[:, cols]
            scores = jnp.where(
                memory_ok, dot(km_ref[0, :, cols], query, NT) * (SCALE * LOG2E), NEG
            )
            top = jnp.max(scores, axis=0, keepdims=True)
            if with_segment:
                near = jnp.where(
                    segment_ok, dot(ks_ref[0, :, cols], query, NT) * (SCALE * LOG2E), NEG
                )
                top = jnp.maximum(top, jnp.max(near, axis=0, keepdims=True))
            raw = jnp.exp2(scores - top)
            spent = jnp.sum(raw, axis=0, keepdims=True)
            mixed = dot(vm_ref[0, :, cols], raw.astype(LOW), TN)
            if with_segment:
                raw_near = jnp.exp2(near - top)
                spent = spent + jnp.sum(raw_near, axis=0, keepdims=True)
                mixed = mixed + dot(vs_ref[0, :, cols], raw_near.astype(LOW), TN)
            out_ref[:rows, cols] = (mixed / spent).T.astype(LOW)
            totals[head : head + 1, :] = top + jnp.log2(spent)
        put_packed(out_ref, rows, totals[...])

    by_tier(own, meta_ref, body)


def one_stream(array, stream):
    return pl.BlockSpec((1,) + array.shape[1:], lambda i: (stream, 0, 0))


def attend(chain, own, stream, meta, q, km, vm, ks, vs):
    rows, features = q.shape
    heads = features // HD
    out = shaped((rows + packed_rows(heads), features))
    return chain.call(
        functools.partial(attend_kernel, own, stream, km.shape[0]),
        (1,),
        [scalars(), whole(q.shape)] + [one_stream(a, stream) for a in (km, vm, ks, vs)],
        whole(out.shape),
        out,
        scratch=[pltpu.VMEM((heads, rows), WIDE)],
        us=2.6,
    )(meta, q, km, vm, ks, vs)


def merge_kernel(w_ref, own_ref, other_ref, low_ref, total_ref, part_ref):
    rows, features = low_ref.shape
    heads = features // HD
    first = get_packed(own_ref, rows, heads, rows)
    second = get_packed(other_ref, rows, heads, rows)
    top = jnp.maximum(first, second)
    total = top + jnp.log2(jnp.exp2(first - top) + jnp.exp2(second - top))
    total_ref[...] = total
    share_own, share_other = jnp.exp2(first - total), jnp.exp2(second - total)
    for head in range(heads):
        cols = slice(head * HD, (head + 1) * HD)
        column_own = jnp.broadcast_to(share_own[head : head + 1], (HD, rows)).T
        column_other = jnp.broadcast_to(share_other[head : head + 1], (HD, rows)).T
        merged = (
            own_ref[:rows, cols].astype(WIDE) * column_own
            + other_ref[:rows, cols].astype(WIDE) * column_other
        )
        low_ref[:, cols] = merged.astype(LOW)
    part_ref[...] = dot(low_ref[...], w_ref[...]).astype(LOW)


def merge(chain, rows, own, other, w):
    features = own.shape[1]
    outs = [
        shaped((rows, features)),
        shaped((features // HD, rows), WIDE),
        shaped((rows, w.shape[1])),
    ]
    args = (w, own, other)
    return chain.call(
        merge_kernel,
        (1,),
        [whole(v.shape) for v in args],
        [whole(o.shape) for o in outs],
        outs,
        us=1.0,
    )(*args)


def evicted_kernel(streams, meta_ref, memory_ref, evicted_ref):
    part = evicted_ref.shape[2]
    start = pl.multiple_of(meta_ref[META_HEAD] * part, part)
    filled = meta_ref[META_STREAMS + streams + pl.program_id(0)]
    ok = lax.broadcasted_iota(jnp.int32, (evicted_ref.shape[1], 1), 0) < filled
    rows = memory_ref[0, 0, :, pl.ds(start, part)].astype(WIDE)
    evicted_ref[0] = jnp.where(ok, rows, 0.0).astype(LOW)


def evicted_rows(chain, meta, memories):
    streams, _, slots, width = memories.shape
    out = (streams, slots, width // 2)
    return chain.call(
        functools.partial(evicted_kernel, streams),
        (streams,),
        [scalars(), per_stream(memories.shape)],
        per_stream(out),
        shaped(out),
        us=2,
    )(meta, memories)


def pause_kernel(out_ref):
    out_ref[...] = jnp.zeros_like(out_ref)


def pause(chain):
    shape = shaped((8, HD), WIDE)
    return chain.call(pause_kernel, (1,), [], whole(shape.shape), shape, us=PAUSE)()


def copied_kernel(in_ref, out_ref):
    out_ref[...] = in_ref[...]


def copied(chain, array):
    return chain.call(
        copied_kernel, (1,), [whole(array.shape)], whole(array.shape), shaped(array.shape)
    )(array)


def pick(stream, refs, scratch):
    for place, ref in enumerate(refs):

        @pl.when(stream == place)
        def _():
            scratch[...] = ref[...]


def valid_rows(meta_ref, streams, rows):
    place = lax.broadcasted_iota(jnp.int32, (streams * rows, 1), 0)
    ok = None
    for stream in range(streams):
        inside = (
            (place >= stream * rows)
            & (place < stream * rows + meta_ref[META_STREAMS + stream] - meta_ref[META_TIER] * rows)
            & (place < (stream + 1) * rows)
        )
        ok = inside if ok is None else ok | inside
    return ok


def side_of(meta_ref, bit):
    axis, step = bit
    if axis == "tier":
        return meta_ref[META_TIER]
    return lax.rem(lax.div(meta_ref[META_DP], jnp.int32(step)), jnp.int32(2))


def pair_side(meta_ref, bits):
    first, second = (side_of(meta_ref, bit) for bit in bits)
    return jnp.where(meta_ref[META_HEAD] == 0, first, second)


def ffn_kernel(streams, bits, meta_ref, *refs):
    x_ref, cot_ref, gain_ref, bias_ref = refs[:4]
    a_refs, b_refs = refs[4 : 4 + streams], refs[4 + streams : 4 + 2 * streams]
    wi_ref, wo_ref, act_ref, back_ref, *refs = refs[4 + 2 * streams :]
    parts, (low_ref, turned_ref, grad_ref, back_acc) = refs[:-4], refs[-4:]
    step = pl.program_id(0)
    units = wi_ref.shape[1]

    @pl.when(step == 0)
    def _():
        rows = x_ref.shape[0] // streams
        for stream in range(streams):
            own = slice(stream * rows, (stream + 1) * rows)
            attended = a_refs[stream][...].astype(WIDE) + b_refs[stream][...].astype(WIDE)
            normed, _ = norm_stats(x_ref[own, :].astype(WIDE) + attended)
            low = (normed * gain_ref[...] + bias_ref[...]).astype(LOW)
            low_ref[own, :] = low
            turned_ref[:, own] = low.T
        ok = valid_rows(meta_ref, streams, x_ref.shape[0] // streams)
        grad_ref[...] = jnp.where(ok, cot_ref[...].astype(WIDE), 0.0).astype(LOW)

    lifted = dot(low_ref[...], wi_ref[...])
    square = lifted * lifted
    bent = jnp.tanh(GELU_ROOT * lifted * (1.0 + GELU_CUBE * square))
    half = 0.5 * (1.0 + bent)
    activated = (lifted * half).astype(LOW)
    act_ref[...] = activated
    slope = half + 0.5 * lifted * (1.0 - bent * bent) * (
        GELU_ROOT * (1.0 + 3.0 * GELU_CUBE * square)
    )
    grad_out = dot(activated, grad_ref[...], TN).astype(LOW)
    grad_lifted = (slope * dot(grad_ref[...], wo_ref[...], NT)).astype(LOW)
    grad_in = dot(turned_ref[...], grad_lifted).astype(LOW)
    place = pl.multiple_of((step % 2) * units, units)
    for part in range(2):
        sent, kept = parts[2 * part : 2 * part + 2]
        side = pair_side(meta_ref, bits[part])
        for out_ref, in_ref, which in ((kept, sent, 0), (sent, kept, 1)):

            @pl.when((step // 2 == part) & (side == which))
            def _():
                out_ref[pl.ds(place, units), :] = grad_out
                in_ref[:, pl.ds(place, units)] = grad_in

    more = dot(grad_lifted, wi_ref[...], NT)

    @pl.when(step == 0)
    def _():
        back_acc[...] = more

    @pl.when(step != 0)
    def _():
        back_acc[...] += more

    @pl.when(step == pl.num_programs(0) - 1)
    def _():
        back_ref[...] = back_acc[...].astype(LOW)


def ffn(chain, streams, orders, meta, whole_args, w_in, w_out):
    rows, width = whole_args[0].shape
    units = w_in.shape[1]
    steps = 4
    block = units // steps
    outs = [shaped((rows, units)), shaped((rows, width))]
    parts = [shaped((units // 2, width))] * 4
    turned = pltpu.VMEM((width, rows), LOW)
    return chain.call(
        functools.partial(ffn_kernel, streams, tuple((p[0][0], p[1][0]) for p in orders)),
        (steps,),
        [scalars()]
        + [whole(v.shape) for v in whole_args]
        + [
            pl.BlockSpec((width, block), lambda j: (0, j)),
            pl.BlockSpec((block, width), lambda j: (j, 0)),
        ],
        [pl.BlockSpec((rows, block), lambda j: (0, j)), whole((rows, width))]
        + [whole(o.shape) for o in parts],
        outs + parts,
        scratch=[
            pltpu.VMEM((rows, width), LOW),
            turned,
            pltpu.VMEM((rows, width), LOW),
            pltpu.VMEM((rows, width), WIDE),
        ],
        vmem=VMEM_FFN,
        us=24,
    )(meta, *whole_args, w_in, w_out)


def ffn_out_kernel(act_ref, w_ref, out_ref, acc):
    step = pl.program_id(0)
    more = dot(act_ref[...], w_ref[...])

    @pl.when(step == 0)
    def _():
        acc[...] = more

    @pl.when(step != 0)
    def _():
        acc[...] += more

    @pl.when(step == pl.num_programs(0) - 1)
    def _():
        out_ref[...] = acc[...].astype(LOW)


def ffn_out(chain, act, w):
    rows, units = act.shape
    width = w.shape[1]
    steps = 4
    block = units // steps
    return chain.call(
        ffn_out_kernel,
        (steps,),
        [pl.BlockSpec((rows, block), lambda j: (0, j)), pl.BlockSpec((block, width), lambda j: (j, 0))],
        whole((rows, width)),
        shaped((rows, width)),
        scratch=[pltpu.VMEM((rows, width), WIDE)],
        us=4,
    )(act, w)


def output_kernel(streams, meta_ref, x_ref, own_ref, other_ref, *refs):
    a_refs, b_refs, out_ref = refs[:streams], refs[streams : 2 * streams], refs[2 * streams]
    rows = x_ref.shape[1]
    place = meta_ref[META_TIER] * rows + lax.broadcasted_iota(jnp.int32, (rows, 1), 0)
    for stream in range(streams):
        ok = place < meta_ref[META_STREAMS + stream]
        attended = a_refs[stream][...].astype(WIDE) + b_refs[stream][...].astype(WIDE)
        hidden = x_ref[stream].astype(WIDE) + attended
        result = hidden + (own_ref[stream].astype(WIDE) + other_ref[stream].astype(WIDE))
        out_ref[stream] = jnp.where(ok, result, 0.0).astype(LOW)


def output_rows(chain, meta, x, own, other, a, b):
    args = (x, own, other, *a, *b)
    return chain.call(
        functools.partial(output_kernel, x.shape[0]),
        (1,),
        [scalars()] + [whole(v.shape) for v in args],
        whole(x.shape),
        shaped(x.shape),
        us=3,
    )(meta, *args)


def hidden_back_kernel(
    streams,
    meta_ref,
    x_ref,
    back_ref,
    back_other_ref,
    cot_ref,
    w_ref,
    gain_ref,
    *refs,
):
    lists, refs = refs[: 4 * streams], refs[4 * streams :]
    grad_hidden_ref, grad_merged_ref, grad_w_ref, vector_ref, w_acc, stats = refs[:6]
    stream = pl.program_id(0)
    rows = x_ref.shape[1]
    for place, scratch in enumerate(refs[6:]):
        pick(stream, lists[place * streams : (place + 1) * streams], scratch)
    a_ref, b_ref, merged_ref, total_ref = refs[6:]
    hidden = x_ref[0].astype(WIDE) + (a_ref[...].astype(WIDE) + b_ref[...].astype(WIDE))
    normed, inverse = norm_stats(hidden)
    place = meta_ref[META_TIER] * rows + lax.broadcasted_iota(jnp.int32, (rows, 1), 0)
    ok = place < meta_ref[META_STREAMS + stream]
    back = back_ref[0].astype(WIDE) + back_other_ref[0].astype(WIDE)
    grad_out = jnp.where(ok, cot_ref[0].astype(WIDE), 0.0)
    grad_hidden = grad_out + norm_back(back, normed, inverse, gain_ref[...])
    grad_hidden_ref[0] = grad_hidden
    low = grad_hidden.astype(LOW)
    merged = merged_ref[...]
    grad_merged = dot(low, w_ref[...], NT).astype(LOW)
    grad_merged_ref[0, :rows, :] = grad_merged
    heads = merged.shape[1] // HD
    stats[:heads, :] = total_ref[...]
    product = grad_merged.astype(WIDE) * merged.astype(WIDE)
    for head in range(heads):
        turned = product[:, head * HD : (head + 1) * HD].T
        stats[heads + head : heads + head + 1, :] = jnp.sum(turned, axis=0, keepdims=True)
    put_packed(grad_merged_ref.at[0], rows, stats[...])
    grad_w = dot(merged, low, TN)
    gain_part = jnp.sum(back * normed, axis=0, keepdims=True)
    bias_part = jnp.sum(back, axis=0, keepdims=True)

    @pl.when(stream == 0)
    def _():
        w_acc[...] = grad_w
        vector_ref[0:1, :] = gain_part
        vector_ref[1:2, :] = bias_part

    @pl.when(stream != 0)
    def _():
        w_acc[...] += grad_w
        vector_ref[0:1, :] += gain_part
        vector_ref[1:2, :] += bias_part

    @pl.when(stream == pl.num_programs(0) - 1)
    def _():
        grad_w_ref[...] = w_acc[...].astype(LOW)


def hidden_back(chain, meta, x, a, b, back, back_other, cot, merged, total, w, gain):
    streams, rows, width = x.shape
    features = w.shape[0]
    heads = features // HD
    outs = [
        shaped(x.shape, WIDE),
        shaped((streams, rows + packed_rows(2 * heads), features)),
        shaped(w.shape),
        shaped((2, width), WIDE),
    ]
    streamed = (x, back, back_other, cot)
    lists = (*a, *b, *merged, *total)
    return chain.call(
        functools.partial(hidden_back_kernel, streams),
        (streams,),
        [scalars()]
        + [per_stream(v.shape) for v in streamed]
        + [whole(v.shape) for v in (w, gain, *lists)],
        [per_stream(o.shape) for o in outs[:2]] + [whole(o.shape) for o in outs[2:]],
        outs,
        scratch=[
            pltpu.VMEM(w.shape, WIDE),
            pltpu.VMEM((2 * heads, rows), WIDE),
            pltpu.VMEM((rows, width), LOW),
            pltpu.VMEM((rows, width), LOW),
            pltpu.VMEM((rows, features), LOW),
            pltpu.VMEM((heads, rows), WIDE),
        ],
        us=6.5,
        vmem=VMEM_WIDE,
    )(meta, *streamed, w, gain, *lists)


def attend_back_kernel(own, streams, meta_ref, gm_ref, km_ref, vm_ref, ks_ref, vs_ref, *refs):
    *refs, q_ref = refs
    pick(pl.program_id(0), refs[: streams], q_ref)
    refs = refs[streams :]
    if own:
        gq_ref, gkm_ref, gvm_ref, gks_ref, gvs_ref = refs
        before = None
    else:
        before, (gq_ref, gkm_ref, gvm_ref, gks_ref, gvs_ref) = refs[:4], refs[4:]
    stream = pl.program_id(0)
    slots, rows = km_ref.shape[1], q_ref.shape[0]
    heads = q_ref.shape[1] // HD
    stats = get_packed(gm_ref.at[0], rows, 2 * heads, rows)

    def put(ref, index, cols, value):
        if before is not None:
            value = value + before[index][0, :, cols]
        ref[0, :, cols] = value.astype(ref.dtype)

    def body(with_segment):
        memory_ok, segment_ok = slot_masks(own, meta_ref, stream, streams, slots, rows)
        for head in range(heads):
            cols = slice(head * HD, (head + 1) * HD)
            query = q_ref[:, cols]
            grad = gm_ref[0, :rows, cols]
            total = stats[head : head + 1, :]
            delta = stats[heads + head : heads + head + 1, :]

            def tier(key, value, ok):
                scores = jnp.where(ok, dot(key, query, NT) * (SCALE * LOG2E), NEG)
                weights = jnp.exp2(scores - total)
                grad_scores = (weights * (dot(value, grad, NT) - delta)).astype(LOW)
                return (
                    dot(key, grad_scores, TN),
                    dot(grad_scores, query) * SCALE,
                    dot(weights.astype(LOW), grad),
                )

            turned, grad_key, grad_value = tier(km_ref[0, :, cols], vm_ref[0, :, cols], memory_ok)
            put(gkm_ref, 0, cols, grad_key)
            put(gvm_ref, 1, cols, grad_value)
            if with_segment:
                more, grad_key, grad_value = tier(
                    ks_ref[0, :, cols], vs_ref[0, :, cols], segment_ok
                )
                turned = turned + more
                put(gks_ref, 2, cols, grad_key)
                put(gvs_ref, 3, cols, grad_value)
            else:
                gks_ref[0, :, cols] = before[2][0, :, cols].astype(gks_ref.dtype)
                gvs_ref[0, :, cols] = before[3][0, :, cols].astype(gvs_ref.dtype)
            gq_ref[0, :, cols] = (turned * SCALE).T.astype(LOW)

    by_tier(own, meta_ref, body)


def attend_back(chain, own, meta, queries, gm, km, vm, ks, vs, before=()):
    streams = len(queries)
    rows, features = queries[0].shape
    kind = WIDE if own else LOW
    outs = [shaped((streams, rows, features))] + [shaped(a.shape, kind) for a in (km, vm, ks, vs)]
    return chain.call(
        functools.partial(attend_back_kernel, own, streams),
        (streams,),
        [scalars()]
        + [per_stream(a.shape) for a in (gm, km, vm, ks, vs)]
        + [whole(q.shape) for q in queries]
        + [per_stream(a.shape) for a in before],
        [per_stream(o.shape) for o in outs],
        outs,
        scratch=[pltpu.VMEM((rows, features), LOW)],
        us=10,
        vmem=VMEM_WIDE,
    )(meta, gm, km, vm, ks, vs, *queries, *before)


def row_of(column):
    return jnp.broadcast_to(column, (column.shape[0], HD)).T[0:1, :]


def key_value_kernel_back(
    bits, meta_ref, unit_ref, stored_ref, gks_ref, gvs_ref, gkm_ref, gvm_ref,
    wk_ref, wv_ref, gain_ref, bias_ref, column_ref, sent_ref, kept_ref, k_acc, v_acc, sums
):
    stream = pl.program_id(0)
    width, features = wk_ref.shape

    @pl.when(stream == 0)
    def _():
        k_acc[...] = jnp.zeros_like(k_acc)
        v_acc[...] = jnp.zeros_like(v_acc)
        sums[...] = jnp.zeros_like(sums)

    unit, stored = unit_ref[0].T, stored_ref[0].T
    gks, gvs, gkm, gvm = gks_ref[0], gvs_ref[0], gkm_ref[0], gvm_ref[0]
    k_acc[...] += dot(unit, gks) + dot(stored, gkm)
    v_acc[...] += dot(unit, gvs) + dot(stored, gvm)
    for place, pair in enumerate(((gks, gkm), (gvs, gvm))):
        for piece in pair:
            sums[place : place + 1, :] += jnp.sum(piece.astype(WIDE), axis=0, keepdims=True)

    @pl.when(stream == pl.num_programs(0) - 1)
    def _():
        wk, wv = wk_ref[...].astype(WIDE), wv_ref[...].astype(WIDE)
        column_ref[0:1, :] = row_of(jnp.sum(wk * k_acc[...] + wv * v_acc[...], axis=1, keepdims=True))
        column_ref[1:2, :] = row_of(
            jnp.sum(wk * sums[0:1, :] + wv * sums[1:2, :], axis=1, keepdims=True)
        )
        half = width // 2
        side = pair_side(meta_ref, bits)
        for ref, which in ((sent_ref, 1 - side), (kept_ref, side)):
            rows = pl.ds(pl.multiple_of(which * half, half), half)
            gain, bias = gain_ref[rows, :], bias_ref[rows, :]
            ref[:, :features] = (gain * k_acc[rows, :] + bias * sums[0:1, :]).astype(LOW)
            ref[:, features:] = (gain * v_acc[rows, :] + bias * sums[1:2, :]).astype(LOW)


def key_value_grads(chain, orders, meta, streamed, fixed):
    width, features = fixed[0].shape
    outs = [shaped((2, width), WIDE)] + [shaped((width // 2, 2 * features))] * 2
    acc = pltpu.VMEM((width, features), WIDE)
    return chain.call(
        functools.partial(key_value_kernel_back, tuple(order[0] for order in orders)),
        (streamed[0].shape[0],),
        [scalars()] + [per_stream(v.shape) for v in streamed] + [whole(v.shape) for v in fixed],
        [whole(o.shape) for o in outs],
        outs,
        scratch=[acc, acc, pltpu.VMEM((2, features), WIDE)],
        vmem=VMEM_WIDE,
        us=10,
    )(meta, *streamed, *fixed)


def query_kernel_back(
    bits, meta_ref, unit_ref, own_ref, came_ref, gks_ref, gvs_ref,
    wq_ref, wk_ref, wv_ref, gwo_ref, gain_ref, bias_ref, column_ref, vector_ref, normed_ref,
    sent_ref, kept_ref, q_acc, sums
):
    stream = pl.program_id(0)
    width, features = wq_ref.shape

    @pl.when(stream == 0)
    def _():
        q_acc[...] = jnp.zeros_like(q_acc)
        sums[...] = jnp.zeros_like(sums)

    grad = (own_ref[0].astype(WIDE) + came_ref[0].astype(WIDE)).astype(LOW)
    q_acc[...] += dot(unit_ref[0], grad, TN)
    sums[...] += jnp.sum(grad.astype(WIDE), axis=0, keepdims=True)
    normed_ref[0] = (
        dot(grad, wq_ref[...], NT) + dot(gks_ref[0], wk_ref[...], NT) + dot(gvs_ref[0], wv_ref[...], NT)
    ).astype(LOW)

    @pl.when(stream == pl.num_programs(0) - 1)
    def _():
        wq = wq_ref[...].astype(WIDE)
        gain_part = row_of(jnp.sum(wq * q_acc[...], axis=1, keepdims=True))
        bias_part = row_of(jnp.sum(wq * sums[...], axis=1, keepdims=True))
        query = (gain_ref[...] * q_acc[...] + bias_ref[...] * sums[...]).astype(LOW)
        half = width // 2
        extra = sent_ref.shape[0] - half

        def put(out_ref, query_ref):
            out_ref[:half, :] = gwo_ref[...]
            out_ref[half:, :] = jnp.zeros((extra, width), LOW)
            out_ref[half : half + 1, :] = (column_ref[0:1, :] + gain_part).astype(LOW)
            out_ref[half + 1 : half + 2, :] = (column_ref[1:2, :] + bias_part).astype(LOW)
            out_ref[half + 2 : half + 4, :] = (0.5 * vector_ref[...]).astype(LOW)
            query_ref[:half, :features] = query[:half]
            query_ref[:half, features:] = query[half:]
            query_ref[half:, :] = jnp.zeros((extra, width), LOW)

        side = pair_side(meta_ref, bits)

        @pl.when(side == 0)
        def _():
            put(kept_ref, sent_ref)

        @pl.when(side != 0)
        def _():
            put(sent_ref, kept_ref)


def query_grads(chain, orders, meta, streamed, fixed):
    width, features = fixed[0].shape
    unit = streamed[0]
    outs = [shaped(unit.shape)]
    outs += [shaped((width // 2 + EXTRA, 2 * features))] * 2
    return chain.call(
        functools.partial(query_kernel_back, tuple(order[0] for order in orders)),
        (unit.shape[0],),
        [scalars()] + [per_stream(v.shape) for v in streamed] + [whole(v.shape) for v in fixed],
        [per_stream(unit.shape)] + [whole(o.shape) for o in outs[1:]],
        outs,
        scratch=[pltpu.VMEM((width, features), WIDE), pltpu.VMEM((1, features), WIDE)],
        vmem=VMEM_WIDE,
        us=9,
    )(meta, *streamed, *fixed)


def input_back_kernel(x_ref, own_ref, other_ref, hidden_ref, gain_ref, out_ref):
    normed, inverse = norm_stats(x_ref[0].astype(WIDE))
    grad = own_ref[0].astype(WIDE) + other_ref[0].astype(WIDE)
    out_ref[0] = (hidden_ref[0] + norm_back(grad, normed, inverse, gain_ref[...])).astype(LOW)


def input_back(chain, x, own, other, grad_hidden, gain):
    streamed = (x, own, other, grad_hidden)
    return chain.call(
        input_back_kernel,
        (x.shape[0],),
        [per_stream(v.shape) for v in streamed] + [whole(gain.shape)],
        per_stream(x.shape),
        shaped(x.shape),
        us=4,
    )(*streamed, gain)


def compress_kernel(bits, meta_ref, memory_ref, came_ref, rest_ref, w_ref, cot_ref, out_ref, *refs):
    sent_ref, kept_ref, acc, grads = refs
    stream = pl.program_id(0)
    streams = pl.num_programs(0)
    head = meta_ref[META_HEAD]
    mine = meta_ref[META_TIER] == 0
    slots, part = came_ref.shape[1], came_ref.shape[2]
    count = out_ref.shape[1]
    place = lax.broadcasted_iota(jnp.int32, (count, slots), 0)
    slot = lax.broadcasted_iota(jnp.int32, (count, slots), 1)
    length = meta_ref[META_STREAMS + stream]
    filled = jnp.where(mine, meta_ref[META_STREAMS + streams + stream], slots)
    ok = lax.broadcasted_iota(jnp.int32, (count, 1), 0) < lax.div(length, jnp.int32(RATE))
    cot = jnp.where(ok, cot_ref[0].astype(WIDE), 0.0).astype(LOW)

    @pl.when(stream == 0)
    def _():
        acc[...] = jnp.zeros_like(acc)

    picks = []
    for shift in range(RATE):
        chosen = (slot == place * RATE + shift) & (slot < filled)
        picks.append(jnp.where(chosen, 1.0, 0.0).astype(LOW))
    result = jnp.zeros(out_ref.shape[1:], WIDE)
    for ref, side in ((came_ref, head), (rest_ref, 1 - head)):
        start = pl.multiple_of(side * part, part)
        stored = jnp.where(mine, memory_ref[0, 0, :, pl.ds(start, part)].astype(WIDE), ref[0].astype(WIDE))
        stored = stored.astype(LOW)
        for shift in range(RATE):
            rows = dot(picks[shift], stored).astype(LOW)
            result = result + dot(rows, w_ref[shift, pl.ds(start, part), :])
            acc[shift, pl.ds(start, part), :] += dot(rows, cot, TN)
    out_ref[0] = jnp.where(ok, result, 0.0).astype(LOW)

    @pl.when(stream == streams - 1)
    def _():
        width = w_ref.shape[1]
        for shift in range(RATE):
            grads[shift * width : (shift + 1) * width, :] = acc[shift].astype(LOW)
        half = sent_ref.shape[0]
        side = pair_side(meta_ref, bits)
        for ref, which in ((sent_ref, 1 - side), (kept_ref, side)):
            ref[...] = grads[pl.ds(pl.multiple_of(which * half, half), half), :]


def compress(chain, orders, meta, memories, came, rest, w, cot):
    flat = (w.shape[0] * w.shape[1], w.shape[2])
    outs = [shaped(cot.shape)] + [shaped((flat[0] // 2, flat[1]))] * 2
    bits = tuple(order[0] for order in orders)
    return chain.call(
        functools.partial(compress_kernel, bits),
        (cot.shape[0],),
        [scalars()]
        + [per_stream(v.shape) for v in (memories, came, rest)]
        + [whole(w.shape), per_stream(cot.shape)],
        [per_stream(cot.shape)] + [whole(o.shape) for o in outs[1:]],
        outs,
        scratch=[pltpu.VMEM(w.shape, WIDE), pltpu.VMEM(flat, LOW)],
        us=5,
    )(meta, memories, came, rest, w, cot)


def bits_of():
    size = lax.axis_size("dp")
    bits = [("tier", 1)]
    step = 1
    while step < size:
        bits.append(("dp", step))
        step *= 2
    return bits


def swap(value, bit):
    axis, step = bit
    return lax.ppermute(value, axis, [(i, i ^ step) for i in range(lax.axis_size(axis))])


def swap_head(value):
    return swap(value, ("head", 1))


def swap_tier(value):
    return swap(value, ("tier", 1))


def swap_pair(value, bits):
    axes = ("dp", "tier", "head")
    sizes = [lax.axis_size(axis) for axis in axes]
    pairs = []
    for dp in range(sizes[0]):
        for tier in range(sizes[1]):
            for head in range(sizes[2]):
                axis, step = bits[head]
                to_dp = dp ^ step if axis == "dp" else dp
                to_tier = tier ^ step if axis == "tier" else tier
                pairs.append(
                    (
                        (dp * sizes[1] + tier) * sizes[2] + head,
                        (to_dp * sizes[1] + to_tier) * sizes[2] + head,
                    )
                )
    return lax.ppermute(value, axes, pairs)


def total_of(first, second):
    return (first.astype(WIDE) + second.astype(WIDE)).astype(LOW)


def scatter_kernel(bits, meta_ref, kept, came, *refs):
    half = kept.shape[0] // 2
    side = pair_side(meta_ref, bits)
    for ref, which in zip(refs, (1 - side, side)):
        rows = pl.ds(pl.multiple_of(which * half, half), half)
        ref[...] = total_of(kept[rows, :], came[rows, :])


def add_kernel(bits, meta_ref, kept, came, *refs):
    refs[0][...] = total_of(kept[...], came[...])


def gather_kernel(bits, meta_ref, held, came, *refs):
    half = held.shape[0]
    side = pair_side(meta_ref, bits)
    refs[0][pl.ds(pl.multiple_of(side * half, half), half), :] = held[...]
    refs[0][pl.ds(pl.multiple_of((1 - side) * half, half), half), :] = came[...]


class Reduce:
    def __init__(self, chain, meta, orders, sent, kept):
        self.chain, self.meta, self.orders = chain, meta, orders
        self.stages = len(orders[0])
        self.depth = min(3, self.stages - 1)
        self.kept = kept
        self.stage = 0
        self.send(sent, 0)

    def bits(self, level):
        return tuple(order[level] for order in self.orders)

    def send(self, array, level):
        self.came = swap_pair(array, self.bits(level))

    def run(self, kernel, level, outs):
        return self.chain.call(
            functools.partial(kernel, self.bits(level)),
            (1,),
            [scalars(), whole(self.kept.shape), whole(self.came.shape)],
            [whole(o.shape) for o in outs],
            outs,
            vmem=8,
        )(self.meta, self.kept, self.came)

    def ready(self):
        return self.stage >= self.stages + self.depth - 1

    def step(self):
        depth, stage, stages = self.depth, self.stage, self.stages
        self.stage += 1
        rows, width = self.kept.shape
        if stage < depth - 1:
            sent, self.kept = self.run(
                scatter_kernel, stage + 1, [shaped((rows // 2, width))] * 2
            )
            self.send(sent, stage + 1)
        elif stage < stages:
            (self.kept,) = self.run(add_kernel, stage, [shaped((rows, width))])
            self.send(self.kept, stage + 1 if stage + 1 < stages else depth - 1)
        else:
            level = depth - 1 - (stage - stages)
            (self.kept,) = self.run(gather_kernel, level, [shaped((2 * rows, width))])
            self.send(self.kept, level - 1)


def finish_kernel(bits, write, carried, meta_ref, held, came, *refs):
    write(pair_side(meta_ref, bits), held, came, refs[carried:])


def finish(group, write, out_shapes, out_specs, carried=()):
    args = [group.meta, group.kept, group.came, *carried]
    count = len(carried)
    return group.chain.call(
        functools.partial(finish_kernel, group.bits(0), write, count),
        (1,),
        [scalars(), whole(group.kept.shape), whole(group.came.shape)] + [any_spec()] * count,
        out_specs,
        out_shapes,
        vmem=24,
        alias={3 + i: i for i in range(count)},
        us=3,
    )(*args)


def write_rows(side, held, came, outs):
    half = held.shape[0]
    for ref, which in ((held, side), (came, 1 - side)):
        outs[0][pl.ds(pl.multiple_of(which * half, half), half), :] = ref[...].astype(WIDE)


def finish_ffn(group, part, out_shape, in_shape, carried=()):
    specs = [
        pl.BlockSpec((out_shape[0] // 2, out_shape[1]), lambda i: (part, 0)),
        pl.BlockSpec((in_shape[0], in_shape[1] // 2), lambda i: (0, part)),
    ]

    def write(side, held, came, outs):
        for out_ref, in_ref, which in ((held, came, 0), (came, held, 1)):

            @pl.when(side == which)
            def _():
                outs[0][...] = out_ref[...].astype(WIDE)
                outs[1][...] = in_ref[...].astype(WIDE)

    return finish(group, write, [shaped(out_shape, WIDE), shaped(in_shape, WIDE)], specs, carried)


def finish_key_value(group, width, features):
    shapes = [shaped((width, features), WIDE)] * 2

    def write(side, held, came, outs):
        half = held.shape[0]
        for ref, which in ((held, side), (came, 1 - side)):
            rows = pl.ds(pl.multiple_of(which * half, half), half)
            outs[0][rows, :] = ref[:, :features].astype(WIDE)
            outs[1][rows, :] = ref[:, features:].astype(WIDE)

    return finish(group, write, shapes, [whole_block(v.shape) for v in shapes])


def finish_out_query(group, width, features):
    shapes = [shaped((features, width), WIDE), shaped((width, features), WIDE), shaped((16, width))]

    def write(side, held, came, outs):
        def put(out_ref, query_ref):
            half = outs[0].shape[0]
            outs[0][...] = out_ref[:half, :].astype(WIDE)
            outs[1][:half, :] = query_ref[:half, :features].astype(WIDE)
            outs[1][half:, :] = query_ref[:half, features:].astype(WIDE)
            outs[2][...] = out_ref[half : half + 16, :]

        @pl.when(side == 0)
        def _():
            put(held, came)

        @pl.when(side != 0)
        def _():
            put(came, held)

    return finish(
        group, write, shapes, [whole_block(v.shape) for v in shapes[:2]] + [whole(shapes[2].shape)]
    )


def finish_compress(group, shape):
    flat = (shape[0] * shape[1], shape[2])
    return finish(group, write_rows, [shaped(flat, WIDE)], [whole_block(flat)])[0].reshape(shape)


def on_device(
    inputs,
    memories,
    seg_len,
    mem_count,
    w_query,
    w_key,
    w_value,
    w_attn_out,
    w_ffn_in,
    w_ffn_out,
    w_compress,
    gain_attn,
    bias_attn,
    gain_ffn,
    bias_ffn,
    cotan_output,
    cotan_compressed,
):
    tier_index = lax.axis_index("tier")
    streams, rows, width = inputs.shape
    features = w_query.shape[1]
    hidden_units = w_ffn_in.shape[1]
    counts = mem_count[:, 0]
    place = jnp.stack([tier_index, lax.axis_index("head"), lax.axis_index("dp")])
    meta = jnp.concatenate([place, seg_len, counts], 0).astype(jnp.int32)
    gain_row, bias_row = gain_attn[None], bias_attn[None]
    gain_second, bias_second = gain_ffn[None], bias_ffn[None]
    chain = Chain()

    unit, low, queries = query_rows(chain, meta, inputs, gain_row, bias_row, w_query)
    queries_other = [swap_tier(q) for q in queries]
    keys, values = key_values(chain, low, w_key, w_value)
    stored, memory_keys, memory_values = stored_rows(
        chain, memories, gain_row, bias_row, w_key, w_value
    )
    tiers = (memory_keys, memory_values, keys, values)
    own, came = [], []
    for stream in range(streams):
        came.append(swap_tier(attend(chain, False, stream, meta, queries_other[stream], *tiers)))
        own.append(attend(chain, True, stream, meta, queries[stream], *tiers))
    got = {}
    merged, totals, attended, attended_other = [], [], [], []
    for stream in range(streams):
        low, total, part = merge(chain, rows, own[stream], came[stream], w_attn_out)
        merged.append(low)
        totals.append(total)
        attended.append(part)
        attended_other.append(swap_head(part))
    got["evicted"] = lax.ppermute(evicted_rows(chain, meta, memories), "tier", [(0, 1)])

    tier, low_bit, *more = bits_of()
    high_bit, far_bit, more = more[0], more[1], more[2:]
    axes = {"x": tier, "y": low_bit, "z": high_bit, "w": far_bit}
    orders = {}
    for name, paths in PATHS.items():
        rest = "yzw" if name == "compress" else "xyzw"
        orders[name] = tuple(
            tuple(axes[axis] for axis in dict.fromkeys(path + rest)) + tuple(more)
            for path in paths.split("/")
        )
    flat = (streams * rows, width)
    hidden_args = (
        inputs.reshape(flat),
        cotan_output.reshape(flat),
        gain_second,
        bias_second,
        *attended,
        *attended_other,
    )
    groups = {}

    def begin(name, sent, kept):
        groups[name] = Reduce(chain, meta, orders[name], sent, kept)

    def run_ffn():
        names = ("f1", "f2")
        got["act"], back, *parts = ffn(
            chain, streams, [orders[name] for name in names], meta, hidden_args, w_ffn_in, w_ffn_out
        )
        got["back"] = back.reshape(inputs.shape)
        got["back_other"] = swap_head(got["back"])
        for place, name in enumerate(names):
            begin(name, *parts[2 * place : 2 * place + 2])

    def run_ffn3():
        got["ffn"] = ffn_out(chain, got["act"], w_ffn_out).reshape(inputs.shape)
        got["ffn_other"] = swap_head(got["ffn"])

    def run_hidden():
        got["hidden"], got["gm"], got["gwo"], vectors_ffn = hidden_back(
            chain, meta, inputs, attended, attended_other, got["back"], got["back_other"],
            cotan_output, merged, totals, w_attn_out, gain_second,
        )
        got["gm_other"] = swap_tier(got["gm"])
        got["vectors"] = vectors_ffn

    def run_own():
        got["own"], *got["sums"] = attend_back(chain, True, meta, queries, got["gm"], *tiers)

    def run_other():
        got["other"], *got["grads"] = attend_back(
            chain, False, meta, queries_other, got["gm_other"], *tiers,
            before=tuple(got["sums"]),
        )
        got["came"] = swap_tier(got["other"])

    def run_output():
        got["output"] = output_rows(
            chain, meta, inputs, got["ffn"], got["ffn_other"], attended, attended_other
        )

    def run_grads():
        grad_km, grad_vm, grad_ks, grad_vs = got["grads"]
        got["column"], *parts = key_value_grads(
            chain, orders["kv"], meta, (unit, stored, grad_ks, grad_vs, grad_km, grad_vm),
            (w_key, w_value, gain_attn[:, None], bias_attn[:, None]),
        )
        begin("kv", *parts)

    def run_query():
        _, _, grad_ks, grad_vs = got["grads"]
        got["normed"], *parts = query_grads(
            chain, orders["oq"], meta, (unit, got["own"], got["came"], grad_ks, grad_vs),
            (
                w_query, w_key, w_value, got["gwo"], gain_attn[:, None], bias_attn[:, None],
                got["column"], got["vectors"],
            ),
        )
        got["normed_other"] = swap_head(got["normed"])
        begin("oq", *parts)

    def run_evict2():
        got["evicted"] = copied(chain, got["evicted"])
        got["evicted_other"] = swap_head(got["evicted"])

    def run_evict3():
        got["evicted_other"] = copied(chain, got["evicted_other"])

    def run_input():
        got["grad_inputs"] = input_back(
            chain, inputs, got["normed"], got["normed_other"], got["hidden"], gain_row
        )

    def run_compress():
        got["compressed"], *parts = compress(
            chain, orders["compress"], meta, memories, got["evicted"], got["evicted_other"],
            w_compress, cotan_compressed,
        )
        begin("compress", *parts)

    def end(name):
        group = groups.pop(name)
        out_shape, in_shape = w_ffn_out.shape, w_ffn_in.shape
        if name == "f1":
            got["ffn_grads"] = finish_ffn(group, 0, out_shape, in_shape)
        elif name == "f2":
            got["ffn_grads"] = finish_ffn(group, 1, out_shape, in_shape, got["ffn_grads"])
        elif name == "kv":
            got["kv"] = finish_key_value(group, width, features)
        elif name == "oq":
            got["oq"] = finish_out_query(group, width, features)
            got["vector"] = got["oq"][2]
        else:
            got["compress"] = finish_compress(group, w_compress.shape)

    runs = {
        "ffn": run_ffn, "ffn3": run_ffn3, "hidden": run_hidden, "own": run_own,
        "other": run_other, "output": run_output, "grads": run_grads, "query": run_query,
        "evict2": run_evict2, "evict3": run_evict3, "input": run_input, "compr": run_compress, "pause": lambda: pause(chain),
    }
    chain.cost = COST
    for name in ORDER:
        if name in runs:
            runs[name]()
        elif name in groups and groups[name].ready():
            end(name)
        elif name in groups:
            groups[name].step()
    while groups:
        for name in list(groups):
            if groups[name].ready():
                end(name)
            else:
                groups[name].step()
    vectors = got["vector"].astype(WIDE) + swap_head(got["vector"]).astype(WIDE)
    return (
        got["output"],
        got["compressed"],
        got["grad_inputs"],
        got["oq"][1],
        *got["kv"],
        got["oq"][0],
        got["ffn_grads"][1],
        got["ffn_grads"][0],
        got["compress"],
        vectors[0],
        vectors[1],
        vectors[2],
        vectors[3],
    )


def solution(mesh):
    return jax.shard_map(
        on_device,
        mesh=mesh,
        in_specs=(
            P("dp", "tier", None),
            P("dp", "tier", None, None),
            P("dp"),
            P("dp", "tier"),
            P(None, "head"),
            P(None, "head"),
            P(None, "head"),
            P("head", None),
            P(None, "head"),
            P("head", None),
            P(None, None, ("tier", "head")),
            P(),
            P(),
            P(),
            P(),
            P("dp", "tier", None),
            P("dp", None, ("tier", "head")),
        ),
        out_specs=(
            P("dp", "tier", None),
            P("dp", None, ("tier", "head")),
            P("dp", "tier", None),
            P(None, "head"),
            P(None, "head"),
            P(None, "head"),
            P("head", None),
            P(None, "head"),
            P("head", None),
            P(None, None, ("tier", "head")),
            P(),
            P(),
            P(),
            P(),
        ),
        check_vma=False,
    )
```

```python
import functools

import jax
import jax.numpy as jnp
from jax import lax
from jax.experimental import pallas as pl
from jax.experimental.pallas import tpu as pltpu
from jax.sharding import PartitionSpec as P

HD = 128
RATE = 3
EPS = 1e-05
NEG = -1000000000.0
LOG2E = 1.4426950408889634
SCALE = HD ** (-0.5)
GELU_ROOT = 0.7978845608028654
GELU_CUBE = 0.044715

ORDER = (
    "ffn", "back", "pause", "hidden", "evict2", "own", "evict3", "ffn3", "f1", "f2", "other",
    "output", "grads", "f1", "f2", "query", "f1", "f2", "kv", "input", "oq", "f1", "f2", "kv",
    "compr", "oq", "f1", "f2", "kv", "compress", "oq", "f1", "f2", "kv", "compress", "oq", "kv",
    "compress", "oq", "f1", "f2", "kv", "compress", "oq", "kv", "oq",
)

PATHS = {
    "f1": "yxw/zxy",
    "f2": "xwz/yzx",
    "kv": "zxy/xzy",
    "oq": "xyw/yzx",
    "compress": "yz/zy",
}

COST = 1e10
COST_EARLY = 1e8
PAUSE = 10
VMEM_FFN = 28
VMEM_WIDE = 25
EXTRA = 64

LOW = jnp.bfloat16
WIDE = jnp.float32
NN = (((1,), (0,)), ((), ()))
NT = (((1,), (1,)), ((), ()))
TN = (((0,), (0,)), ((), ()))


def dot(first, second, dims=NN):
    return lax.dot_general(first, second, dims, preferred_element_type=WIDE)


def norm_stats(values):
    centre = values - jnp.mean(values, axis=-1, keepdims=True)
    inverse = lax.rsqrt(jnp.mean(centre * centre, axis=-1, keepdims=True) + EPS)
    return (centre * inverse, inverse)


def norm_back(grad_normed, normed, inverse, gain_vector):
    scaled = grad_normed * gain_vector
    return inverse * (
        scaled
        - jnp.mean(scaled, axis=-1, keepdims=True)
        - normed * jnp.mean(scaled * normed, axis=-1, keepdims=True)
    )


def per_stream(array_shape):
    block = (1,) + tuple(array_shape[1:])
    zeros = (0,) * (len(block) - 1)
    return pl.BlockSpec(block, lambda s: (s,) + zeros)


def whole(array_shape):
    return pl.BlockSpec(memory_space=pltpu.VMEM)


def whole_block(array_shape):
    zeros = (0,) * len(array_shape)
    return pl.BlockSpec(tuple(array_shape), lambda *_: zeros)


def scalars():
    return pl.BlockSpec(memory_space=pltpu.SMEM)


def shaped(shape, dtype=LOW):
    return jax.ShapeDtypeStruct(tuple(shape), dtype)


class Chain:
    def __init__(self):
        self.last = None
        self.cost = COST_EARLY

    def call(self, kernel, grid, in_specs, out_specs, out_shape, scratch=(), vmem=16, alias=None, us=1.0):
        last = self.last
        count = len(in_specs)

        def ordered(*refs):
            kernel(*refs[:count], *refs[count + 1 :])

        def run(*args):
            specs = list(in_specs)
            args = list(args)
            body = kernel
            if last is not None:
                specs.append(pl.BlockSpec(memory_space=pl.ANY))
                args.append(last)
                body = ordered
            outs = pl.pallas_call(
                body,
                grid=grid,
                in_specs=specs,
                out_specs=out_specs,
                out_shape=out_shape,
                scratch_shapes=list(scratch),
                input_output_aliases=alias or {},
                compiler_params=pltpu.CompilerParams(vmem_limit_bytes=vmem * 1024 * 1024),
                cost_estimate=pl.CostEstimate(
                    flops=int(us * self.cost), bytes_accessed=0, transcendentals=0
                ),
            )(*args)
            if not alias:
                self.last = outs[0] if isinstance(outs, (list, tuple)) else outs
            return outs

        return run


META_TIER, META_HEAD, META_DP, META_STREAMS = 0, 1, 2, 3


def any_spec():
    return pl.BlockSpec(memory_space=pl.ANY)


def query_kernel(meta_ref, x_ref, gain_ref, bias_ref, w_ref, unit_ref, low_ref, *outs):
    for stream in range(x_ref.shape[0]):
        normed, _ = norm_stats(x_ref[stream].astype(WIDE))
        unit_ref[stream] = normed.astype(LOW)
        low = (normed * gain_ref[...] + bias_ref[...]).astype(LOW)
        low_ref[stream] = low
        outs[stream][...] = dot(low, w_ref[...]).astype(LOW)


def query_rows(chain, meta, x, gain, bias, w):
    streams, rows, width = x.shape
    outs = [shaped(x.shape), shaped(x.shape)]
    outs += [shaped((rows, w.shape[1]))] * streams
    unit, low, *queries = chain.call(
        query_kernel,
        (1,),
        [scalars()] + [whole(v.shape) for v in (x, gain, bias, w)],
        [whole(o.shape) for o in outs],
        outs,
        us=3,
    )(meta, x, gain, bias, w)
    return unit, low, queries


def key_value_kernel(low_ref, wk_ref, wv_ref, k_ref, v_ref):
    k_ref[0] = dot(low_ref[0], wk_ref[...]).astype(LOW)
    v_ref[0] = dot(low_ref[0], wv_ref[...]).astype(LOW)


def key_values(chain, low, wk, wv):
    outs = [shaped(low.shape[:2] + wk.shape[1:])] * 2
    return chain.call(
        key_value_kernel,
        (low.shape[0],),
        [per_stream(low.shape), whole(wk.shape), whole(wv.shape)],
        [per_stream(o.shape) for o in outs],
        outs,
        us=2.5,
    )(low, wk, wv)


def stored_kernel(x_ref, gain_ref, bias_ref, wk_ref, wv_ref, unit_ref, k_ref, v_ref):
    normed, _ = norm_stats(x_ref[0, 0].astype(WIDE))
    unit_ref[0] = normed.astype(LOW)
    low = (normed * gain_ref[...] + bias_ref[...]).astype(LOW)
    k_ref[0] = dot(low, wk_ref[...]).astype(LOW)
    v_ref[0] = dot(low, wv_ref[...]).astype(LOW)


def stored_rows(chain, x, gain, bias, wk, wv):
    streams, _, slots, width = x.shape
    outs = [shaped((streams, slots, width))] + [shaped((streams, slots, wk.shape[1]))] * 2
    return chain.call(
        stored_kernel,
        (streams,),
        [per_stream(x.shape)] + [whole(v.shape) for v in (gain, bias, wk, wv)],
        [per_stream(o.shape) for o in outs],
        outs,
        us=6,
    )(x, gain, bias, wk, wv)


def slot_masks(own, meta_ref, stream, streams, slots, rows):
    tier = meta_ref[META_TIER]
    length = meta_ref[META_STREAMS + stream]
    filled = meta_ref[META_STREAMS + streams + stream]
    memory_ok = lax.broadcasted_iota(jnp.int32, (slots, rows), 0) < filled
    key_row = lax.broadcasted_iota(jnp.int32, (rows, rows), 0)
    segment_ok = (tier * rows + key_row) < length
    if own:
        query_row = lax.broadcasted_iota(jnp.int32, (rows, rows), 1)
        segment_ok = segment_ok & (key_row <= query_row)
    return memory_ok, segment_ok


def by_tier(own, meta_ref, body):
    if own:
        body(True)
        return

    @pl.when(meta_ref[META_TIER] == 0)
    def _():
        body(True)

    @pl.when(meta_ref[META_TIER] != 0)
    def _():
        body(False)


def put_packed(ref, row, value):
    count, width = value.shape
    for part in range(3):
        low = value.astype(LOW)
        ref[row + part * count : row + (part + 1) * count, :width] = low
        value = value - low.astype(WIDE)


def get_packed(ref, row, count, width):
    parts = [
        ref[row + part * count : row + (part + 1) * count, :width].astype(WIDE) for part in range(3)
    ]
    return parts[0] + (parts[1] + parts[2])


def packed_rows(count):
    return -(-3 * count // 16) * 16


def attend_kernel(own, stream, streams, meta_ref, q_ref, km_ref, vm_ref, ks_ref, vs_ref, out_ref, totals):
    slots, rows = km_ref.shape[1], q_ref.shape[0]
    heads = q_ref.shape[1] // HD

    def body(with_segment):
        memory_ok, segment_ok = slot_masks(own, meta_ref, stream, streams, slots, rows)
        for head in range(heads):
            cols = slice(head * HD, (head + 1) * HD)
            query = q_ref[:, cols]
            scores = jnp.where(
                memory_ok, dot(km_ref[0, :, cols], query, NT) * (SCALE * LOG2E), NEG
            )
            top = jnp.max(scores, axis=0, keepdims=True)
            if with_segment:
                near = jnp.where(
                    segment_ok, dot(ks_ref[0, :, cols], query, NT) * (SCALE * LOG2E), NEG
                )
                top = jnp.maximum(top, jnp.max(near, axis=0, keepdims=True))
            raw = jnp.exp2(scores - top)
            spent = jnp.sum(raw, axis=0, keepdims=True)
            mixed = dot(vm_ref[0, :, cols], raw.astype(LOW), TN)
            if with_segment:
                raw_near = jnp.exp2(near - top)
                spent = spent + jnp.sum(raw_near, axis=0, keepdims=True)
                mixed = mixed + dot(vs_ref[0, :, cols], raw_near.astype(LOW), TN)
            out_ref[:rows, cols] = (mixed / spent).T.astype(LOW)
            totals[head : head + 1, :] = top + jnp.log2(spent)
        put_packed(out_ref, rows, totals[...])

    by_tier(own, meta_ref, body)


def one_stream(array, stream):
    return pl.BlockSpec((1,) + array.shape[1:], lambda i: (stream, 0, 0))


def attend(chain, own, stream, meta, q, km, vm, ks, vs):
    rows, features = q.shape
    heads = features // HD
    out = shaped((rows + packed_rows(heads), features))
    return chain.call(
        functools.partial(attend_kernel, own, stream, km.shape[0]),
        (1,),
        [scalars(), whole(q.shape)] + [one_stream(a, stream) for a in (km, vm, ks, vs)],
        whole(out.shape),
        out,
        scratch=[pltpu.VMEM((heads, rows), WIDE)],
        us=2.6,
    )(meta, q, km, vm, ks, vs)


def merge_kernel(w_ref, own_ref, other_ref, low_ref, total_ref, part_ref):
    rows, features = low_ref.shape
    heads = features // HD
    first = get_packed(own_ref, rows, heads, rows)
    second = get_packed(other_ref, rows, heads, rows)
    top = jnp.maximum(first, second)
    total = top + jnp.log2(jnp.exp2(first - top) + jnp.exp2(second - top))
    total_ref[...] = total
    share_own, share_other = jnp.exp2(first - total), jnp.exp2(second - total)
    for head in range(heads):
        cols = slice(head * HD, (head + 1) * HD)
        column_own = jnp.broadcast_to(share_own[head : head + 1], (HD, rows)).T
        column_other = jnp.broadcast_to(share_other[head : head + 1], (HD, rows)).T
        merged = (
            own_ref[:rows, cols].astype(WIDE) * column_own
            + other_ref[:rows, cols].astype(WIDE) * column_other
        )
        low_ref[:, cols] = merged.astype(LOW)
    part_ref[...] = dot(low_ref[...], w_ref[...]).astype(LOW)


def merge(chain, rows, own, other, w):
    features = own.shape[1]
    outs = [
        shaped((rows, features)),
        shaped((features // HD, rows), WIDE),
        shaped((rows, w.shape[1])),
    ]
    args = (w, own, other)
    return chain.call(
        merge_kernel,
        (1,),
        [whole(v.shape) for v in args],
        [whole(o.shape) for o in outs],
        outs,
        us=1.0,
    )(*args)


def evicted_kernel(streams, meta_ref, memory_ref, evicted_ref):
    part = evicted_ref.shape[2]
    start = pl.multiple_of(meta_ref[META_HEAD] * part, part)
    filled = meta_ref[META_STREAMS + streams + pl.program_id(0)]
    ok = lax.broadcasted_iota(jnp.int32, (evicted_ref.shape[1], 1), 0) < filled
    rows = memory_ref[0, 0, :, pl.ds(start, part)].astype(WIDE)
    evicted_ref[0] = jnp.where(ok, rows, 0.0).astype(LOW)


def evicted_rows(chain, meta, memories):
    streams, _, slots, width = memories.shape
    out = (streams, slots, width // 2)
    return chain.call(
        functools.partial(evicted_kernel, streams),
        (streams,),
        [scalars(), per_stream(memories.shape)],
        per_stream(out),
        shaped(out),
        us=2,
    )(meta, memories)


def pause_kernel(out_ref):
    out_ref[...] = jnp.zeros_like(out_ref)


def pause(chain):
    shape = shaped((8, HD), WIDE)
    return chain.call(pause_kernel, (1,), [], whole(shape.shape), shape, us=PAUSE)()


def copied_kernel(in_ref, out_ref):
    out_ref[...] = in_ref[...]


def copied(chain, array):
    return chain.call(
        copied_kernel, (1,), [whole(array.shape)], whole(array.shape), shaped(array.shape)
    )(array)


def pick(stream, refs, scratch):
    for place, ref in enumerate(refs):

        @pl.when(stream == place)
        def _():
            scratch[...] = ref[...]


def valid_rows(meta_ref, streams, rows):
    place = lax.broadcasted_iota(jnp.int32, (streams * rows, 1), 0)
    ok = None
    for stream in range(streams):
        inside = (
            (place >= stream * rows)
            & (place < stream * rows + meta_ref[META_STREAMS + stream] - meta_ref[META_TIER] * rows)
            & (place < (stream + 1) * rows)
        )
        ok = inside if ok is None else ok | inside
    return ok


def side_of(meta_ref, bit):
    axis, step = bit
    if axis == "tier":
        return meta_ref[META_TIER]
    return lax.rem(lax.div(meta_ref[META_DP], jnp.int32(step)), jnp.int32(2))


def pair_side(meta_ref, bits):
    first, second = (side_of(meta_ref, bit) for bit in bits)
    return jnp.where(meta_ref[META_HEAD] == 0, first, second)


def ffn_kernel(streams, bits, meta_ref, *refs):
    x_ref, cot_ref, gain_ref, bias_ref = refs[:4]
    a_refs, b_refs = refs[4 : 4 + streams], refs[4 + streams : 4 + 2 * streams]
    wi_ref, wo_ref, act_ref, lifted_ref, *refs = refs[4 + 2 * streams :]
    parts, (low_ref, turned_ref, grad_ref) = refs[:-3], refs[-3:]
    step = pl.program_id(0)
    units = wi_ref.shape[1]

    @pl.when(step == 0)
    def _():
        rows = x_ref.shape[0] // streams
        for stream in range(streams):
            own = slice(stream * rows, (stream + 1) * rows)
            attended = a_refs[stream][...].astype(WIDE) + b_refs[stream][...].astype(WIDE)
            normed, _ = norm_stats(x_ref[own, :].astype(WIDE) + attended)
            low = (normed * gain_ref[...] + bias_ref[...]).astype(LOW)
            low_ref[own, :] = low
            turned_ref[:, own] = low.T
        ok = valid_rows(meta_ref, streams, x_ref.shape[0] // streams)
        grad_ref[...] = jnp.where(ok, cot_ref[...].astype(WIDE), 0.0).astype(LOW)

    lifted = dot(low_ref[...], wi_ref[...])
    square = lifted * lifted
    bent = jnp.tanh(GELU_ROOT * lifted * (1.0 + GELU_CUBE * square))
    half = 0.5 * (1.0 + bent)
    activated = (lifted * half).astype(LOW)
    act_ref[...] = activated
    slope = half + 0.5 * lifted * (1.0 - bent * bent) * (
        GELU_ROOT * (1.0 + 3.0 * GELU_CUBE * square)
    )
    grad_out = dot(activated, grad_ref[...], TN).astype(LOW)
    grad_lifted = (slope * dot(grad_ref[...], wo_ref[...], NT)).astype(LOW)
    grad_in = dot(turned_ref[...], grad_lifted).astype(LOW)
    place = pl.multiple_of((step % 2) * units, units)
    for part in range(2):
        sent, kept = parts[2 * part : 2 * part + 2]
        side = pair_side(meta_ref, bits[part])
        for out_ref, in_ref, which in ((kept, sent, 0), (sent, kept, 1)):

            @pl.when((step // 2 == part) & (side == which))
            def _():
                out_ref[pl.ds(place, units), :] = grad_out
                in_ref[:, pl.ds(place, units)] = grad_in

    lifted_ref[...] = grad_lifted


def ffn(chain, streams, orders, meta, whole_args, w_in, w_out):
    rows, width = whole_args[0].shape
    units = w_in.shape[1]
    steps = 4
    block = units // steps
    outs = [shaped((rows, units))] * 2
    parts = [shaped((units // 2, width))] * 4
    turned = pltpu.VMEM((width, rows), LOW)
    return chain.call(
        functools.partial(ffn_kernel, streams, tuple((p[0][0], p[1][0]) for p in orders)),
        (steps,),
        [scalars()]
        + [whole(v.shape) for v in whole_args]
        + [
            pl.BlockSpec((width, block), lambda j: (0, j)),
            pl.BlockSpec((block, width), lambda j: (j, 0)),
        ],
        [pl.BlockSpec((rows, block), lambda j: (0, j))] * 2 + [whole(o.shape) for o in parts],
        outs + parts,
        scratch=[
            pltpu.VMEM((rows, width), LOW),
            turned,
            pltpu.VMEM((rows, width), LOW),
        ],
        vmem=VMEM_FFN,
        us=24,
    )(meta, *whole_args, w_in, w_out)


def ffn_back_kernel(grad_ref, w_ref, out_ref, acc):
    step = pl.program_id(0)
    more = dot(grad_ref[...], w_ref[...], NT)

    @pl.when(step == 0)
    def _():
        acc[...] = more

    @pl.when(step != 0)
    def _():
        acc[...] += more

    @pl.when(step == pl.num_programs(0) - 1)
    def _():
        out_ref[...] = acc[...].astype(LOW)


def ffn_back(chain, grad, w):
    rows, units = grad.shape
    width = w.shape[0]
    steps = 2
    block = units // steps
    return chain.call(
        ffn_back_kernel,
        (steps,),
        [pl.BlockSpec((rows, block), lambda j: (0, j)), pl.BlockSpec((width, block), lambda j: (0, j))],
        whole((rows, width)),
        shaped((rows, width)),
        scratch=[pltpu.VMEM((rows, width), WIDE)],
        vmem=24,
        us=5,
    )(grad, w)


def ffn_out_kernel(act_ref, w_ref, out_ref, acc):
    step = pl.program_id(0)
    more = dot(act_ref[...], w_ref[...])

    @pl.when(step == 0)
    def _():
        acc[...] = more

    @pl.when(step != 0)
    def _():
        acc[...] += more

    @pl.when(step == pl.num_programs(0) - 1)
    def _():
        out_ref[...] = acc[...].astype(LOW)


def ffn_out(chain, act, w):
    rows, units = act.shape
    width = w.shape[1]
    steps = 4
    block = units // steps
    return chain.call(
        ffn_out_kernel,
        (steps,),
        [pl.BlockSpec((rows, block), lambda j: (0, j)), pl.BlockSpec((block, width), lambda j: (j, 0))],
        whole((rows, width)),
        shaped((rows, width)),
        scratch=[pltpu.VMEM((rows, width), WIDE)],
        us=4,
    )(act, w)


def output_kernel(streams, meta_ref, x_ref, own_ref, other_ref, *refs):
    a_refs, b_refs, out_ref = refs[:streams], refs[streams : 2 * streams], refs[2 * streams]
    rows = x_ref.shape[1]
    place = meta_ref[META_TIER] * rows + lax.broadcasted_iota(jnp.int32, (rows, 1), 0)
    for stream in range(streams):
        ok = place < meta_ref[META_STREAMS + stream]
        attended = a_refs[stream][...].astype(WIDE) + b_refs[stream][...].astype(WIDE)
        hidden = x_ref[stream].astype(WIDE) + attended
        result = hidden + (own_ref[stream].astype(WIDE) + other_ref[stream].astype(WIDE))
        out_ref[stream] = jnp.where(ok, result, 0.0).astype(LOW)


def output_rows(chain, meta, x, own, other, a, b):
    args = (x, own, other, *a, *b)
    return chain.call(
        functools.partial(output_kernel, x.shape[0]),
        (1,),
        [scalars()] + [whole(v.shape) for v in args],
        whole(x.shape),
        shaped(x.shape),
        us=3,
    )(meta, *args)


def hidden_back_kernel(
    streams,
    meta_ref,
    x_ref,
    back_ref,
    back_other_ref,
    cot_ref,
    w_ref,
    gain_ref,
    *refs,
):
    lists, refs = refs[: 4 * streams], refs[4 * streams :]
    grad_hidden_ref, grad_merged_ref, grad_w_ref, vector_ref, w_acc, stats = refs[:6]
    stream = pl.program_id(0)
    rows = x_ref.shape[1]
    for place, scratch in enumerate(refs[6:]):
        pick(stream, lists[place * streams : (place + 1) * streams], scratch)
    a_ref, b_ref, merged_ref, total_ref = refs[6:]
    hidden = x_ref[0].astype(WIDE) + (a_ref[...].astype(WIDE) + b_ref[...].astype(WIDE))
    normed, inverse = norm_stats(hidden)
    place = meta_ref[META_TIER] * rows + lax.broadcasted_iota(jnp.int32, (rows, 1), 0)
    ok = place < meta_ref[META_STREAMS + stream]
    back = back_ref[0].astype(WIDE) + back_other_ref[0].astype(WIDE)
    grad_out = jnp.where(ok, cot_ref[0].astype(WIDE), 0.0)
    grad_hidden = grad_out + norm_back(back, normed, inverse, gain_ref[...])
    grad_hidden_ref[0] = grad_hidden
    low = grad_hidden.astype(LOW)
    merged = merged_ref[...]
    grad_merged = dot(low, w_ref[...], NT).astype(LOW)
    grad_merged_ref[0, :rows, :] = grad_merged
    heads = merged.shape[1] // HD
    stats[:heads, :] = total_ref[...]
    product = grad_merged.astype(WIDE) * merged.astype(WIDE)
    for head in range(heads):
        turned = product[:, head * HD : (head + 1) * HD].T
        stats[heads + head : heads + head + 1, :] = jnp.sum(turned, axis=0, keepdims=True)
    put_packed(grad_merged_ref.at[0], rows, stats[...])
    grad_w = dot(merged, low, TN)
    gain_part = jnp.sum(back * normed, axis=0, keepdims=True)
    bias_part = jnp.sum(back, axis=0, keepdims=True)

    @pl.when(stream == 0)
    def _():
        w_acc[...] = grad_w
        vector_ref[0:1, :] = gain_part
        vector_ref[1:2, :] = bias_part

    @pl.when(stream != 0)
    def _():
        w_acc[...] += grad_w
        vector_ref[0:1, :] += gain_part
        vector_ref[1:2, :] += bias_part

    @pl.when(stream == pl.num_programs(0) - 1)
    def _():
        grad_w_ref[...] = w_acc[...].astype(LOW)


def hidden_back(chain, meta, x, a, b, back, back_other, cot, merged, total, w, gain):
    streams, rows, width = x.shape
    features = w.shape[0]
    heads = features // HD
    outs = [
        shaped(x.shape, WIDE),
        shaped((streams, rows + packed_rows(2 * heads), features)),
        shaped(w.shape),
        shaped((2, width), WIDE),
    ]
    streamed = (x, back, back_other, cot)
    lists = (*a, *b, *merged, *total)
    return chain.call(
        functools.partial(hidden_back_kernel, streams),
        (streams,),
        [scalars()]
        + [per_stream(v.shape) for v in streamed]
        + [whole(v.shape) for v in (w, gain, *lists)],
        [per_stream(o.shape) for o in outs[:2]] + [whole(o.shape) for o in outs[2:]],
        outs,
        scratch=[
            pltpu.VMEM(w.shape, WIDE),
            pltpu.VMEM((2 * heads, rows), WIDE),
            pltpu.VMEM((rows, width), LOW),
            pltpu.VMEM((rows, width), LOW),
            pltpu.VMEM((rows, features), LOW),
            pltpu.VMEM((heads, rows), WIDE),
        ],
        us=6.5,
        vmem=VMEM_WIDE,
    )(meta, *streamed, w, gain, *lists)


def attend_back_kernel(own, streams, meta_ref, gm_ref, km_ref, vm_ref, ks_ref, vs_ref, *refs):
    *refs, q_ref = refs
    pick(pl.program_id(0), refs[: streams], q_ref)
    refs = refs[streams :]
    if own:
        gq_ref, gkm_ref, gvm_ref, gks_ref, gvs_ref = refs
        before = None
    else:
        before, (gq_ref, gkm_ref, gvm_ref, gks_ref, gvs_ref) = refs[:4], refs[4:]
    stream = pl.program_id(0)
    slots, rows = km_ref.shape[1], q_ref.shape[0]
    heads = q_ref.shape[1] // HD
    stats = get_packed(gm_ref.at[0], rows, 2 * heads, rows)

    def put(ref, index, cols, value):
        if before is not None:
            value = value + before[index][0, :, cols]
        ref[0, :, cols] = value.astype(ref.dtype)

    def body(with_segment):
        memory_ok, segment_ok = slot_masks(own, meta_ref, stream, streams, slots, rows)
        for head in range(heads):
            cols = slice(head * HD, (head + 1) * HD)
            query = q_ref[:, cols]
            grad = gm_ref[0, :rows, cols]
            total = stats[head : head + 1, :]
            delta = stats[heads + head : heads + head + 1, :]

            def tier(key, value, ok):
                scores = jnp.where(ok, dot(key, query, NT) * (SCALE * LOG2E), NEG)
                weights = jnp.exp2(scores - total)
                grad_scores = (weights * (dot(value, grad, NT) - delta)).astype(LOW)
                return (
                    dot(key, grad_scores, TN),
                    dot(grad_scores, query) * SCALE,
                    dot(weights.astype(LOW), grad),
                )

            turned, grad_key, grad_value = tier(km_ref[0, :, cols], vm_ref[0, :, cols], memory_ok)
            put(gkm_ref, 0, cols, grad_key)
            put(gvm_ref, 1, cols, grad_value)
            if with_segment:
                more, grad_key, grad_value = tier(
                    ks_ref[0, :, cols], vs_ref[0, :, cols], segment_ok
                )
                turned = turned + more
                put(gks_ref, 2, cols, grad_key)
                put(gvs_ref, 3, cols, grad_value)
            else:
                gks_ref[0, :, cols] = before[2][0, :, cols].astype(gks_ref.dtype)
                gvs_ref[0, :, cols] = before[3][0, :, cols].astype(gvs_ref.dtype)
            gq_ref[0, :, cols] = (turned * SCALE).T.astype(LOW)

    by_tier(own, meta_ref, body)


def attend_back(chain, own, meta, queries, gm, km, vm, ks, vs, before=()):
    streams = len(queries)
    rows, features = queries[0].shape
    kind = WIDE if own else LOW
    outs = [shaped((streams, rows, features))] + [shaped(a.shape, kind) for a in (km, vm, ks, vs)]
    return chain.call(
        functools.partial(attend_back_kernel, own, streams),
        (streams,),
        [scalars()]
        + [per_stream(a.shape) for a in (gm, km, vm, ks, vs)]
        + [whole(q.shape) for q in queries]
        + [per_stream(a.shape) for a in before],
        [per_stream(o.shape) for o in outs],
        outs,
        scratch=[pltpu.VMEM((rows, features), LOW)],
        us=10,
        vmem=VMEM_WIDE,
    )(meta, gm, km, vm, ks, vs, *queries, *before)


def column_of(row):
    return jnp.broadcast_to(row, (HD, row.shape[1])).T[:, 0:1]


def row_of(column):
    return jnp.broadcast_to(column, (column.shape[0], HD)).T[0:1, :]


def key_value_kernel_back(
    bits, meta_ref, unit_ref, stored_ref, gks_ref, gvs_ref, gkm_ref, gvm_ref,
    wk_ref, wv_ref, gain_ref, bias_ref, column_ref, sent_ref, kept_ref, k_acc, v_acc, sums
):
    stream = pl.program_id(0)
    width, features = wk_ref.shape

    @pl.when(stream == 0)
    def _():
        k_acc[...] = jnp.zeros_like(k_acc)
        v_acc[...] = jnp.zeros_like(v_acc)
        sums[...] = jnp.zeros_like(sums)

    unit, stored = unit_ref[0].T, stored_ref[0].T
    gks, gvs, gkm, gvm = gks_ref[0], gvs_ref[0], gkm_ref[0], gvm_ref[0]
    k_acc[...] += dot(unit, gks) + dot(stored, gkm)
    v_acc[...] += dot(unit, gvs) + dot(stored, gvm)
    for place, pair in enumerate(((gks, gkm), (gvs, gvm))):
        for piece in pair:
            sums[place : place + 1, :] += jnp.sum(piece.astype(WIDE), axis=0, keepdims=True)

    @pl.when(stream == pl.num_programs(0) - 1)
    def _():
        wk, wv = wk_ref[...].astype(WIDE), wv_ref[...].astype(WIDE)
        column_ref[0:1, :] = row_of(jnp.sum(wk * k_acc[...] + wv * v_acc[...], axis=1, keepdims=True))
        column_ref[1:2, :] = row_of(
            jnp.sum(wk * sums[0:1, :] + wv * sums[1:2, :], axis=1, keepdims=True)
        )
        gain, bias = column_of(gain_ref[...]), column_of(bias_ref[...])
        k_acc[...] = gain * k_acc[...] + bias * sums[0:1, :]
        v_acc[...] = gain * v_acc[...] + bias * sums[1:2, :]
        half = width // 2
        side = pair_side(meta_ref, bits)
        for ref, which in ((sent_ref, 1 - side), (kept_ref, side)):
            rows = pl.ds(pl.multiple_of(which * half, half), half)
            ref[:, :features] = k_acc[rows, :].astype(LOW)
            ref[:, features:] = v_acc[rows, :].astype(LOW)


def key_value_grads(chain, orders, meta, streamed, fixed):
    width, features = fixed[0].shape
    outs = [shaped((2, width), WIDE)] + [shaped((width // 2, 2 * features))] * 2
    acc = pltpu.VMEM((width, features), WIDE)
    return chain.call(
        functools.partial(key_value_kernel_back, tuple(order[0] for order in orders)),
        (streamed[0].shape[0],),
        [scalars()] + [per_stream(v.shape) for v in streamed] + [whole(v.shape) for v in fixed],
        [whole(o.shape) for o in outs],
        outs,
        scratch=[acc, acc, pltpu.VMEM((2, features), WIDE)],
        vmem=VMEM_WIDE,
        us=10,
    )(meta, *streamed, *fixed)


def query_kernel_back(
    bits, meta_ref, unit_ref, own_ref, came_ref, gks_ref, gvs_ref,
    wq_ref, wk_ref, wv_ref, gwo_ref, gain_ref, bias_ref, column_ref, vector_ref, normed_ref,
    sent_ref, kept_ref, q_acc, sums
):
    stream = pl.program_id(0)
    width, features = wq_ref.shape

    @pl.when(stream == 0)
    def _():
        q_acc[...] = jnp.zeros_like(q_acc)
        sums[...] = jnp.zeros_like(sums)

    grad = (own_ref[0].astype(WIDE) + came_ref[0].astype(WIDE)).astype(LOW)
    q_acc[...] += dot(unit_ref[0], grad, TN)
    sums[...] += jnp.sum(grad.astype(WIDE), axis=0, keepdims=True)
    normed_ref[0] = (
        dot(grad, wq_ref[...], NT) + dot(gks_ref[0], wk_ref[...], NT) + dot(gvs_ref[0], wv_ref[...], NT)
    ).astype(LOW)

    @pl.when(stream == pl.num_programs(0) - 1)
    def _():
        wq = wq_ref[...].astype(WIDE)
        gain_part = row_of(jnp.sum(wq * q_acc[...], axis=1, keepdims=True))
        bias_part = row_of(jnp.sum(wq * sums[...], axis=1, keepdims=True))
        gain, bias = column_of(gain_ref[...]), column_of(bias_ref[...])
        query = (gain * q_acc[...] + bias * sums[...]).astype(LOW)
        half = width // 2
        extra = sent_ref.shape[0] - half

        def put(out_ref, query_ref):
            out_ref[:half, :] = gwo_ref[...]
            out_ref[half:, :] = jnp.zeros((extra, width), LOW)
            out_ref[half : half + 1, :] = (column_ref[0:1, :] + gain_part).astype(LOW)
            out_ref[half + 1 : half + 2, :] = (column_ref[1:2, :] + bias_part).astype(LOW)
            out_ref[half + 2 : half + 4, :] = (0.5 * vector_ref[...]).astype(LOW)
            query_ref[:half, :features] = query[:half]
            query_ref[:half, features:] = query[half:]
            query_ref[half:, :] = jnp.zeros((extra, width), LOW)

        side = pair_side(meta_ref, bits)

        @pl.when(side == 0)
        def _():
            put(kept_ref, sent_ref)

        @pl.when(side != 0)
        def _():
            put(sent_ref, kept_ref)


def query_grads(chain, orders, meta, streamed, fixed):
    width, features = fixed[0].shape
    unit = streamed[0]
    outs = [shaped(unit.shape)]
    outs += [shaped((width // 2 + EXTRA, 2 * features))] * 2
    return chain.call(
        functools.partial(query_kernel_back, tuple(order[0] for order in orders)),
        (unit.shape[0],),
        [scalars()] + [per_stream(v.shape) for v in streamed] + [whole(v.shape) for v in fixed],
        [per_stream(unit.shape)] + [whole(o.shape) for o in outs[1:]],
        outs,
        scratch=[pltpu.VMEM((width, features), WIDE), pltpu.VMEM((1, features), WIDE)],
        vmem=VMEM_WIDE,
        us=9,
    )(meta, *streamed, *fixed)


def input_back_kernel(x_ref, own_ref, other_ref, hidden_ref, gain_ref, out_ref):
    normed, inverse = norm_stats(x_ref[0].astype(WIDE))
    grad = own_ref[0].astype(WIDE) + other_ref[0].astype(WIDE)
    out_ref[0] = (hidden_ref[0] + norm_back(grad, normed, inverse, gain_ref[...])).astype(LOW)


def input_back(chain, x, own, other, grad_hidden, gain):
    streamed = (x, own, other, grad_hidden)
    return chain.call(
        input_back_kernel,
        (x.shape[0],),
        [per_stream(v.shape) for v in streamed] + [whole(gain.shape)],
        per_stream(x.shape),
        shaped(x.shape),
        us=4,
    )(*streamed, gain)


def compress_kernel(bits, meta_ref, memory_ref, came_ref, rest_ref, w_ref, cot_ref, out_ref, *refs):
    sent_ref, kept_ref, acc, grads = refs
    stream = pl.program_id(0)
    streams = pl.num_programs(0)
    head = meta_ref[META_HEAD]
    mine = meta_ref[META_TIER] == 0
    slots, part = came_ref.shape[1], came_ref.shape[2]
    count = out_ref.shape[1]
    place = lax.broadcasted_iota(jnp.int32, (count, slots), 0)
    slot = lax.broadcasted_iota(jnp.int32, (count, slots), 1)
    length = meta_ref[META_STREAMS + stream]
    filled = jnp.where(mine, meta_ref[META_STREAMS + streams + stream], slots)
    ok = lax.broadcasted_iota(jnp.int32, (count, 1), 0) < lax.div(length, jnp.int32(RATE))
    cot = jnp.where(ok, cot_ref[0].astype(WIDE), 0.0).astype(LOW)

    @pl.when(stream == 0)
    def _():
        acc[...] = jnp.zeros_like(acc)

    picks = []
    for shift in range(RATE):
        chosen = (slot == place * RATE + shift) & (slot < filled)
        picks.append(jnp.where(chosen, 1.0, 0.0).astype(LOW))
    result = jnp.zeros(out_ref.shape[1:], WIDE)
    for ref, side in ((came_ref, head), (rest_ref, 1 - head)):
        start = pl.multiple_of(side * part, part)
        stored = jnp.where(mine, memory_ref[0, 0, :, pl.ds(start, part)].astype(WIDE), ref[0].astype(WIDE))
        stored = stored.astype(LOW)
        for shift in range(RATE):
            rows = dot(picks[shift], stored).astype(LOW)
            result = result + dot(rows, w_ref[shift, pl.ds(start, part), :])
            acc[shift, pl.ds(start, part), :] += dot(rows, cot, TN)
    out_ref[0] = jnp.where(ok, result, 0.0).astype(LOW)

    @pl.when(stream == streams - 1)
    def _():
        width = w_ref.shape[1]
        for shift in range(RATE):
            grads[shift * width : (shift + 1) * width, :] = acc[shift].astype(LOW)
        half = sent_ref.shape[0]
        side = pair_side(meta_ref, bits)
        for ref, which in ((sent_ref, 1 - side), (kept_ref, side)):
            ref[...] = grads[pl.ds(pl.multiple_of(which * half, half), half), :]


def compress(chain, orders, meta, memories, came, rest, w, cot):
    flat = (w.shape[0] * w.shape[1], w.shape[2])
    outs = [shaped(cot.shape)] + [shaped((flat[0] // 2, flat[1]))] * 2
    bits = tuple(order[0] for order in orders)
    return chain.call(
        functools.partial(compress_kernel, bits),
        (cot.shape[0],),
        [scalars()]
        + [per_stream(v.shape) for v in (memories, came, rest)]
        + [whole(w.shape), per_stream(cot.shape)],
        [per_stream(cot.shape)] + [whole(o.shape) for o in outs[1:]],
        outs,
        scratch=[pltpu.VMEM(w.shape, WIDE), pltpu.VMEM(flat, LOW)],
        us=5,
    )(meta, memories, came, rest, w, cot)


def bits_of():
    size = lax.axis_size("dp")
    bits = [("tier", 1)]
    step = 1
    while step < size:
        bits.append(("dp", step))
        step *= 2
    return bits


def swap(value, bit):
    axis, step = bit
    return lax.ppermute(value, axis, [(i, i ^ step) for i in range(lax.axis_size(axis))])


def swap_head(value):
    return swap(value, ("head", 1))


def swap_tier(value):
    return swap(value, ("tier", 1))


def swap_pair(value, bits):
    axes = ("dp", "tier", "head")
    sizes = [lax.axis_size(axis) for axis in axes]
    pairs = []
    for dp in range(sizes[0]):
        for tier in range(sizes[1]):
            for head in range(sizes[2]):
                axis, step = bits[head]
                to_dp = dp ^ step if axis == "dp" else dp
                to_tier = tier ^ step if axis == "tier" else tier
                pairs.append(
                    (
                        (dp * sizes[1] + tier) * sizes[2] + head,
                        (to_dp * sizes[1] + to_tier) * sizes[2] + head,
                    )
                )
    return lax.ppermute(value, axes, pairs)


def total_of(first, second):
    return (first.astype(WIDE) + second.astype(WIDE)).astype(LOW)


def scatter_kernel(bits, meta_ref, kept, came, *refs):
    half = kept.shape[0] // 2
    side = pair_side(meta_ref, bits)
    for ref, which in zip(refs, (1 - side, side)):
        rows = pl.ds(pl.multiple_of(which * half, half), half)
        ref[...] = total_of(kept[rows, :], came[rows, :])


def add_kernel(bits, meta_ref, kept, came, *refs):
    refs[0][...] = total_of(kept[...], came[...])


def gather_kernel(bits, meta_ref, held, came, *refs):
    half = held.shape[0]
    side = pair_side(meta_ref, bits)
    refs[0][pl.ds(pl.multiple_of(side * half, half), half), :] = held[...]
    refs[0][pl.ds(pl.multiple_of((1 - side) * half, half), half), :] = came[...]


class Reduce:
    def __init__(self, chain, meta, orders, sent, kept):
        self.chain, self.meta, self.orders = chain, meta, orders
        self.stages = len(orders[0])
        self.depth = min(3, self.stages - 1)
        self.kept = kept
        self.stage = 0
        self.send(sent, 0)

    def bits(self, level):
        return tuple(order[level] for order in self.orders)

    def send(self, array, level):
        self.came = swap_pair(array, self.bits(level))

    def run(self, kernel, level, outs):
        return self.chain.call(
            functools.partial(kernel, self.bits(level)),
            (1,),
            [scalars(), whole(self.kept.shape), whole(self.came.shape)],
            [whole(o.shape) for o in outs],
            outs,
            vmem=8,
        )(self.meta, self.kept, self.came)

    def ready(self):
        return self.stage >= self.stages + self.depth - 1

    def step(self):
        depth, stage, stages = self.depth, self.stage, self.stages
        self.stage += 1
        rows, width = self.kept.shape
        if stage < depth - 1:
            sent, self.kept = self.run(
                scatter_kernel, stage + 1, [shaped((rows // 2, width))] * 2
            )
            self.send(sent, stage + 1)
        elif stage < stages:
            (self.kept,) = self.run(add_kernel, stage, [shaped((rows, width))])
            self.send(self.kept, stage + 1 if stage + 1 < stages else depth - 1)
        else:
            level = depth - 1 - (stage - stages)
            (self.kept,) = self.run(gather_kernel, level, [shaped((2 * rows, width))])
            self.send(self.kept, level - 1)


def finish_kernel(bits, write, carried, meta_ref, held, came, *refs):
    write(pair_side(meta_ref, bits), held, came, refs[carried:])


def finish(group, write, out_shapes, out_specs, carried=()):
    args = [group.meta, group.kept, group.came, *carried]
    count = len(carried)
    return group.chain.call(
        functools.partial(finish_kernel, group.bits(0), write, count),
        (1,),
        [scalars(), whole(group.kept.shape), whole(group.came.shape)] + [any_spec()] * count,
        out_specs,
        out_shapes,
        vmem=24,
        alias={3 + i: i for i in range(count)},
        us=3,
    )(*args)


def write_rows(side, held, came, outs):
    half = held.shape[0]
    for ref, which in ((held, side), (came, 1 - side)):
        outs[0][pl.ds(pl.multiple_of(which * half, half), half), :] = ref[...].astype(WIDE)


def finish_ffn(group, part, out_shape, in_shape, carried=()):
    specs = [
        pl.BlockSpec((out_shape[0] // 2, out_shape[1]), lambda i: (part, 0)),
        pl.BlockSpec((in_shape[0], in_shape[1] // 2), lambda i: (0, part)),
    ]

    def write(side, held, came, outs):
        for out_ref, in_ref, which in ((held, came, 0), (came, held, 1)):

            @pl.when(side == which)
            def _():
                outs[0][...] = out_ref[...].astype(WIDE)
                outs[1][...] = in_ref[...].astype(WIDE)

    return finish(group, write, [shaped(out_shape, WIDE), shaped(in_shape, WIDE)], specs, carried)


def finish_key_value(group, width, features):
    shapes = [shaped((width, features), WIDE)] * 2

    def write(side, held, came, outs):
        half = held.shape[0]
        for ref, which in ((held, side), (came, 1 - side)):
            rows = pl.ds(pl.multiple_of(which * half, half), half)
            outs[0][rows, :] = ref[:, :features].astype(WIDE)
            outs[1][rows, :] = ref[:, features:].astype(WIDE)

    return finish(group, write, shapes, [whole_block(v.shape) for v in shapes])


def finish_out_query(group, width, features):
    shapes = [shaped((features, width), WIDE), shaped((width, features), WIDE), shaped((16, width))]

    def write(side, held, came, outs):
        def put(out_ref, query_ref):
            half = outs[0].shape[0]
            outs[0][...] = out_ref[:half, :].astype(WIDE)
            outs[1][:half, :] = query_ref[:half, :features].astype(WIDE)
            outs[1][half:, :] = query_ref[:half, features:].astype(WIDE)
            outs[2][...] = out_ref[half : half + 16, :]

        @pl.when(side == 0)
        def _():
            put(held, came)

        @pl.when(side != 0)
        def _():
            put(came, held)

    return finish(
        group, write, shapes, [whole_block(v.shape) for v in shapes[:2]] + [whole(shapes[2].shape)]
    )


def finish_compress(group, shape):
    flat = (shape[0] * shape[1], shape[2])
    return finish(group, write_rows, [shaped(flat, WIDE)], [whole_block(flat)])[0].reshape(shape)


def on_device(
    inputs,
    memories,
    seg_len,
    mem_count,
    w_query,
    w_key,
    w_value,
    w_attn_out,
    w_ffn_in,
    w_ffn_out,
    w_compress,
    gain_attn,
    bias_attn,
    gain_ffn,
    bias_ffn,
    cotan_output,
    cotan_compressed,
):
    tier_index = lax.axis_index("tier")
    streams, rows, width = inputs.shape
    features = w_query.shape[1]
    hidden_units = w_ffn_in.shape[1]
    counts = mem_count[:, 0]
    place = jnp.stack([tier_index, lax.axis_index("head"), lax.axis_index("dp")])
    meta = jnp.concatenate([place, seg_len, counts], 0).astype(jnp.int32)
    gain_row, bias_row = gain_attn[None], bias_attn[None]
    gain_second, bias_second = gain_ffn[None], bias_ffn[None]
    chain = Chain()

    unit, low, queries = query_rows(chain, meta, inputs, gain_row, bias_row, w_query)
    queries_other = [swap_tier(q) for q in queries]
    keys, values = key_values(chain, low, w_key, w_value)
    stored, memory_keys, memory_values = stored_rows(
        chain, memories, gain_row, bias_row, w_key, w_value
    )
    tiers = (memory_keys, memory_values, keys, values)
    own, came = [], []
    for stream in range(streams):
        came.append(swap_tier(attend(chain, False, stream, meta, queries_other[stream], *tiers)))
        own.append(attend(chain, True, stream, meta, queries[stream], *tiers))
    got = {}
    merged, totals, attended, attended_other = [], [], [], []
    for stream in range(streams):
        low, total, part = merge(chain, rows, own[stream], came[stream], w_attn_out)
        merged.append(low)
        totals.append(total)
        attended.append(part)
        attended_other.append(swap_head(part))
    got["evicted"] = lax.ppermute(evicted_rows(chain, meta, memories), "tier", [(0, 1)])

    tier, low_bit, *more = bits_of()
    high_bit, far_bit, more = more[0], more[1], more[2:]
    axes = {"x": tier, "y": low_bit, "z": high_bit, "w": far_bit}
    orders = {}
    for name, paths in PATHS.items():
        rest = "yzw" if name == "compress" else "xyzw"
        orders[name] = tuple(
            tuple(axes[axis] for axis in dict.fromkeys(path + rest)) + tuple(more)
            for path in paths.split("/")
        )
    flat = (streams * rows, width)
    hidden_args = (
        inputs.reshape(flat),
        cotan_output.reshape(flat),
        gain_second,
        bias_second,
        *attended,
        *attended_other,
    )
    groups = {}

    def begin(name, sent, kept):
        groups[name] = Reduce(chain, meta, orders[name], sent, kept)

    def run_ffn():
        names = ("f1", "f2")
        got["act"], got["lifted"], *parts = ffn(
            chain, streams, [orders[name] for name in names], meta, hidden_args, w_ffn_in, w_ffn_out
        )
        for place, name in enumerate(names):
            begin(name, *parts[2 * place : 2 * place + 2])

    def run_back():
        got["back"] = ffn_back(chain, got["lifted"], w_ffn_in).reshape(inputs.shape)
        got["back_other"] = swap_head(got["back"])

    def run_ffn3():
        got["ffn"] = ffn_out(chain, got["act"], w_ffn_out).reshape(inputs.shape)
        got["ffn_other"] = swap_head(got["ffn"])

    def run_hidden():
        got["hidden"], got["gm"], got["gwo"], vectors_ffn = hidden_back(
            chain, meta, inputs, attended, attended_other, got["back"], got["back_other"],
            cotan_output, merged, totals, w_attn_out, gain_second,
        )
        got["gm_other"] = swap_tier(got["gm"])
        got["vectors"] = vectors_ffn

    def run_own():
        got["own"], *got["sums"] = attend_back(chain, True, meta, queries, got["gm"], *tiers)

    def run_other():
        got["other"], *got["grads"] = attend_back(
            chain, False, meta, queries_other, got["gm_other"], *tiers,
            before=tuple(got["sums"]),
        )
        got["came"] = swap_tier(got["other"])

    def run_output():
        got["output"] = output_rows(
            chain, meta, inputs, got["ffn"], got["ffn_other"], attended, attended_other
        )

    def run_grads():
        grad_km, grad_vm, grad_ks, grad_vs = got["grads"]
        got["column"], *parts = key_value_grads(
            chain, orders["kv"], meta, (unit, stored, grad_ks, grad_vs, grad_km, grad_vm),
            (w_key, w_value, gain_row, bias_row),
        )
        begin("kv", *parts)

    def run_query():
        _, _, grad_ks, grad_vs = got["grads"]
        got["normed"], *parts = query_grads(
            chain, orders["oq"], meta, (unit, got["own"], got["came"], grad_ks, grad_vs),
            (
                w_query, w_key, w_value, got["gwo"], gain_row, bias_row,
                got["column"], got["vectors"],
            ),
        )
        got["normed_other"] = swap_head(got["normed"])
        begin("oq", *parts)

    def run_evict2():
        got["evicted"] = copied(chain, got["evicted"])
        got["evicted_other"] = swap_head(got["evicted"])

    def run_evict3():
        got["evicted_other"] = copied(chain, got["evicted_other"])

    def run_input():
        got["grad_inputs"] = input_back(
            chain, inputs, got["normed"], got["normed_other"], got["hidden"], gain_row
        )

    def run_compress():
        got["compressed"], *parts = compress(
            chain, orders["compress"], meta, memories, got["evicted"], got["evicted_other"],
            w_compress, cotan_compressed,
        )
        begin("compress", *parts)

    def end(name):
        group = groups.pop(name)
        out_shape, in_shape = w_ffn_out.shape, w_ffn_in.shape
        if name == "f1":
            got["ffn_grads"] = finish_ffn(group, 0, out_shape, in_shape)
        elif name == "f2":
            got["ffn_grads"] = finish_ffn(group, 1, out_shape, in_shape, got["ffn_grads"])
        elif name == "kv":
            got["kv"] = finish_key_value(group, width, features)
        elif name == "oq":
            got["oq"] = finish_out_query(group, width, features)
            got["vector"] = got["oq"][2]
        else:
            got["compress"] = finish_compress(group, w_compress.shape)

    runs = {
        "ffn": run_ffn, "back": run_back, "ffn3": run_ffn3, "hidden": run_hidden, "own": run_own,
        "other": run_other, "output": run_output, "grads": run_grads, "query": run_query,
        "evict2": run_evict2, "evict3": run_evict3, "input": run_input, "compr": run_compress, "pause": lambda: pause(chain),
    }
    chain.cost = COST
    for name in ORDER:
        if name in runs:
            runs[name]()
        elif name in groups and groups[name].ready():
            end(name)
        elif name in groups:
            groups[name].step()
    while groups:
        for name in list(groups):
            if groups[name].ready():
                end(name)
            else:
                groups[name].step()
    vectors = got["vector"].astype(WIDE) + swap_head(got["vector"]).astype(WIDE)
    return (
        got["output"],
        got["compressed"],
        got["grad_inputs"],
        got["oq"][1],
        *got["kv"],
        got["oq"][0],
        got["ffn_grads"][1],
        got["ffn_grads"][0],
        got["compress"],
        vectors[0],
        vectors[1],
        vectors[2],
        vectors[3],
    )


def solution(mesh):
    return jax.shard_map(
        on_device,
        mesh=mesh,
        in_specs=(
            P("dp", "tier", None),
            P("dp", "tier", None, None),
            P("dp"),
            P("dp", "tier"),
            P(None, "head"),
            P(None, "head"),
            P(None, "head"),
            P("head", None),
            P(None, "head"),
            P("head", None),
            P(None, None, ("tier", "head")),
            P(),
            P(),
            P(),
            P(),
            P("dp", "tier", None),
            P("dp", None, ("tier", "head")),
        ),
        out_specs=(
            P("dp", "tier", None),
            P("dp", None, ("tier", "head")),
            P("dp", "tier", None),
            P(None, "head"),
            P(None, "head"),
            P(None, "head"),
            P("head", None),
            P(None, "head"),
            P("head", None),
            P(None, None, ("tier", "head")),
            P(),
            P(),
            P(),
            P(),
        ),
        check_vma=False,
    )
```

```python
import functools

import jax
import jax.numpy as jnp
from jax import lax
from jax.experimental import pallas as pl
from jax.experimental.pallas import tpu as pltpu
from jax.sharding import PartitionSpec as P

HD = 128
RATE = 3
EPS = 1e-05
NEG = -1000000000.0
LOG2E = 1.4426950408889634
SCALE = HD ** (-0.5)
GELU_ROOT = 0.7978845608028654
GELU_CUBE = 0.044715

ORDER = (
    "ffn", "back", "pause", "hidden", "evict2", "own", "evict3", "ffn3", "f1", "f2", "other",
    "output", "grads", "f1", "f2", "query", "f1", "f2", "kv", "input", "oq", "f1", "f2", "kv",
    "compr", "oq", "f1", "f2", "kv", "compress", "oq", "f1", "f2", "kv", "compress", "oq", "kv",
    "compress", "oq", "f1", "f2", "kv", "compress", "oq", "kv", "oq",
)

PATHS = {
    "f1": "yxw/zxy",
    "f2": "xwz/yzx",
    "kv": "zxy/xzy",
    "oq": "xyw/yzx",
    "compress": "yz/zy",
}

COST = 1e10
COST_EARLY = 1e8
PAUSE = 10
VMEM_FFN = 28
VMEM_WIDE = 22
EXTRA = 64

LOW = jnp.bfloat16
WIDE = jnp.float32
NN = (((1,), (0,)), ((), ()))
NT = (((1,), (1,)), ((), ()))
TN = (((0,), (0,)), ((), ()))


def dot(first, second, dims=NN):
    return lax.dot_general(first, second, dims, preferred_element_type=WIDE)


def norm_stats(values):
    centre = values - jnp.mean(values, axis=-1, keepdims=True)
    inverse = lax.rsqrt(jnp.mean(centre * centre, axis=-1, keepdims=True) + EPS)
    return (centre * inverse, inverse)


def norm_back(grad_normed, normed, inverse, gain_vector):
    scaled = grad_normed * gain_vector
    return inverse * (
        scaled
        - jnp.mean(scaled, axis=-1, keepdims=True)
        - normed * jnp.mean(scaled * normed, axis=-1, keepdims=True)
    )


def per_stream(array_shape):
    block = (1,) + tuple(array_shape[1:])
    zeros = (0,) * (len(block) - 1)
    return pl.BlockSpec(block, lambda s: (s,) + zeros)


def whole(array_shape):
    return pl.BlockSpec(memory_space=pltpu.VMEM)


def whole_block(array_shape):
    zeros = (0,) * len(array_shape)
    return pl.BlockSpec(tuple(array_shape), lambda *_: zeros)


def scalars():
    return pl.BlockSpec(memory_space=pltpu.SMEM)


def shaped(shape, dtype=LOW):
    return jax.ShapeDtypeStruct(tuple(shape), dtype)


class Chain:
    def __init__(self):
        self.last = None
        self.cost = COST_EARLY

    def call(self, kernel, grid, in_specs, out_specs, out_shape, scratch=(), vmem=16, alias=None, us=1.0):
        last = self.last
        count = len(in_specs)

        def ordered(*refs):
            kernel(*refs[:count], *refs[count + 1 :])

        def run(*args):
            specs = list(in_specs)
            args = list(args)
            body = kernel
            if last is not None:
                specs.append(pl.BlockSpec(memory_space=pl.ANY))
                args.append(last)
                body = ordered
            outs = pl.pallas_call(
                body,
                grid=grid,
                in_specs=specs,
                out_specs=out_specs,
                out_shape=out_shape,
                scratch_shapes=list(scratch),
                input_output_aliases=alias or {},
                compiler_params=pltpu.CompilerParams(vmem_limit_bytes=vmem * 1024 * 1024),
                cost_estimate=pl.CostEstimate(
                    flops=int(us * self.cost), bytes_accessed=0, transcendentals=0
                ),
            )(*args)
            if not alias:
                self.last = outs[0] if isinstance(outs, (list, tuple)) else outs
            return outs

        return run


META_TIER, META_HEAD, META_DP, META_STREAMS = 0, 1, 2, 3


def any_spec():
    return pl.BlockSpec(memory_space=pl.ANY)


def query_kernel(meta_ref, x_ref, gain_ref, bias_ref, w_ref, unit_ref, low_ref, *outs):
    for stream in range(x_ref.shape[0]):
        normed, _ = norm_stats(x_ref[stream].astype(WIDE))
        unit_ref[stream] = normed.astype(LOW)
        low = (normed * gain_ref[...] + bias_ref[...]).astype(LOW)
        low_ref[stream] = low
        outs[stream][...] = dot(low, w_ref[...]).astype(LOW)


def query_rows(chain, meta, x, gain, bias, w):
    streams, rows, width = x.shape
    outs = [shaped(x.shape), shaped(x.shape)]
    outs += [shaped((rows, w.shape[1]))] * streams
    unit, low, *queries = chain.call(
        query_kernel,
        (1,),
        [scalars()] + [whole(v.shape) for v in (x, gain, bias, w)],
        [whole(o.shape) for o in outs],
        outs,
        us=3,
    )(meta, x, gain, bias, w)
    return unit, low, queries


def key_value_kernel(low_ref, wk_ref, wv_ref, k_ref, v_ref):
    k_ref[0] = dot(low_ref[0], wk_ref[...]).astype(LOW)
    v_ref[0] = dot(low_ref[0], wv_ref[...]).astype(LOW)


def key_values(chain, low, wk, wv):
    outs = [shaped(low.shape[:2] + wk.shape[1:])] * 2
    return chain.call(
        key_value_kernel,
        (low.shape[0],),
        [per_stream(low.shape), whole(wk.shape), whole(wv.shape)],
        [per_stream(o.shape) for o in outs],
        outs,
        us=2.5,
    )(low, wk, wv)


def stored_kernel(x_ref, gain_ref, bias_ref, wk_ref, wv_ref, unit_ref, k_ref, v_ref):
    normed, _ = norm_stats(x_ref[0, 0].astype(WIDE))
    unit_ref[0] = normed.astype(LOW)
    low = (normed * gain_ref[...] + bias_ref[...]).astype(LOW)
    k_ref[0] = dot(low, wk_ref[...]).astype(LOW)
    v_ref[0] = dot(low, wv_ref[...]).astype(LOW)


def stored_rows(chain, x, gain, bias, wk, wv):
    streams, _, slots, width = x.shape
    outs = [shaped((streams, slots, width))] + [shaped((streams, slots, wk.shape[1]))] * 2
    return chain.call(
        stored_kernel,
        (streams,),
        [per_stream(x.shape)] + [whole(v.shape) for v in (gain, bias, wk, wv)],
        [per_stream(o.shape) for o in outs],
        outs,
        us=6,
    )(x, gain, bias, wk, wv)


def slot_masks(own, meta_ref, stream, streams, slots, rows):
    tier = meta_ref[META_TIER]
    length = meta_ref[META_STREAMS + stream]
    filled = meta_ref[META_STREAMS + streams + stream]
    memory_ok = lax.broadcasted_iota(jnp.int32, (slots, rows), 0) < filled
    key_row = lax.broadcasted_iota(jnp.int32, (rows, rows), 0)
    segment_ok = (tier * rows + key_row) < length
    if own:
        query_row = lax.broadcasted_iota(jnp.int32, (rows, rows), 1)
        segment_ok = segment_ok & (key_row <= query_row)
    return memory_ok, segment_ok


def by_tier(own, meta_ref, body):
    if own:
        body(True)
        return

    @pl.when(meta_ref[META_TIER] == 0)
    def _():
        body(True)

    @pl.when(meta_ref[META_TIER] != 0)
    def _():
        body(False)


def put_packed(ref, row, value):
    count, width = value.shape
    for part in range(3):
        low = value.astype(LOW)
        ref[row + part * count : row + (part + 1) * count, :width] = low
        value = value - low.astype(WIDE)


def get_packed(ref, row, count, width):
    parts = [
        ref[row + part * count : row + (part + 1) * count, :width].astype(WIDE) for part in range(3)
    ]
    return parts[0] + (parts[1] + parts[2])


def packed_rows(count):
    return -(-3 * count // 16) * 16


def attend_kernel(own, stream, streams, meta_ref, q_ref, km_ref, vm_ref, ks_ref, vs_ref, out_ref, totals):
    slots, rows = km_ref.shape[1], q_ref.shape[0]
    heads = q_ref.shape[1] // HD

    def body(with_segment):
        memory_ok, segment_ok = slot_masks(own, meta_ref, stream, streams, slots, rows)
        for head in range(heads):
            cols = slice(head * HD, (head + 1) * HD)
            query = q_ref[:, cols]
            scores = jnp.where(
                memory_ok, dot(km_ref[0, :, cols], query, NT) * (SCALE * LOG2E), NEG
            )
            top = jnp.max(scores, axis=0, keepdims=True)
            if with_segment:
                near = jnp.where(
                    segment_ok, dot(ks_ref[0, :, cols], query, NT) * (SCALE * LOG2E), NEG
                )
                top = jnp.maximum(top, jnp.max(near, axis=0, keepdims=True))
            raw = jnp.exp2(scores - top)
            spent = jnp.sum(raw, axis=0, keepdims=True)
            mixed = dot(vm_ref[0, :, cols], raw.astype(LOW), TN)
            if with_segment:
                raw_near = jnp.exp2(near - top)
                spent = spent + jnp.sum(raw_near, axis=0, keepdims=True)
                mixed = mixed + dot(vs_ref[0, :, cols], raw_near.astype(LOW), TN)
            out_ref[:rows, cols] = (mixed / spent).T.astype(LOW)
            totals[head : head + 1, :] = top + jnp.log2(spent)
        put_packed(out_ref, rows, totals[...])

    by_tier(own, meta_ref, body)


def one_stream(array, stream):
    return pl.BlockSpec((1,) + array.shape[1:], lambda i: (stream, 0, 0))


def attend(chain, own, stream, meta, q, km, vm, ks, vs):
    rows, features = q.shape
    heads = features // HD
    out = shaped((rows + packed_rows(heads), features))
    return chain.call(
        functools.partial(attend_kernel, own, stream, km.shape[0]),
        (1,),
        [scalars(), whole(q.shape)] + [one_stream(a, stream) for a in (km, vm, ks, vs)],
        whole(out.shape),
        out,
        scratch=[pltpu.VMEM((heads, rows), WIDE)],
        us=2.6,
    )(meta, q, km, vm, ks, vs)


def merge_kernel(w_ref, own_ref, other_ref, low_ref, total_ref, part_ref):
    rows, features = low_ref.shape
    heads = features // HD
    first = get_packed(own_ref, rows, heads, rows)
    second = get_packed(other_ref, rows, heads, rows)
    top = jnp.maximum(first, second)
    total = top + jnp.log2(jnp.exp2(first - top) + jnp.exp2(second - top))
    total_ref[...] = total
    share_own, share_other = jnp.exp2(first - total), jnp.exp2(second - total)
    for head in range(heads):
        cols = slice(head * HD, (head + 1) * HD)
        column_own = jnp.broadcast_to(share_own[head : head + 1], (HD, rows)).T
        column_other = jnp.broadcast_to(share_other[head : head + 1], (HD, rows)).T
        merged = (
            own_ref[:rows, cols].astype(WIDE) * column_own
            + other_ref[:rows, cols].astype(WIDE) * column_other
        )
        low_ref[:, cols] = merged.astype(LOW)
    part_ref[...] = dot(low_ref[...], w_ref[...]).astype(LOW)


def merge(chain, rows, own, other, w):
    features = own.shape[1]
    outs = [
        shaped((rows, features)),
        shaped((features // HD, rows), WIDE),
        shaped((rows, w.shape[1])),
    ]
    args = (w, own, other)
    return chain.call(
        merge_kernel,
        (1,),
        [whole(v.shape) for v in args],
        [whole(o.shape) for o in outs],
        outs,
        us=1.0,
    )(*args)


def evicted_kernel(streams, meta_ref, memory_ref, evicted_ref):
    part = evicted_ref.shape[2]
    start = pl.multiple_of(meta_ref[META_HEAD] * part, part)
    filled = meta_ref[META_STREAMS + streams + pl.program_id(0)]
    ok = lax.broadcasted_iota(jnp.int32, (evicted_ref.shape[1], 1), 0) < filled
    rows = memory_ref[0, 0, :, pl.ds(start, part)].astype(WIDE)
    evicted_ref[0] = jnp.where(ok, rows, 0.0).astype(LOW)


def evicted_rows(chain, meta, memories):
    streams, _, slots, width = memories.shape
    out = (streams, slots, width // 2)
    return chain.call(
        functools.partial(evicted_kernel, streams),
        (streams,),
        [scalars(), per_stream(memories.shape)],
        per_stream(out),
        shaped(out),
        us=2,
    )(meta, memories)


def pause_kernel(out_ref):
    out_ref[...] = jnp.zeros_like(out_ref)


def pause(chain):
    shape = shaped((8, HD), WIDE)
    return chain.call(pause_kernel, (1,), [], whole(shape.shape), shape, us=PAUSE)()


def copied_kernel(in_ref, out_ref):
    out_ref[...] = in_ref[...]


def copied(chain, array):
    return chain.call(
        copied_kernel, (1,), [whole(array.shape)], whole(array.shape), shaped(array.shape)
    )(array)


def pick(stream, refs, scratch):
    for place, ref in enumerate(refs):

        @pl.when(stream == place)
        def _():
            scratch[...] = ref[...]


def valid_rows(meta_ref, streams, rows):
    place = lax.broadcasted_iota(jnp.int32, (streams * rows, 1), 0)
    ok = None
    for stream in range(streams):
        inside = (
            (place >= stream * rows)
            & (place < stream * rows + meta_ref[META_STREAMS + stream] - meta_ref[META_TIER] * rows)
            & (place < (stream + 1) * rows)
        )
        ok = inside if ok is None else ok | inside
    return ok


def side_of(meta_ref, bit):
    axis, step = bit
    if axis == "tier":
        return meta_ref[META_TIER]
    return lax.rem(lax.div(meta_ref[META_DP], jnp.int32(step)), jnp.int32(2))


def pair_side(meta_ref, bits):
    first, second = (side_of(meta_ref, bit) for bit in bits)
    return jnp.where(meta_ref[META_HEAD] == 0, first, second)


def ffn_kernel(streams, bits, meta_ref, *refs):
    x_ref, cot_ref, gain_ref, bias_ref = refs[:4]
    a_refs, b_refs = refs[4 : 4 + streams], refs[4 + streams : 4 + 2 * streams]
    wi_ref, wo_ref, act_ref, lifted_ref, *refs = refs[4 + 2 * streams :]
    parts, (low_ref, turned_ref, grad_ref) = refs[:-3], refs[-3:]
    step = pl.program_id(0)
    units = wi_ref.shape[1]

    @pl.when(step == 0)
    def _():
        rows = x_ref.shape[0] // streams
        for stream in range(streams):
            own = slice(stream * rows, (stream + 1) * rows)
            attended = a_refs[stream][...].astype(WIDE) + b_refs[stream][...].astype(WIDE)
            normed, _ = norm_stats(x_ref[own, :].astype(WIDE) + attended)
            low = (normed * gain_ref[...] + bias_ref[...]).astype(LOW)
            low_ref[own, :] = low
            turned_ref[:, own] = low.T
        ok = valid_rows(meta_ref, streams, x_ref.shape[0] // streams)
        grad_ref[...] = jnp.where(ok, cot_ref[...].astype(WIDE), 0.0).astype(LOW)

    lifted = dot(low_ref[...], wi_ref[...])
    square = lifted * lifted
    bent = jnp.tanh(GELU_ROOT * lifted * (1.0 + GELU_CUBE * square))
    half = 0.5 * (1.0 + bent)
    activated = (lifted * half).astype(LOW)
    act_ref[...] = activated
    slope = half + 0.5 * lifted * (1.0 - bent * bent) * (
        GELU_ROOT * (1.0 + 3.0 * GELU_CUBE * square)
    )
    grad_out = dot(activated, grad_ref[...], TN).astype(LOW)
    grad_lifted = (slope * dot(grad_ref[...], wo_ref[...], NT)).astype(LOW)
    grad_in = dot(turned_ref[...], grad_lifted).astype(LOW)
    place = pl.multiple_of((step % 2) * units, units)
    for part in range(2):
        sent, kept = parts[2 * part : 2 * part + 2]
        side = pair_side(meta_ref, bits[part])
        for out_ref, in_ref, which in ((kept, sent, 0), (sent, kept, 1)):

            @pl.when((step // 2 == part) & (side == which))
            def _():
                out_ref[pl.ds(place, units), :] = grad_out
                in_ref[:, pl.ds(place, units)] = grad_in

    lifted_ref[...] = grad_lifted


def ffn(chain, streams, orders, meta, whole_args, w_in, w_out):
    rows, width = whole_args[0].shape
    units = w_in.shape[1]
    steps = 4
    block = units // steps
    outs = [shaped((rows, units))] * 2
    parts = [shaped((units // 2, width))] * 4
    turned = pltpu.VMEM((width, rows), LOW)
    return chain.call(
        functools.partial(ffn_kernel, streams, tuple((p[0][0], p[1][0]) for p in orders)),
        (steps,),
        [scalars()]
        + [whole(v.shape) for v in whole_args]
        + [
            pl.BlockSpec((width, block), lambda j: (0, j)),
            pl.BlockSpec((block, width), lambda j: (j, 0)),
        ],
        [pl.BlockSpec((rows, block), lambda j: (0, j))] * 2 + [whole(o.shape) for o in parts],
        outs + parts,
        scratch=[
            pltpu.VMEM((rows, width), LOW),
            turned,
            pltpu.VMEM((rows, width), LOW),
        ],
        vmem=VMEM_FFN,
        us=24,
    )(meta, *whole_args, w_in, w_out)


def ffn_back_kernel(grad_ref, w_ref, out_ref, acc):
    step = pl.program_id(0)
    more = dot(grad_ref[...], w_ref[...], NT)

    @pl.when(step == 0)
    def _():
        acc[...] = more

    @pl.when(step != 0)
    def _():
        acc[...] += more

    @pl.when(step == pl.num_programs(0) - 1)
    def _():
        out_ref[...] = acc[...].astype(LOW)


def ffn_back(chain, grad, w):
    rows, units = grad.shape
    width = w.shape[0]
    steps = 2
    block = units // steps
    return chain.call(
        ffn_back_kernel,
        (steps,),
        [pl.BlockSpec((rows, block), lambda j: (0, j)), pl.BlockSpec((width, block), lambda j: (0, j))],
        whole((rows, width)),
        shaped((rows, width)),
        scratch=[pltpu.VMEM((rows, width), WIDE)],
        vmem=24,
        us=5,
    )(grad, w)


def ffn_out_kernel(act_ref, w_ref, out_ref, acc):
    step = pl.program_id(0)
    more = dot(act_ref[...], w_ref[...])

    @pl.when(step == 0)
    def _():
        acc[...] = more

    @pl.when(step != 0)
    def _():
        acc[...] += more

    @pl.when(step == pl.num_programs(0) - 1)
    def _():
        out_ref[...] = acc[...].astype(LOW)


def ffn_out(chain, act, w):
    rows, units = act.shape
    width = w.shape[1]
    steps = 4
    block = units // steps
    return chain.call(
        ffn_out_kernel,
        (steps,),
        [pl.BlockSpec((rows, block), lambda j: (0, j)), pl.BlockSpec((block, width), lambda j: (j, 0))],
        whole((rows, width)),
        shaped((rows, width)),
        scratch=[pltpu.VMEM((rows, width), WIDE)],
        us=4,
    )(act, w)


def output_kernel(streams, meta_ref, x_ref, own_ref, other_ref, *refs):
    a_refs, b_refs, out_ref = refs[:streams], refs[streams : 2 * streams], refs[2 * streams]
    rows = x_ref.shape[1]
    place = meta_ref[META_TIER] * rows + lax.broadcasted_iota(jnp.int32, (rows, 1), 0)
    for stream in range(streams):
        ok = place < meta_ref[META_STREAMS + stream]
        attended = a_refs[stream][...].astype(WIDE) + b_refs[stream][...].astype(WIDE)
        hidden = x_ref[stream].astype(WIDE) + attended
        result = hidden + (own_ref[stream].astype(WIDE) + other_ref[stream].astype(WIDE))
        out_ref[stream] = jnp.where(ok, result, 0.0).astype(LOW)


def output_rows(chain, meta, x, own, other, a, b):
    args = (x, own, other, *a, *b)
    return chain.call(
        functools.partial(output_kernel, x.shape[0]),
        (1,),
        [scalars()] + [whole(v.shape) for v in args],
        whole(x.shape),
        shaped(x.shape),
        us=3,
    )(meta, *args)


def hidden_back_kernel(
    streams,
    meta_ref,
    x_ref,
    back_ref,
    back_other_ref,
    cot_ref,
    w_ref,
    gain_ref,
    *refs,
):
    lists, refs = refs[: 4 * streams], refs[4 * streams :]
    grad_hidden_ref, grad_merged_ref, grad_w_ref, vector_ref, w_acc, stats = refs[:6]
    stream = pl.program_id(0)
    rows = x_ref.shape[1]
    for place, scratch in enumerate(refs[6:]):
        pick(stream, lists[place * streams : (place + 1) * streams], scratch)
    a_ref, b_ref, merged_ref, total_ref = refs[6:]
    hidden = x_ref[0].astype(WIDE) + (a_ref[...].astype(WIDE) + b_ref[...].astype(WIDE))
    normed, inverse = norm_stats(hidden)
    place = meta_ref[META_TIER] * rows + lax.broadcasted_iota(jnp.int32, (rows, 1), 0)
    ok = place < meta_ref[META_STREAMS + stream]
    back = back_ref[0].astype(WIDE) + back_other_ref[0].astype(WIDE)
    grad_out = jnp.where(ok, cot_ref[0].astype(WIDE), 0.0)
    grad_hidden = grad_out + norm_back(back, normed, inverse, gain_ref[...])
    grad_hidden_ref[0] = grad_hidden
    low = grad_hidden.astype(LOW)
    merged = merged_ref[...]
    grad_merged = dot(low, w_ref[...], NT).astype(LOW)
    grad_merged_ref[0, :rows, :] = grad_merged
    heads = merged.shape[1] // HD
    stats[:heads, :] = total_ref[...]
    product = grad_merged.astype(WIDE) * merged.astype(WIDE)
    for head in range(heads):
        turned = product[:, head * HD : (head + 1) * HD].T
        stats[heads + head : heads + head + 1, :] = jnp.sum(turned, axis=0, keepdims=True)
    put_packed(grad_merged_ref.at[0], rows, stats[...])
    grad_w = dot(merged, low, TN)
    gain_part = jnp.sum(back * normed, axis=0, keepdims=True)
    bias_part = jnp.sum(back, axis=0, keepdims=True)

    @pl.when(stream == 0)
    def _():
        w_acc[...] = grad_w
        vector_ref[0:1, :] = gain_part
        vector_ref[1:2, :] = bias_part

    @pl.when(stream != 0)
    def _():
        w_acc[...] += grad_w
        vector_ref[0:1, :] += gain_part
        vector_ref[1:2, :] += bias_part

    @pl.when(stream == pl.num_programs(0) - 1)
    def _():
        grad_w_ref[...] = w_acc[...].astype(LOW)


def hidden_back(chain, meta, x, a, b, back, back_other, cot, merged, total, w, gain):
    streams, rows, width = x.shape
    features = w.shape[0]
    heads = features // HD
    outs = [
        shaped(x.shape, WIDE),
        shaped((streams, rows + packed_rows(2 * heads), features)),
        shaped(w.shape),
        shaped((2, width), WIDE),
    ]
    streamed = (x, back, back_other, cot)
    lists = (*a, *b, *merged, *total)
    return chain.call(
        functools.partial(hidden_back_kernel, streams),
        (streams,),
        [scalars()]
        + [per_stream(v.shape) for v in streamed]
        + [whole(v.shape) for v in (w, gain, *lists)],
        [per_stream(o.shape) for o in outs[:2]] + [whole(o.shape) for o in outs[2:]],
        outs,
        scratch=[
            pltpu.VMEM(w.shape, WIDE),
            pltpu.VMEM((2 * heads, rows), WIDE),
            pltpu.VMEM((rows, width), LOW),
            pltpu.VMEM((rows, width), LOW),
            pltpu.VMEM((rows, features), LOW),
            pltpu.VMEM((heads, rows), WIDE),
        ],
        us=6.5,
        vmem=VMEM_WIDE,
    )(meta, *streamed, w, gain, *lists)


def attend_back_kernel(own, streams, meta_ref, gm_ref, km_ref, vm_ref, ks_ref, vs_ref, *refs):
    *refs, q_ref = refs
    pick(pl.program_id(0), refs[: streams], q_ref)
    refs = refs[streams :]
    if own:
        gq_ref, gkm_ref, gvm_ref, gks_ref, gvs_ref = refs
        before = None
    else:
        before, (gq_ref, gkm_ref, gvm_ref, gks_ref, gvs_ref) = refs[:4], refs[4:]
    stream = pl.program_id(0)
    slots, rows = km_ref.shape[1], q_ref.shape[0]
    heads = q_ref.shape[1] // HD
    stats = get_packed(gm_ref.at[0], rows, 2 * heads, rows)

    def put(ref, index, cols, value):
        if before is not None:
            value = value + before[index][0, :, cols]
        ref[0, :, cols] = value.astype(ref.dtype)

    def body(with_segment):
        memory_ok, segment_ok = slot_masks(own, meta_ref, stream, streams, slots, rows)
        for head in range(heads):
            cols = slice(head * HD, (head + 1) * HD)
            query = q_ref[:, cols]
            grad = gm_ref[0, :rows, cols]
            total = stats[head : head + 1, :]
            delta = stats[heads + head : heads + head + 1, :]

            def tier(key, value, ok):
                scores = jnp.where(ok, dot(key, query, NT) * (SCALE * LOG2E), NEG)
                weights = jnp.exp2(scores - total)
                grad_scores = (weights * (dot(value, grad, NT) - delta)).astype(LOW)
                return (
                    dot(key, grad_scores, TN),
                    dot(grad_scores, query) * SCALE,
                    dot(weights.astype(LOW), grad),
                )

            turned, grad_key, grad_value = tier(km_ref[0, :, cols], vm_ref[0, :, cols], memory_ok)
            put(gkm_ref, 0, cols, grad_key)
            put(gvm_ref, 1, cols, grad_value)
            if with_segment:
                more, grad_key, grad_value = tier(
                    ks_ref[0, :, cols], vs_ref[0, :, cols], segment_ok
                )
                turned = turned + more
                put(gks_ref, 2, cols, grad_key)
                put(gvs_ref, 3, cols, grad_value)
            else:
                gks_ref[0, :, cols] = before[2][0, :, cols].astype(gks_ref.dtype)
                gvs_ref[0, :, cols] = before[3][0, :, cols].astype(gvs_ref.dtype)
            gq_ref[0, :, cols] = (turned * SCALE).T.astype(LOW)

    by_tier(own, meta_ref, body)


def attend_back(chain, own, meta, queries, gm, km, vm, ks, vs, before=()):
    streams = len(queries)
    rows, features = queries[0].shape
    kind = WIDE if own else LOW
    outs = [shaped((streams, rows, features))] + [shaped(a.shape, kind) for a in (km, vm, ks, vs)]
    return chain.call(
        functools.partial(attend_back_kernel, own, streams),
        (streams,),
        [scalars()]
        + [per_stream(a.shape) for a in (gm, km, vm, ks, vs)]
        + [whole(q.shape) for q in queries]
        + [per_stream(a.shape) for a in before],
        [per_stream(o.shape) for o in outs],
        outs,
        scratch=[pltpu.VMEM((rows, features), LOW)],
        us=10,
        vmem=VMEM_WIDE,
    )(meta, gm, km, vm, ks, vs, *queries, *before)


def column_of(row):
    return jnp.broadcast_to(row, (HD, row.shape[1])).T[:, 0:1]


def row_of(column):
    return jnp.broadcast_to(column, (column.shape[0], HD)).T[0:1, :]


def key_value_kernel_back(
    bits, meta_ref, unit_ref, stored_ref, gks_ref, gvs_ref, gkm_ref, gvm_ref,
    wk_ref, wv_ref, gain_ref, bias_ref, column_ref, sent_ref, kept_ref, k_acc, v_acc, sums
):
    stream = pl.program_id(0)
    width, features = wk_ref.shape

    @pl.when(stream == 0)
    def _():
        k_acc[...] = jnp.zeros_like(k_acc)
        v_acc[...] = jnp.zeros_like(v_acc)
        sums[...] = jnp.zeros_like(sums)

    unit, stored = unit_ref[0].T, stored_ref[0].T
    gks, gvs, gkm, gvm = gks_ref[0], gvs_ref[0], gkm_ref[0], gvm_ref[0]
    k_acc[...] += dot(unit, gks) + dot(stored, gkm)
    v_acc[...] += dot(unit, gvs) + dot(stored, gvm)
    for place, pair in enumerate(((gks, gkm), (gvs, gvm))):
        for piece in pair:
            sums[place : place + 1, :] += jnp.sum(piece.astype(WIDE), axis=0, keepdims=True)

    @pl.when(stream == pl.num_programs(0) - 1)
    def _():
        wk, wv = wk_ref[...].astype(WIDE), wv_ref[...].astype(WIDE)
        column_ref[0:1, :] = row_of(jnp.sum(wk * k_acc[...] + wv * v_acc[...], axis=1, keepdims=True))
        column_ref[1:2, :] = row_of(
            jnp.sum(wk * sums[0:1, :] + wv * sums[1:2, :], axis=1, keepdims=True)
        )
        gain, bias = column_of(gain_ref[...]), column_of(bias_ref[...])
        k_acc[...] = gain * k_acc[...] + bias * sums[0:1, :]
        v_acc[...] = gain * v_acc[...] + bias * sums[1:2, :]
        half = width // 2
        side = pair_side(meta_ref, bits)
        for ref, which in ((sent_ref, 1 - side), (kept_ref, side)):
            rows = pl.ds(pl.multiple_of(which * half, half), half)
            ref[:, :features] = k_acc[rows, :].astype(LOW)
            ref[:, features:] = v_acc[rows, :].astype(LOW)


def key_value_grads(chain, orders, meta, streamed, fixed):
    width, features = fixed[0].shape
    outs = [shaped((2, width), WIDE)] + [shaped((width // 2, 2 * features))] * 2
    acc = pltpu.VMEM((width, features), WIDE)
    return chain.call(
        functools.partial(key_value_kernel_back, tuple(order[0] for order in orders)),
        (streamed[0].shape[0],),
        [scalars()] + [per_stream(v.shape) for v in streamed] + [whole(v.shape) for v in fixed],
        [whole(o.shape) for o in outs],
        outs,
        scratch=[acc, acc, pltpu.VMEM((2, features), WIDE)],
        vmem=VMEM_WIDE,
        us=10,
    )(meta, *streamed, *fixed)


def query_kernel_back(
    bits, meta_ref, unit_ref, own_ref, came_ref, gks_ref, gvs_ref,
    wq_ref, wk_ref, wv_ref, gwo_ref, gain_ref, bias_ref, column_ref, vector_ref, normed_ref,
    sent_ref, kept_ref, q_acc, sums
):
    stream = pl.program_id(0)
    width, features = wq_ref.shape

    @pl.when(stream == 0)
    def _():
        q_acc[...] = jnp.zeros_like(q_acc)
        sums[...] = jnp.zeros_like(sums)

    grad = (own_ref[0].astype(WIDE) + came_ref[0].astype(WIDE)).astype(LOW)
    q_acc[...] += dot(unit_ref[0], grad, TN)
    sums[...] += jnp.sum(grad.astype(WIDE), axis=0, keepdims=True)
    normed_ref[0] = (
        dot(grad, wq_ref[...], NT) + dot(gks_ref[0], wk_ref[...], NT) + dot(gvs_ref[0], wv_ref[...], NT)
    ).astype(LOW)

    @pl.when(stream == pl.num_programs(0) - 1)
    def _():
        wq = wq_ref[...].astype(WIDE)
        gain_part = row_of(jnp.sum(wq * q_acc[...], axis=1, keepdims=True))
        bias_part = row_of(jnp.sum(wq * sums[...], axis=1, keepdims=True))
        gain, bias = column_of(gain_ref[...]), column_of(bias_ref[...])
        query = (gain * q_acc[...] + bias * sums[...]).astype(LOW)
        half = width // 2
        extra = sent_ref.shape[0] - half

        def put(out_ref, query_ref):
            out_ref[:half, :] = gwo_ref[...]
            out_ref[half:, :] = jnp.zeros((extra, width), LOW)
            out_ref[half : half + 1, :] = (column_ref[0:1, :] + gain_part).astype(LOW)
            out_ref[half + 1 : half + 2, :] = (column_ref[1:2, :] + bias_part).astype(LOW)
            out_ref[half + 2 : half + 4, :] = (0.5 * vector_ref[...]).astype(LOW)
            query_ref[:half, :features] = query[:half]
            query_ref[:half, features:] = query[half:]
            query_ref[half:, :] = jnp.zeros((extra, width), LOW)

        side = pair_side(meta_ref, bits)

        @pl.when(side == 0)
        def _():
            put(kept_ref, sent_ref)

        @pl.when(side != 0)
        def _():
            put(sent_ref, kept_ref)


def query_grads(chain, orders, meta, streamed, fixed):
    width, features = fixed[0].shape
    unit = streamed[0]
    outs = [shaped(unit.shape)]
    outs += [shaped((width // 2 + EXTRA, 2 * features))] * 2
    return chain.call(
        functools.partial(query_kernel_back, tuple(order[0] for order in orders)),
        (unit.shape[0],),
        [scalars()] + [per_stream(v.shape) for v in streamed] + [whole(v.shape) for v in fixed],
        [per_stream(unit.shape)] + [whole(o.shape) for o in outs[1:]],
        outs,
        scratch=[pltpu.VMEM((width, features), WIDE), pltpu.VMEM((1, features), WIDE)],
        vmem=VMEM_WIDE,
        us=9,
    )(meta, *streamed, *fixed)


def input_back_kernel(x_ref, own_ref, other_ref, hidden_ref, gain_ref, out_ref):
    normed, inverse = norm_stats(x_ref[0].astype(WIDE))
    grad = own_ref[0].astype(WIDE) + other_ref[0].astype(WIDE)
    out_ref[0] = (hidden_ref[0] + norm_back(grad, normed, inverse, gain_ref[...])).astype(LOW)


def input_back(chain, x, own, other, grad_hidden, gain):
    streamed = (x, own, other, grad_hidden)
    return chain.call(
        input_back_kernel,
        (x.shape[0],),
        [per_stream(v.shape) for v in streamed] + [whole(gain.shape)],
        per_stream(x.shape),
        shaped(x.shape),
        us=4,
    )(*streamed, gain)


def compress_kernel(bits, meta_ref, memory_ref, came_ref, rest_ref, w_ref, cot_ref, out_ref, *refs):
    sent_ref, kept_ref, acc, grads = refs
    stream = pl.program_id(0)
    streams = pl.num_programs(0)
    head = meta_ref[META_HEAD]
    mine = meta_ref[META_TIER] == 0
    slots, part = came_ref.shape[1], came_ref.shape[2]
    count = out_ref.shape[1]
    place = lax.broadcasted_iota(jnp.int32, (count, slots), 0)
    slot = lax.broadcasted_iota(jnp.int32, (count, slots), 1)
    length = meta_ref[META_STREAMS + stream]
    filled = jnp.where(mine, meta_ref[META_STREAMS + streams + stream], slots)
    ok = lax.broadcasted_iota(jnp.int32, (count, 1), 0) < lax.div(length, jnp.int32(RATE))
    cot = jnp.where(ok, cot_ref[0].astype(WIDE), 0.0).astype(LOW)

    @pl.when(stream == 0)
    def _():
        acc[...] = jnp.zeros_like(acc)

    picks = []
    for shift in range(RATE):
        chosen = (slot == place * RATE + shift) & (slot < filled)
        picks.append(jnp.where(chosen, 1.0, 0.0).astype(LOW))
    result = jnp.zeros(out_ref.shape[1:], WIDE)
    for ref, side in ((came_ref, head), (rest_ref, 1 - head)):
        start = pl.multiple_of(side * part, part)
        stored = jnp.where(mine, memory_ref[0, 0, :, pl.ds(start, part)].astype(WIDE), ref[0].astype(WIDE))
        stored = stored.astype(LOW)
        for shift in range(RATE):
            rows = dot(picks[shift], stored).astype(LOW)
            result = result + dot(rows, w_ref[shift, pl.ds(start, part), :])
            acc[shift, pl.ds(start, part), :] += dot(rows, cot, TN)
    out_ref[0] = jnp.where(ok, result, 0.0).astype(LOW)

    @pl.when(stream == streams - 1)
    def _():
        width = w_ref.shape[1]
        for shift in range(RATE):
            grads[shift * width : (shift + 1) * width, :] = acc[shift].astype(LOW)
        half = sent_ref.shape[0]
        side = pair_side(meta_ref, bits)
        for ref, which in ((sent_ref, 1 - side), (kept_ref, side)):
            ref[...] = grads[pl.ds(pl.multiple_of(which * half, half), half), :]


def compress(chain, orders, meta, memories, came, rest, w, cot):
    flat = (w.shape[0] * w.shape[1], w.shape[2])
    outs = [shaped(cot.shape)] + [shaped((flat[0] // 2, flat[1]))] * 2
    bits = tuple(order[0] for order in orders)
    return chain.call(
        functools.partial(compress_kernel, bits),
        (cot.shape[0],),
        [scalars()]
        + [per_stream(v.shape) for v in (memories, came, rest)]
        + [whole(w.shape), per_stream(cot.shape)],
        [per_stream(cot.shape)] + [whole(o.shape) for o in outs[1:]],
        outs,
        scratch=[pltpu.VMEM(w.shape, WIDE), pltpu.VMEM(flat, LOW)],
        us=5,
    )(meta, memories, came, rest, w, cot)


def bits_of():
    size = lax.axis_size("dp")
    bits = [("tier", 1)]
    step = 1
    while step < size:
        bits.append(("dp", step))
        step *= 2
    return bits


def swap(value, bit):
    axis, step = bit
    return lax.ppermute(value, axis, [(i, i ^ step) for i in range(lax.axis_size(axis))])


def swap_head(value):
    return swap(value, ("head", 1))


def swap_tier(value):
    return swap(value, ("tier", 1))


def swap_pair(value, bits):
    axes = ("dp", "tier", "head")
    sizes = [lax.axis_size(axis) for axis in axes]
    pairs = []
    for dp in range(sizes[0]):
        for tier in range(sizes[1]):
            for head in range(sizes[2]):
                axis, step = bits[head]
                to_dp = dp ^ step if axis == "dp" else dp
                to_tier = tier ^ step if axis == "tier" else tier
                pairs.append(
                    (
                        (dp * sizes[1] + tier) * sizes[2] + head,
                        (to_dp * sizes[1] + to_tier) * sizes[2] + head,
                    )
                )
    return lax.ppermute(value, axes, pairs)


def total_of(first, second):
    return (first.astype(WIDE) + second.astype(WIDE)).astype(LOW)


def scatter_kernel(bits, meta_ref, kept, came, *refs):
    half = kept.shape[0] // 2
    side = pair_side(meta_ref, bits)
    for ref, which in zip(refs, (1 - side, side)):
        rows = pl.ds(pl.multiple_of(which * half, half), half)
        ref[...] = total_of(kept[rows, :], came[rows, :])


def add_kernel(bits, meta_ref, kept, came, *refs):
    refs[0][...] = total_of(kept[...], came[...])


def gather_kernel(bits, meta_ref, held, came, *refs):
    half = held.shape[0]
    side = pair_side(meta_ref, bits)
    refs[0][pl.ds(pl.multiple_of(side * half, half), half), :] = held[...]
    refs[0][pl.ds(pl.multiple_of((1 - side) * half, half), half), :] = came[...]


class Reduce:
    def __init__(self, chain, meta, orders, sent, kept):
        self.chain, self.meta, self.orders = chain, meta, orders
        self.stages = len(orders[0])
        self.depth = min(3, self.stages - 1)
        self.kept = kept
        self.stage = 0
        self.send(sent, 0)

    def bits(self, level):
        return tuple(order[level] for order in self.orders)

    def send(self, array, level):
        self.came = swap_pair(array, self.bits(level))

    def run(self, kernel, level, outs):
        return self.chain.call(
            functools.partial(kernel, self.bits(level)),
            (1,),
            [scalars(), whole(self.kept.shape), whole(self.came.shape)],
            [whole(o.shape) for o in outs],
            outs,
            vmem=8,
        )(self.meta, self.kept, self.came)

    def ready(self):
        return self.stage >= self.stages + self.depth - 1

    def step(self):
        depth, stage, stages = self.depth, self.stage, self.stages
        self.stage += 1
        rows, width = self.kept.shape
        if stage < depth - 1:
            sent, self.kept = self.run(
                scatter_kernel, stage + 1, [shaped((rows // 2, width))] * 2
            )
            self.send(sent, stage + 1)
        elif stage < stages:
            (self.kept,) = self.run(add_kernel, stage, [shaped((rows, width))])
            self.send(self.kept, stage + 1 if stage + 1 < stages else depth - 1)
        else:
            level = depth - 1 - (stage - stages)
            (self.kept,) = self.run(gather_kernel, level, [shaped((2 * rows, width))])
            self.send(self.kept, level - 1)


def finish_kernel(bits, write, carried, meta_ref, held, came, *refs):
    write(pair_side(meta_ref, bits), held, came, refs[carried:])


def finish(group, write, out_shapes, out_specs, carried=()):
    args = [group.meta, group.kept, group.came, *carried]
    count = len(carried)
    return group.chain.call(
        functools.partial(finish_kernel, group.bits(0), write, count),
        (1,),
        [scalars(), whole(group.kept.shape), whole(group.came.shape)] + [any_spec()] * count,
        out_specs,
        out_shapes,
        vmem=24,
        alias={3 + i: i for i in range(count)},
        us=3,
    )(*args)


def write_rows(side, held, came, outs):
    half = held.shape[0]
    for ref, which in ((held, side), (came, 1 - side)):
        outs[0][pl.ds(pl.multiple_of(which * half, half), half), :] = ref[...].astype(WIDE)


def finish_ffn(group, part, out_shape, in_shape, carried=()):
    specs = [
        pl.BlockSpec((out_shape[0] // 2, out_shape[1]), lambda i: (part, 0)),
        pl.BlockSpec((in_shape[0], in_shape[1] // 2), lambda i: (0, part)),
    ]

    def write(side, held, came, outs):
        for out_ref, in_ref, which in ((held, came, 0), (came, held, 1)):

            @pl.when(side == which)
            def _():
                outs[0][...] = out_ref[...].astype(WIDE)
                outs[1][...] = in_ref[...].astype(WIDE)

    return finish(group, write, [shaped(out_shape, WIDE), shaped(in_shape, WIDE)], specs, carried)


def finish_key_value(group, width, features):
    shapes = [shaped((width, features), WIDE)] * 2

    def write(side, held, came, outs):
        half = held.shape[0]
        for ref, which in ((held, side), (came, 1 - side)):
            rows = pl.ds(pl.multiple_of(which * half, half), half)
            outs[0][rows, :] = ref[:, :features].astype(WIDE)
            outs[1][rows, :] = ref[:, features:].astype(WIDE)

    return finish(group, write, shapes, [whole_block(v.shape) for v in shapes])


def finish_out_query(group, width, features):
    shapes = [shaped((features, width), WIDE), shaped((width, features), WIDE), shaped((16, width))]

    def write(side, held, came, outs):
        def put(out_ref, query_ref):
            half = outs[0].shape[0]
            outs[0][...] = out_ref[:half, :].astype(WIDE)
            outs[1][:half, :] = query_ref[:half, :features].astype(WIDE)
            outs[1][half:, :] = query_ref[:half, features:].astype(WIDE)
            outs[2][...] = out_ref[half : half + 16, :]

        @pl.when(side == 0)
        def _():
            put(held, came)

        @pl.when(side != 0)
        def _():
            put(came, held)

    return finish(
        group, write, shapes, [whole_block(v.shape) for v in shapes[:2]] + [whole(shapes[2].shape)]
    )


def finish_compress(group, shape):
    flat = (shape[0] * shape[1], shape[2])
    return finish(group, write_rows, [shaped(flat, WIDE)], [whole_block(flat)])[0].reshape(shape)


def on_device(
    inputs,
    memories,
    seg_len,
    mem_count,
    w_query,
    w_key,
    w_value,
    w_attn_out,
    w_ffn_in,
    w_ffn_out,
    w_compress,
    gain_attn,
    bias_attn,
    gain_ffn,
    bias_ffn,
    cotan_output,
    cotan_compressed,
):
    tier_index = lax.axis_index("tier")
    streams, rows, width = inputs.shape
    features = w_query.shape[1]
    hidden_units = w_ffn_in.shape[1]
    counts = mem_count[:, 0]
    place = jnp.stack([tier_index, lax.axis_index("head"), lax.axis_index("dp")])
    meta = jnp.concatenate([place, seg_len, counts], 0).astype(jnp.int32)
    gain_row, bias_row = gain_attn[None], bias_attn[None]
    gain_second, bias_second = gain_ffn[None], bias_ffn[None]
    chain = Chain()

    unit, low, queries = query_rows(chain, meta, inputs, gain_row, bias_row, w_query)
    queries_other = [swap_tier(q) for q in queries]
    keys, values = key_values(chain, low, w_key, w_value)
    stored, memory_keys, memory_values = stored_rows(
        chain, memories, gain_row, bias_row, w_key, w_value
    )
    tiers = (memory_keys, memory_values, keys, values)
    own, came = [], []
    for stream in range(streams):
        came.append(swap_tier(attend(chain, False, stream, meta, queries_other[stream], *tiers)))
        own.append(attend(chain, True, stream, meta, queries[stream], *tiers))
    got = {}
    merged, totals, attended, attended_other = [], [], [], []
    for stream in range(streams):
        low, total, part = merge(chain, rows, own[stream], came[stream], w_attn_out)
        merged.append(low)
        totals.append(total)
        attended.append(part)
        attended_other.append(swap_head(part))
    got["evicted"] = lax.ppermute(evicted_rows(chain, meta, memories), "tier", [(0, 1)])

    tier, low_bit, *more = bits_of()
    high_bit, far_bit, more = more[0], more[1], more[2:]
    axes = {"x": tier, "y": low_bit, "z": high_bit, "w": far_bit}
    orders = {}
    for name, paths in PATHS.items():
        rest = "yzw" if name == "compress" else "xyzw"
        orders[name] = tuple(
            tuple(axes[axis] for axis in dict.fromkeys(path + rest)) + tuple(more)
            for path in paths.split("/")
        )
    flat = (streams * rows, width)
    hidden_args = (
        inputs.reshape(flat),
        cotan_output.reshape(flat),
        gain_second,
        bias_second,
        *attended,
        *attended_other,
    )
    groups = {}

    def begin(name, sent, kept):
        groups[name] = Reduce(chain, meta, orders[name], sent, kept)

    def run_ffn():
        names = ("f1", "f2")
        got["act"], got["lifted"], *parts = ffn(
            chain, streams, [orders[name] for name in names], meta, hidden_args, w_ffn_in, w_ffn_out
        )
        for place, name in enumerate(names):
            begin(name, *parts[2 * place : 2 * place + 2])

    def run_back():
        got["back"] = ffn_back(chain, got["lifted"], w_ffn_in).reshape(inputs.shape)
        got["back_other"] = swap_head(got["back"])

    def run_ffn3():
        got["ffn"] = ffn_out(chain, got["act"], w_ffn_out).reshape(inputs.shape)
        got["ffn_other"] = swap_head(got["ffn"])

    def run_hidden():
        got["hidden"], got["gm"], got["gwo"], vectors_ffn = hidden_back(
            chain, meta, inputs, attended, attended_other, got["back"], got["back_other"],
            cotan_output, merged, totals, w_attn_out, gain_second,
        )
        got["gm_other"] = swap_tier(got["gm"])
        got["vectors"] = vectors_ffn

    def run_own():
        got["own"], *got["sums"] = attend_back(chain, True, meta, queries, got["gm"], *tiers)

    def run_other():
        got["other"], *got["grads"] = attend_back(
            chain, False, meta, queries_other, got["gm_other"], *tiers,
            before=tuple(got["sums"]),
        )
        got["came"] = swap_tier(got["other"])

    def run_output():
        got["output"] = output_rows(
            chain, meta, inputs, got["ffn"], got["ffn_other"], attended, attended_other
        )

    def run_grads():
        grad_km, grad_vm, grad_ks, grad_vs = got["grads"]
        got["column"], *parts = key_value_grads(
            chain, orders["kv"], meta, (unit, stored, grad_ks, grad_vs, grad_km, grad_vm),
            (w_key, w_value, gain_row, bias_row),
        )
        begin("kv", *parts)

    def run_query():
        _, _, grad_ks, grad_vs = got["grads"]
        got["normed"], *parts = query_grads(
            chain, orders["oq"], meta, (unit, got["own"], got["came"], grad_ks, grad_vs),
            (
                w_query, w_key, w_value, got["gwo"], gain_row, bias_row,
                got["column"], got["vectors"],
            ),
        )
        got["normed_other"] = swap_head(got["normed"])
        begin("oq", *parts)

    def run_evict2():
        got["evicted"] = copied(chain, got["evicted"])
        got["evicted_other"] = swap_head(got["evicted"])

    def run_evict3():
        got["evicted_other"] = copied(chain, got["evicted_other"])

    def run_input():
        got["grad_inputs"] = input_back(
            chain, inputs, got["normed"], got["normed_other"], got["hidden"], gain_row
        )

    def run_compress():
        got["compressed"], *parts = compress(
            chain, orders["compress"], meta, memories, got["evicted"], got["evicted_other"],
            w_compress, cotan_compressed,
        )
        begin("compress", *parts)

    def end(name):
        group = groups.pop(name)
        out_shape, in_shape = w_ffn_out.shape, w_ffn_in.shape
        if name == "f1":
            got["ffn_grads"] = finish_ffn(group, 0, out_shape, in_shape)
        elif name == "f2":
            got["ffn_grads"] = finish_ffn(group, 1, out_shape, in_shape, got["ffn_grads"])
        elif name == "kv":
            got["kv"] = finish_key_value(group, width, features)
        elif name == "oq":
            got["oq"] = finish_out_query(group, width, features)
            got["vector"] = got["oq"][2]
        else:
            got["compress"] = finish_compress(group, w_compress.shape)

    runs = {
        "ffn": run_ffn, "back": run_back, "ffn3": run_ffn3, "hidden": run_hidden, "own": run_own,
        "other": run_other, "output": run_output, "grads": run_grads, "query": run_query,
        "evict2": run_evict2, "evict3": run_evict3, "input": run_input, "compr": run_compress, "pause": lambda: pause(chain),
    }
    chain.cost = COST
    for name in ORDER:
        if name in runs:
            runs[name]()
        elif name in groups and groups[name].ready():
            end(name)
        elif name in groups:
            groups[name].step()
    while groups:
        for name in list(groups):
            if groups[name].ready():
                end(name)
            else:
                groups[name].step()
    vectors = got["vector"].astype(WIDE) + swap_head(got["vector"]).astype(WIDE)
    return (
        got["output"],
        got["compressed"],
        got["grad_inputs"],
        got["oq"][1],
        *got["kv"],
        got["oq"][0],
        got["ffn_grads"][1],
        got["ffn_grads"][0],
        got["compress"],
        vectors[0],
        vectors[1],
        vectors[2],
        vectors[3],
    )


def solution(mesh):
    return jax.shard_map(
        on_device,
        mesh=mesh,
        in_specs=(
            P("dp", "tier", None),
            P("dp", "tier", None, None),
            P("dp"),
            P("dp", "tier"),
            P(None, "head"),
            P(None, "head"),
            P(None, "head"),
            P("head", None),
            P(None, "head"),
            P("head", None),
            P(None, None, ("tier", "head")),
            P(),
            P(),
            P(),
            P(),
            P("dp", "tier", None),
            P("dp", None, ("tier", "head")),
        ),
        out_specs=(
            P("dp", "tier", None),
            P("dp", None, ("tier", "head")),
            P("dp", "tier", None),
            P(None, "head"),
            P(None, "head"),
            P(None, "head"),
            P("head", None),
            P(None, "head"),
            P("head", None),
            P(None, None, ("tier", "head")),
            P(),
            P(),
            P(),
            P(),
        ),
        check_vma=False,
    )
```
